128 devices in a mesh: tm: 32 (over x, y, core), head: 4 (over z).
Axes of the slice: x: 4, y: 4, z: 4, core: 2. Of those that a mesh axis runs over, the one named last changes fastest.
Arguments:
- activations: bfloat16 [8192, 5120], P('tm'), may hold values from -24 to 24
- frozen_query_weight: bfloat16 [5120, 1024], P(None, 'head'), may hold values from -0.078125 to 0.078125
- frozen_key_weight: bfloat16 [5120, 1024], P(None, 'head'), may hold values from -0.078125 to 0.078125
- frozen_value_weight: bfloat16 [5120, 1024], P(None, 'head'), may hold values from -0.078125 to 0.078125
- query_down_adapter: bfloat16 [5120, 128], replicated, may hold values from -0.078125 to 0.078125
- query_up_adapter: bfloat16 [128, 1024], P(None, 'head'), may hold values from -0.5 to 0.5
- value_down_adapter: bfloat16 [5120, 128], replicated, may hold values from -0.078125 to 0.078125
- value_up_adapter: bfloat16 [128, 1024], P(None, 'head'), may hold values from -0.5 to 0.5
- output_gradient: bfloat16 [8192, 1024], P('tm', 'head'), may hold values from -6 to 6
- levels: int32 [64, 64], replicated, may hold values from 1 to 4, as said below
- key_block_order: int32 [64, 64, 4], replicated, may hold values from 0 to 3, as said below
- slot_true_frame: int32 [64], replicated, may hold values from 0 to 63, each once
Outputs:
- attention_out: bfloat16 [8192, 1024], P('tm', 'head')
- grad_down_q: float32 [5120, 128], replicated
- grad_up_q: float32 [128, 1024], P(None, 'head')
- grad_down_v: float32 [5120, 128], replicated
- grad_up_v: float32 [128, 1024], P(None, 'head')
The draws below stay inside these ranges and needn't reach their ends.
Inputs may be any that keep to these rules, and one draw needn't show every extreme that they name: levels[f, g] is 4 wherever |f - g| <= 1. Each key_block_order[f, g] is a permutation of the key blocks of one frame.
All inputs are finite; a program needn't handle non-finite values.
Results may differ from the reference program's by a relative error of at most 0.0303.
The reference program's roundings to bfloat16 on the way count: a program that leaves them out, or rounds other values in their place, can miss the bound.
Values may be sent and summed in bfloat16 or wider, within the bound.
No kernel may reach another device: no remote copies, remote signals or barrier semaphores. Data moves between devices by JAX's collectives and lax.ppermute only.
A program may use at most 192 MiB of HBM per device.

```python
import jax
import jax.numpy as jnp
from jax import lax

MODEL_WIDTH = 5120
HEAD_SIZE = 128
ADAPTER_RANK = 128
FT = 128
BLK = 32
BPF = 4
FRAMES = 64
TOKENS = 8192
WINDOW_HEADS = 8


def draw_activations(key, part):
    key = jax.random.fold_in(key, 11)
    base_key = jax.random.fold_in(key, 0)
    base = jnp.clip(jax.random.normal(base_key, (TOKENS, MODEL_WIDTH), jnp.float32), -6.0, 6.0)
    return base.astype(jnp.bfloat16)


def draw_levels(key, part):
    key = jax.random.fold_in(key, 12)
    frame_index = jnp.arange(FRAMES, dtype=jnp.int32)
    distance = jnp.abs(frame_index[:, None] - frame_index[None, :])
    shift_count = jnp.zeros((FRAMES, FRAMES), jnp.int32)
    for power in range(1, 16):
        shift_count = shift_count + (distance >= 2 ** power).astype(jnp.int32)
    base = jnp.maximum(jnp.right_shift(jnp.full((FRAMES, FRAMES), BPF, jnp.int32), shift_count), 1)
    jitter = jax.random.randint(key, (FRAMES, FRAMES), -1, 2, dtype=jnp.int32)
    level_value = jnp.clip(base + jitter, 1, BPF)
    return jnp.where(distance <= 1, BPF, level_value).astype(jnp.int32)


def draw_key_block_order(key, part):
    key = jax.random.fold_in(key, 13)
    scores = jax.random.randint(key, (FRAMES, FRAMES, BPF), 0, 1 << 20, dtype=jnp.int32) * BPF + jnp.arange(BPF, dtype=jnp.int32)
    return jnp.argsort(scores, axis=-1, stable=True).astype(jnp.int32)


def shard_levels(stream_key, extent, shards, smallest, high):
    def one(axis_at, shards_of):
        steps = jax.random.uniform(jax.random.fold_in(jax.random.fold_in(stream_key, 6), axis_at), (shards_of,), jnp.float32, smallest / len(shards), high / len(shards))
        return jnp.repeat(jnp.exp(steps), extent[axis_at] // shards_of).reshape((-1,) + (1,) * (len(extent) - axis_at - 1))

    level = one(*shards[0])
    for cut in shards[1:]:
        level = level * one(*cut)
    return level


def noise(stream_key, extent, spread, most, cuts=(), held_as=jnp.bfloat16):
    values = jax.random.normal(stream_key, extent, jnp.float32) * spread
    if len(cuts) > 0:
        values = shard_levels(stream_key, extent, cuts, -0.22, 0.18) * values
    return jnp.clip(values, min=-most, max=most).astype(held_as)


def setup_inputs(seed: int = 0) -> dict:
    key_list = jax.random.split(jax.random.key(seed), 13)
    return {
        "activations": draw_activations(jax.random.fold_in(key_list[12], 71), 0),
        "frozen_query_weight": noise(key_list[1], (MODEL_WIDTH, WINDOW_HEADS * HEAD_SIZE), MODEL_WIDTH ** -0.5, 0.078125, ((1, 4),)),
        "frozen_key_weight": noise(key_list[2], (MODEL_WIDTH, WINDOW_HEADS * HEAD_SIZE), MODEL_WIDTH ** -0.5, 0.078125, ((1, 4),)),
        "frozen_value_weight": noise(key_list[3], (MODEL_WIDTH, WINDOW_HEADS * HEAD_SIZE), MODEL_WIDTH ** -0.5, 0.078125, ((1, 4),)),
        "query_down_adapter": noise(key_list[4], (MODEL_WIDTH, ADAPTER_RANK), MODEL_WIDTH ** -0.5, 0.078125),
        "query_up_adapter": noise(key_list[5], (ADAPTER_RANK, WINDOW_HEADS * HEAD_SIZE), ADAPTER_RANK ** -0.5, 0.5, ((1, 4),)),
        "value_down_adapter": noise(key_list[6], (MODEL_WIDTH, ADAPTER_RANK), MODEL_WIDTH ** -0.5, 0.078125),
        "value_up_adapter": noise(key_list[7], (ADAPTER_RANK, WINDOW_HEADS * HEAD_SIZE), ADAPTER_RANK ** -0.5, 0.5, ((1, 4),)),
        "output_gradient": noise(key_list[8], (TOKENS, WINDOW_HEADS * HEAD_SIZE), 1.0, 6.0, ((0, 32), (1, 4))),
        "levels": draw_levels(jax.random.fold_in(key_list[12], 71), 0),
        "key_block_order": draw_key_block_order(jax.random.fold_in(key_list[12], 71), 0),
        "slot_true_frame": jax.random.permutation(key_list[11], FRAMES).astype(jnp.int32),
    }


NEGATIVE = -1e30


def slot_table(levels, key_block_order, slot_true_frame):
    frame_count = levels.shape[0]
    block_count = key_block_order.shape[2]
    ranks = jnp.arange(block_count, dtype=jnp.int32)
    hits = (key_block_order[:, :, :, None] == ranks[None, None, None, :]) & (ranks[None, None, :, None] < levels[:, :, None, None])
    visible = jnp.sum(hits.astype(jnp.float32), axis=2)
    select = (slot_true_frame[:, None] == jnp.arange(frame_count, dtype=jnp.int32)[None, :]).astype(jnp.float32)
    slots = jnp.einsum("sf,fgb,tg->stb", select, visible, select)
    return slots.reshape(frame_count, frame_count * block_count)


def block_mask(table, q_start, q_count, k_start, k_count):
    query_slot = ((q_start + jnp.arange(q_count, dtype=jnp.int32)) // FT).astype(jnp.int32)
    key_index = ((k_start + jnp.arange(k_count, dtype=jnp.int32)) // BLK).astype(jnp.int32)
    rows = jnp.take(table, query_slot, axis=0)
    return jnp.take(rows, key_index, axis=1) > 0.5


def split_heads(array):
    return array.reshape(array.shape[0], WINDOW_HEADS, HEAD_SIZE).transpose(1, 0, 2)


def join_heads(array):
    return array.transpose(1, 0, 2).reshape(array.shape[1], WINDOW_HEADS * HEAD_SIZE)


def reference(activations, frozen_query_weight, frozen_key_weight, frozen_value_weight, query_down_adapter, query_up_adapter, value_down_adapter, value_up_adapter, output_gradient, levels, key_block_order, slot_true_frame):
    single_float = jnp.float32
    brain_half_float = jnp.bfloat16
    query_rank_state = jnp.dot(activations, query_down_adapter, preferred_element_type=single_float).astype(brain_half_float)
    value_rank_state = jnp.dot(activations, value_down_adapter, preferred_element_type=single_float).astype(brain_half_float)
    query_matrix = (jnp.dot(activations, frozen_query_weight, preferred_element_type=single_float) + jnp.dot(query_rank_state, query_up_adapter, preferred_element_type=single_float)).astype(brain_half_float)
    keys = jnp.dot(activations, frozen_key_weight, preferred_element_type=single_float).astype(brain_half_float)
    value_matrix = (jnp.dot(activations, frozen_value_weight, preferred_element_type=single_float) + jnp.dot(value_rank_state, value_up_adapter, preferred_element_type=single_float)).astype(brain_half_float)
    table = slot_table(levels, key_block_order, slot_true_frame)
    visible = block_mask(table, 0, TOKENS, 0, TOKENS)
    score_scale = HEAD_SIZE ** -0.5

    def one_head(head_item):
        query_head, key_head, value_head, grad_head = head_item
        scores = jnp.dot(query_head, key_head.T, preferred_element_type=single_float) * score_scale
        scores = jnp.where(visible, scores, NEGATIVE)
        row_peak = jnp.max(scores, axis=1, keepdims=True)
        weights_raw = jnp.where(visible, jnp.exp(scores - row_peak), 0.0)
        probs = weights_raw / jnp.sum(weights_raw, axis=1, keepdims=True)
        probs_low = probs.astype(brain_half_float)
        attended = jnp.dot(probs_low, value_head, preferred_element_type=single_float).astype(brain_half_float)
        value_gradient = jnp.dot(probs_low.T, grad_head, preferred_element_type=single_float).astype(brain_half_float)
        prob_grad = jnp.dot(grad_head, value_head.T, preferred_element_type=single_float)
        row_delta = jnp.sum(grad_head.astype(single_float) * attended.astype(single_float), axis=1, keepdims=True)
        score_grad = (probs * (prob_grad - row_delta) * score_scale).astype(brain_half_float)
        query_gradient = jnp.dot(score_grad, key_head, preferred_element_type=single_float).astype(brain_half_float)
        return attended, query_gradient, value_gradient

    attended, query_gradient, value_gradient = lax.map(one_head, (split_heads(query_matrix), split_heads(keys), split_heads(value_matrix), split_heads(output_gradient)))
    attention_out = join_heads(attended)
    query_gradient = join_heads(query_gradient)
    value_gradient = join_heads(value_gradient)
    grad_up_q = jnp.dot(query_rank_state.T, query_gradient, preferred_element_type=single_float)
    grad_up_v = jnp.dot(value_rank_state.T, value_gradient, preferred_element_type=single_float)
    query_rank_gradient = jnp.dot(query_gradient, query_up_adapter.T, preferred_element_type=single_float).astype(brain_half_float)
    value_rank_gradient = jnp.dot(value_gradient, value_up_adapter.T, preferred_element_type=single_float).astype(brain_half_float)
    grad_down_q = jnp.dot(activations.T, query_rank_gradient, preferred_element_type=single_float)
    grad_down_v = jnp.dot(activations.T, value_rank_gradient, preferred_element_type=single_float)
    return attention_out, grad_down_q, grad_up_q, grad_down_v, grad_up_v
```

```python
import math

import jax
import jax.numpy as jnp
from jax import lax
from jax.experimental import pallas as pl
from jax.experimental.pallas import tpu as pltpu
from jax.sharding import Mesh
from jax.sharding import PartitionSpec as P

HEAD = 128
FT = 128
BLK = 32
RANK = 128
CHUNK = 256
CB = CHUNK // BLK
SCALE = HEAD ** -0.5
SCALE2 = SCALE * math.log2(math.e)
NEG = -1e30
f32 = jnp.float32
bf16 = jnp.bfloat16
WIRE = bf16
VMEM = pl.BlockSpec(memory_space=pltpu.VMEM)
SMEM = pl.BlockSpec(memory_space=pltpu.SMEM)
PARAMS = pltpu.CompilerParams(vmem_limit_bytes=48 * 1024 * 1024)


def dot(a, b, ca=1, cb=0):
    return lax.dot_general(a, b, (((ca,), (cb,)), ((), ())), preferred_element_type=f32)


def proj_kernel(pos, act, wq, wk, wv, dq, dv, uq, uv, kv_keep, kv_send, q_keep, q_send, rank, aq, ak, av, ar):
    step = pl.program_id(0)

    @pl.when(step == 0)
    def _():
        aq[...] = jnp.zeros_like(aq)
        ak[...] = jnp.zeros_like(ak)
        av[...] = jnp.zeros_like(av)
        ar[...] = jnp.zeros_like(ar)

    a = act[...]
    ak[...] += dot(a, wk[...])
    av[...] += dot(a, wv[...])
    aq[...] += dot(a, wq[...])
    ar[:, :RANK] += dot(a, dq[...])
    ar[:, RANK:] += dot(a, dv[...])

    @pl.when(step == pl.num_programs(0) - 1)
    def _():
        low = ar[...].astype(bf16)
        rank[...] = low
        query = (aq[...] + dot(low[:, :RANK], uq[...])).astype(bf16)
        keys = ak[...].astype(bf16)
        values = (av[...] + dot(low[:, RANK:], uv[...])).astype(bf16)

        def put(kv, q, at):
            kv[:, :HEAD] = keys[:, at:at + HEAD]
            kv[:, HEAD:] = values[:, at:at + HEAD]
            q[...] = query[:, at:at + HEAD]

        @pl.when(pos[2] == 0)
        def _():
            put(kv_keep, q_keep, 0)
            put(kv_send, q_send, HEAD)

        @pl.when(pos[2] == 1)
        def _():
            put(kv_keep, q_keep, HEAD)
            put(kv_send, q_send, 0)


def project(pos, act, wq, wk, wv, dq, dv, uq, uv):
    rows, width = act.shape
    kt = 512
    cols = wq.shape[1]
    weight = pl.BlockSpec((kt, cols), lambda k: (k, 0))
    down = pl.BlockSpec((kt, RANK), lambda k: (k, 0))
    whole = lambda shape: pl.BlockSpec(shape, lambda k: (0, 0))
    shapes = [(rows, 2 * HEAD), (rows, 2 * HEAD), (rows, HEAD), (rows, HEAD), (rows, 2 * RANK)]
    return pl.pallas_call(
        proj_kernel,
        grid=(width // kt,),
        in_specs=[SMEM, pl.BlockSpec((rows, kt), lambda k: (0, k)), weight, weight, weight, down, down,
                  whole(uq.shape), whole(uv.shape)],
        out_specs=[whole(s) for s in shapes],
        out_shape=[jax.ShapeDtypeStruct(s, bf16) for s in shapes],
        scratch_shapes=[pltpu.VMEM((rows, cols), f32)] * 3 + [pltpu.VMEM((rows, 2 * RANK), f32)],
        compiler_params=PARAMS,
        cost_estimate=pl.CostEstimate(flops=2 * rows * width * 1024, bytes_accessed=13 << 20, transcendentals=0),
        name="project",
    )(pos, act, wq, wk, wv, dq, dv, uq, uv)


def lists_kernel(pos, slot, levels, order, out):
    x, y, c = pos[0], pos[1], pos[2]

    def frame(xx, yy, local):
        core = c if local < 2 else 1 - c
        return slot[((xx * 4 + yy) * 2 + core) * 2 + local % 2]

    for k in range(16):
        out[17, k] = frame(lax.rem(x + 4 - k // 4, 4), y, k % 4)
        out[18, k] = frame(x, lax.rem(y + 4 - k // 4, 4), k % 4)

    def one(q, _):
        f = out[18, q]

        def pair(k, n):
            g = out[17, k]
            for r in range(4):
                out[q, n + r] = k * 4 + order[f, g * 4 + r]
            return n + levels[f, g]

        n = lax.fori_loop(0, 16, pair, 0)
        for r in range(CB):
            out[q, n + r] = 0
        out[16, q] = n
        return 0

    lax.fori_loop(0, 16, one, 0)


def visible_lists(pos, slot, levels, order):
    return pl.pallas_call(
        lists_kernel,
        in_specs=[SMEM] * 4,
        out_specs=SMEM,
        out_shape=jax.ShapeDtypeStruct((24, 128), jnp.int32),
        name="lists",
    )(pos, slot, levels, order.reshape(64, 256))


def load_chunk(lists, f, ch, kvall, kvc):
    for i in range(CB):
        at = pl.multiple_of(lists[f, ch * CB + i] * BLK, BLK)
        kvc[i * BLK:(i + 1) * BLK, :] = kvall[pl.ds(at, BLK), :]


def fill_all(parts, whole):
    rows = parts[0].shape[0]
    for d, part in enumerate(parts):
        whole[d * rows:(d + 1) * rows, :] = part[...]


def stats_kernel(lists, q0, q1, q2, q3, g0, g1, g2, g3, k0, k1, k2, k3, out, qall, gall, kvall, kvc, both):
    fill_all((q0, q1, q2, q3), qall)
    fill_all((g0, g1, g2, g3), gall)
    fill_all((k0, k1, k2, k3), kvall)
    both[...] = jnp.zeros_like(both)
    row = lax.broadcasted_iota(jnp.int32, (CHUNK, HEAD), 0)

    def frame(f, _):
        at = pl.multiple_of(f * FT, FT)
        both[:FT, :HEAD] = qall[pl.ds(at, FT), :]
        both[FT:, HEAD:] = gall[pl.ds(at, FT), :]
        n = lists[16, f]

        def chunk(ch, carry):
            peak, total, delta = carry
            load_chunk(lists, f, ch, kvall, kvc)
            r = dot(kvc[...], both[...], 1, 1)
            s = jnp.where(row < (n - ch * CB) * BLK, r[:, :FT] * SCALE2, NEG)
            new = jnp.maximum(peak, jnp.max(s, axis=0, keepdims=True))
            p = jnp.exp2(s - new)
            fix = jnp.exp2(peak - new)
            total = total * fix + jnp.sum(p, axis=0, keepdims=True)
            delta = delta * fix + jnp.sum(p * r[:, FT:], axis=0, keepdims=True)
            return new, total, delta

        zero = jnp.zeros((1, FT), f32)
        peak, total, delta = lax.fori_loop(0, (n + CB - 1) // CB, chunk, (zero + NEG, zero, zero))
        out[pl.ds(f, 1), :] = peak
        out[pl.ds(16 + f, 1), :] = total
        out[pl.ds(32 + f, 1), :] = delta
        return 0

    lax.fori_loop(0, 16, frame, 0)


def row_stats(lists, qs, gs, kvs):
    return pl.pallas_call(
        stats_kernel,
        in_specs=[SMEM] + [VMEM] * 12,
        out_specs=VMEM,
        out_shape=jax.ShapeDtypeStruct((48, 128), f32),
        scratch_shapes=[pltpu.VMEM((2048, HEAD), bf16), pltpu.VMEM((2048, HEAD), bf16),
                        pltpu.VMEM((2048, 2 * HEAD), bf16), pltpu.VMEM((CHUNK, 2 * HEAD), bf16),
                        pltpu.VMEM((2 * FT, 2 * HEAD), bf16)],
        compiler_params=PARAMS,
        name="row_stats",
    )(lists, *qs, *gs, *kvs)


def grads_kernel(lists, s0, s1, s2, s3, q0, q1, q2, q3, g0, g1, g2, g3, k0, k1, k2, k3,
                 a0, a1, a2, a3, b0, b1, b2, b3, qall, gall, kvall, kvc, both, pair, acc, dva, norm):
    fill_all((q0, q1, q2, q3), qall)
    fill_all((g0, g1, g2, g3), gall)
    fill_all((k0, k1, k2, k3), kvall)
    both[...] = jnp.zeros_like(both)
    dva[...] = jnp.zeros_like(dva)
    for t in range(4):
        rows = [slice(4 * ((t - d) % 4), 4 * ((t - d) % 4) + 4) for d in range(4)]
        stats = [ref[...] for ref in (s0, s1, s2, s3)]
        peaks = [stats[d][0:16][rows[d]] for d in range(4)]
        peak = jnp.maximum(jnp.maximum(peaks[0], peaks[1]), jnp.maximum(peaks[2], peaks[3]))
        total = jnp.zeros_like(peak)
        delta = jnp.zeros_like(peak)
        for d in range(4):
            fix = jnp.exp2(peaks[d] - peak)
            total += fix * stats[d][16:32][rows[d]]
            delta += fix * stats[d][32:48][rows[d]]
        norm[4 * t:4 * t + 4, :] = peak + jnp.log2(total)
        norm[16 + 4 * t:20 + 4 * t, :] = delta / total
    row = lax.broadcasted_iota(jnp.int32, (CHUNK, HEAD), 0)

    def frame(f, _):
        at = pl.multiple_of(f * FT, FT)
        both[:FT, :HEAD] = qall[pl.ds(at, FT), :]
        both[FT:, HEAD:] = gall[pl.ds(at, FT), :]
        n = lists[16, f]
        lse = norm[pl.ds(f, 1), :]
        delta = norm[pl.ds(16 + f, 1), :]
        acc[pl.ds(at, FT), :] = jnp.zeros((FT, 2 * HEAD), f32)

        def chunk(ch, _):
            load_chunk(lists, f, ch, kvall, kvc)
            kv = kvc[...]
            r = dot(kv, both[...], 1, 1)
            s = jnp.where(row < (n - ch * CB) * BLK, r[:, :FT] * SCALE2, NEG)
            p = jnp.exp2(s - lse)
            low = p.astype(bf16)
            pair[:, :FT] = low
            pair[:, FT:] = (p * (r[:, FT:] - delta) * SCALE).astype(bf16)
            product = dot(pair[...], kv, 0, 0)
            acc[pl.ds(at, FT), :HEAD] += product[:FT, HEAD:]
            acc[pl.ds(at, FT), HEAD:] += product[FT:, :HEAD]
            dv = dot(low, gall[pl.ds(at, FT), :])
            for i in range(CB):
                to = pl.multiple_of(lists[f, ch * CB + i] * BLK, BLK)
                dva[pl.ds(to, BLK), :] += dv[i * BLK:(i + 1) * BLK, :]
            return 0

        lax.fori_loop(0, (n + CB - 1) // CB, chunk, 0)
        return 0

    lax.fori_loop(0, 16, frame, 0)
    for d, (a, b) in enumerate(zip((a0, a1, a2, a3), (b0, b1, b2, b3))):
        a[...] = acc[d * 512:(d + 1) * 512, :].astype(a.dtype)
        b[...] = dva[d * 512:(d + 1) * 512, :].astype(b.dtype)


def attention_grads(lists, stats, qs, gs, kvs):
    wire = [f32, WIRE, WIRE, WIRE]
    return pl.pallas_call(
        grads_kernel,
        in_specs=[SMEM] + [VMEM] * 16,
        out_specs=[VMEM] * 8,
        out_shape=[jax.ShapeDtypeStruct((512, 2 * HEAD), t) for t in wire]
        + [jax.ShapeDtypeStruct((512, HEAD), t) for t in wire],
        scratch_shapes=[pltpu.VMEM((2048, HEAD), bf16), pltpu.VMEM((2048, HEAD), bf16),
                        pltpu.VMEM((2048, 2 * HEAD), bf16), pltpu.VMEM((CHUNK, 2 * HEAD), bf16),
                        pltpu.VMEM((2 * FT, 2 * HEAD), bf16), pltpu.VMEM((CHUNK, 2 * FT), bf16),
                        pltpu.VMEM((2048, 2 * HEAD), f32), pltpu.VMEM((2048, HEAD), f32),
                        pltpu.VMEM((32, 128), f32)],
        compiler_params=PARAMS,
        name="attention_grads",
    )(lists, *stats, *qs, *gs, *kvs)


def finish_kernel(pos, a0, a1, a2, a3, b0, b1, b2, b3, rank_own, rank_other, uq, uv,
                  o_keep, o_send, rg_keep, rg_send, up):
    total = a0[...] + a1[...].astype(f32) + a2[...].astype(f32) + a3[...].astype(f32)
    out = total[:, :HEAD].astype(bf16)
    dq = total[:, HEAD:].astype(bf16)
    dv = (b0[...] + b1[...].astype(f32) + b2[...].astype(f32) + b3[...].astype(f32)).astype(bf16)
    o_keep[...] = out[:256]
    o_send[...] = out[256:]

    def rest(c):
        at = c * HEAD
        upq = uq[:, at:at + HEAD]
        upv = uv[:, at:at + HEAD]
        gq = dot(dq, upq, 1, 1)
        gv = dot(dv, upv, 1, 1)
        rg_keep[:, :RANK] = gq[:256]
        rg_keep[:, RANK:] = gv[:256]
        rg_send[:, :RANK] = gq[256:]
        rg_send[:, RANK:] = gv[256:]
        up[...] = jnp.zeros_like(up)
        up[:RANK, at:at + HEAD] = (dot(rank_own[:, :RANK], dq[:256], 0, 0)
                                   + dot(rank_other[:, :RANK], dq[256:], 0, 0))
        up[RANK:, at:at + HEAD] = (dot(rank_own[:, RANK:], dv[:256], 0, 0)
                                   + dot(rank_other[:, RANK:], dv[256:], 0, 0))

    for c in range(2):
        pl.when(pos[2] == c)(lambda c=c: rest(c))


def finish(pos, a, b, rank_own, rank_other, uq, uv):
    shapes = [((256, HEAD), bf16), ((256, HEAD), bf16), ((256, 256), f32), ((256, 256), f32), ((256, 256), f32)]
    return pl.pallas_call(
        finish_kernel,
        in_specs=[SMEM] + [VMEM] * 12,
        out_specs=[VMEM] * 5,
        out_shape=[jax.ShapeDtypeStruct(s, t) for s, t in shapes],
        compiler_params=PARAMS,
        name="finish",
    )(pos, *a, *b, rank_own, rank_other, uq, uv)


def ring(n, d):
    return [(i, (i + d) % n) for i in range(n)]


def swap(a):
    return lax.ppermute(a, "c", ring(2, 1))


def spread(a, axis):
    return [a] + [lax.ppermute(a, axis, ring(4, d)) for d in (1, 3, 2)]


def reorder(parts):
    return [parts[0], parts[1], parts[3], parts[2]]


def collect(parts, axis):
    return [parts[0]] + [lax.ppermute(parts[d], axis, ring(4, -d)) for d in (1, 2, 3)]


def half(a, index, size):
    return lax.dynamic_slice_in_dim(a, index * size, size, axis=1)


def local(act, wq, wk, wv, dq, uq, dv, uv, grad_out, levels, order, slot):
    x, y, c, z = (lax.axis_index(n).astype(jnp.int32) for n in ("x", "y", "c", "z"))
    pos = jnp.stack([x, y, c, z])
    g_other = swap(half(grad_out, 1 - c, HEAD))
    g = jnp.concatenate([half(grad_out, c, HEAD), g_other], axis=0)
    gs = reorder(spread(g, "y"))
    kv_keep, kv_send, q_keep, q_send, rank = project(pos, act, wq, wk, wv, dq, dv, uq, uv)
    kv = jnp.concatenate([kv_keep, swap(kv_send)], axis=0)
    kvs = reorder(spread(kv, "x"))
    q = jnp.concatenate([q_keep, swap(q_send)], axis=0)
    qs = reorder(spread(q, "y"))
    rank_other = swap(rank)
    lists = visible_lists(pos, slot, levels, order)
    stats = reorder(spread(row_stats(lists, qs, gs, kvs), "y"))
    parts = attention_grads(lists, stats, qs, gs, kvs)
    a = collect(parts[:4], "y")
    b = collect(parts[4:], "x")
    o_keep, o_send, rg_keep, rg_send, up = finish(pos, a, b, rank, rank_other, uq, uv)
    rg = rg_keep + swap(rg_send)
    rgs = spread(rg, "z")
    rank_grad = (rgs[0] + rgs[1] + rgs[2] + rgs[3]).astype(bf16)
    up = lax.psum(up, ("x", "y", "c"))
    o_other = swap(o_send)
    attended = jnp.where(c == 0, jnp.concatenate([o_keep, o_other], axis=1),
                         jnp.concatenate([o_other, o_keep], axis=1))
    cols = act.shape[1] // 4
    down = dot(half(act, z, cols), rank_grad, 0, 0)
    mine = lax.dynamic_slice_in_dim(down, c * (cols // 2), cols // 2, axis=0)
    theirs = swap(lax.dynamic_slice_in_dim(down, (1 - c) * (cols // 2), cols // 2, axis=0))
    down = lax.all_to_all(mine + theirs, ("x", "y"), 0, 0, tiled=True)
    down = jnp.sum(down.reshape(16, cols // 32, 256), axis=0).astype(bf16)
    wide = jnp.broadcast_to(down[None], (64, cols // 32, 256)).reshape(2 * cols, 256)
    wide = lax.all_to_all(wide, ("z", "x", "y"), 0, 0, tiled=True)
    other = swap(wide)
    first = jnp.where(c == 0, wide, other).reshape(4, 1, cols // 2, 256)
    second = jnp.where(c == 0, other, wide).reshape(4, 1, cols // 2, 256)
    full = jnp.concatenate([first, second], axis=1).reshape(4 * cols, 256).astype(f32)
    return attended, full[:, :RANK], up[:RANK], full[:, RANK:], up[RANK:]


def solution(mesh):
    torus = Mesh(mesh.devices.reshape(4, 4, 2, 4), ("x", "y", "c", "z"))
    tm = ("x", "y", "c")
    return jax.shard_map(
        local,
        mesh=torus,
        in_specs=(
            P(tm, None),
            P(None, "z"),
            P(None, "z"),
            P(None, "z"),
            P(),
            P(None, "z"),
            P(),
            P(None, "z"),
            P(tm, "z"),
            P(),
            P(),
            P(),
        ),
        out_specs=(P(tm, "z"), P(), P(None, "z"), P(), P(None, "z")),
        check_vma=False,
    )
```

```python
import math

import jax
import jax.numpy as jnp
from jax import lax
from jax.experimental import pallas as pl
from jax.experimental.pallas import tpu as pltpu
from jax.sharding import Mesh
from jax.sharding import PartitionSpec as P

HEAD = 128
FT = 128
BLK = 32
RANK = 128
CHUNK = 512
CB = CHUNK // BLK
CHAINS = 4
SCALE = HEAD ** -0.5
SCALE2 = SCALE * math.log2(math.e)
NEG = -1e30
f32 = jnp.float32
bf16 = jnp.bfloat16
WIRE = bf16
KT = 1280
VMEM = pl.BlockSpec(memory_space=pltpu.VMEM)
SMEM = pl.BlockSpec(memory_space=pltpu.SMEM)
ANY = pl.BlockSpec(memory_space=pl.ANY)
WIDE = pltpu.CompilerParams(vmem_limit_bytes=60 * 1024 * 1024)
PARAMS = pltpu.CompilerParams(vmem_limit_bytes=48 * 1024 * 1024)


def dot(a, b, ca=1, cb=0):
    return lax.dot_general(a, b, (((ca,), (cb,)), ((), ())), preferred_element_type=f32)


def by_core(pos, put, keep, send):
    for c in range(2):
        @pl.when(pos[2] == c)
        def _():
            put(keep, c * HEAD)
            put(send, (1 - c) * HEAD)


def kv_kernel(pos, act, wk, wv, down, up, after0, after1, keep, send, rank, ak, av, ar):
    step = pl.program_id(0)
    last = pl.num_programs(0) - 1
    a = act[...]
    parts = [(ak, wk), (av, wv), (ar, down)]

    @pl.when(step == 0)
    def _():
        for total, w in parts:
            total[...] = dot(a, w[...])

    @pl.when(step > 0)
    def _():
        for total, w in parts:
            total[...] += dot(a, w[...])

    @pl.when(step == last)
    def _():
        low = ar[...].astype(bf16)
        rank[...] = low
        keys = ak[...].astype(bf16)
        values = (av[...] + dot(low, up[...])).astype(bf16)

        def put(ref, at):
            ref[:, :HEAD] = keys[:, at:at + HEAD]
            ref[:, HEAD:] = values[:, at:at + HEAD]

        by_core(pos, put, keep, send)


def q_kernel(pos, act, wq, down, up, after0, after1, after2, after3, keep, send, rank, aq, ar):
    step = pl.program_id(0)
    last = pl.num_programs(0) - 1
    a = act[...]
    parts = [(aq, wq), (ar, down)]

    @pl.when(step == 0)
    def _():
        for total, w in parts:
            total[...] = dot(a, w[...])

    @pl.when(step > 0)
    def _():
        for total, w in parts:
            total[...] += dot(a, w[...])

    @pl.when(step == last)
    def _():
        low = ar[...].astype(bf16)
        rank[...] = low
        query = (aq[...] + dot(low, up[...])).astype(bf16)

        def put(ref, at):
            ref[...] = query[:, at:at + HEAD]

        by_core(pos, put, keep, send)


def project(kernel, name, pos, act, weights, down, up, lanes, after):
    rows, width = act.shape
    cols = weights[0].shape[1]
    n = len(weights)
    whole = lambda shape: pl.BlockSpec(shape, lambda k: (0, 0))
    shapes = [(rows, lanes), (rows, lanes), (rows, RANK)]
    return pl.pallas_call(
        kernel,
        grid=(width // KT,),
        in_specs=[SMEM, pl.BlockSpec((rows, KT), lambda k: (0, k))]
        + [pl.BlockSpec((KT, cols), lambda k: (k, 0))] * n
        + [pl.BlockSpec((KT, RANK), lambda k: (k, 0)), whole(up.shape)] + [ANY] * len(after),
        out_specs=[whole(s) for s in shapes],
        out_shape=[jax.ShapeDtypeStruct(s, bf16) for s in shapes],
        scratch_shapes=[pltpu.VMEM((rows, cols), f32)] * n + [pltpu.VMEM((rows, RANK), f32)],
        compiler_params=WIDE,
        cost_estimate=pl.CostEstimate(flops=2 * rows * width * (n * cols + RANK),
                                      bytes_accessed=2 * width * (rows + n * cols + RANK), transcendentals=0),
        name=name,
    )(pos, act, *weights, down, up, *after)


def project_kv(pos, act, wk, wv, dv, uv, *after):
    return project(kv_kernel, "project_kv", pos, act, [wk, wv], dv, uv, 2 * HEAD, after)


def project_q(pos, act, wq, dq, uq, *after):
    return project(q_kernel, "project_q", pos, act, [wq], dq, uq, HEAD, after)


def lists_kernel(pos, slot, packed, out):
    x, y, c = pos[0], pos[1], pos[2]

    def frame(xx, yy, local):
        core = c if local < 2 else 1 - c
        return slot[((xx * 4 + yy) * 2 + core) * 2 + local % 2]

    keys = [frame(lax.rem(x + 4 - k // 4, 4), y, k % 4) for k in range(16)]
    for q in range(16):
        out[17, q] = frame(x, lax.rem(y + 4 - q // 4, 4), q % 4)

    def one(q, _):
        f = out[17, q]
        n = 0
        for k in range(16):
            word = packed[f, keys[k]]
            for r in range(4):
                out[q, n + r] = k * 4 + ((word >> (2 * r)) & 3)
            n = n + (word >> 8)
        for r in range(CB):
            out[q, n + r] = 0
        out[16, q] = n
        return 0

    lax.fori_loop(0, 16, one, 0)


def visible_lists(pos, slot, levels, order):
    packed = levels * 256 + jnp.sum(order * jnp.array([1, 4, 16, 64], jnp.int32), axis=-1)
    return pl.pallas_call(
        lists_kernel,
        in_specs=[SMEM] * 3,
        out_specs=SMEM,
        out_shape=jax.ShapeDtypeStruct((24, 128), jnp.int32),
        name="lists",
    )(pos, slot, packed)


def fill_all(parts, whole):
    rows = parts[0].shape[0]
    for d, part in enumerate(parts):
        whole[d * rows:(d + 1) * rows, :] = part[...]


def load_chunk(lists, f, at, kvall):
    blocks = [kvall[pl.ds(pl.multiple_of(lists[f, at + i] * BLK, BLK), BLK), :] for i in range(CB)]
    return jnp.concatenate(blocks, axis=0)


def start_frames(lists, t, qall, gall, both):
    counts = []
    for j in range(CHAINS):
        f = t * CHAINS + j
        at = pl.multiple_of(f * FT, FT)
        both[j, :FT, :HEAD] = qall[pl.ds(at, FT), :]
        both[j, FT:, HEAD:] = gall[pl.ds(at, FT), :]
        counts.append(lists[16, f])
    chunks = [(n + CB - 1) // CB for n in counts]
    most = chunks[0]
    for n in chunks[1:]:
        most = jnp.maximum(most, n)
    return counts, chunks, most


def stats_kernel(lists, q0, q1, q2, q3, g0, g1, g2, g3, k0, k1, k2, k3, out, qall, gall, kvall, both):
    fill_all((q0, q1, q2, q3), qall)
    fill_all((g0, g1, g2, g3), gall)
    fill_all((k0, k1, k2, k3), kvall)
    both[...] = jnp.zeros_like(both)
    row = lax.broadcasted_iota(jnp.int32, (CHUNK, HEAD), 0)

    def frames(t, _):
        counts, chunks, most = start_frames(lists, t, qall, gall, both)

        def chunk(ch, carry):
            kvs = [load_chunk(lists, t * CHAINS + j, jnp.minimum(ch, chunks[j] - 1) * CB, kvall)
                   for j in range(CHAINS)]
            rs = [dot(kvs[j], both[j], 1, 1) for j in range(CHAINS)]
            after = []
            for j in range(CHAINS):
                peak, total, delta = carry[j]
                s = jnp.where(row < (counts[j] - ch * CB) * BLK, rs[j][:, :FT] * SCALE2, NEG)
                new = jnp.maximum(peak, jnp.max(s, axis=0, keepdims=True))
                p = jnp.exp2(s - new)
                fix = jnp.exp2(peak - new)
                total = total * fix + jnp.sum(p, axis=0, keepdims=True)
                delta = delta * fix + jnp.sum(p * rs[j][:, FT:], axis=0, keepdims=True)
                after.append((new, total, delta))
            return tuple(after)

        zero = jnp.zeros((1, FT), f32)
        carry = lax.fori_loop(0, most, chunk, ((zero + NEG, zero, zero),) * CHAINS)
        for j in range(CHAINS):
            for i in range(3):
                out[pl.ds(16 * i + t * CHAINS + j, 1), :] = carry[j][i]
        return 0

    lax.fori_loop(0, 16 // CHAINS, frames, 0)


def row_stats(lists, qs, gs, kvs):
    return pl.pallas_call(
        stats_kernel,
        in_specs=[SMEM] + [VMEM] * 12,
        out_specs=VMEM,
        out_shape=jax.ShapeDtypeStruct((48, 128), f32),
        scratch_shapes=[pltpu.VMEM((2048, HEAD), bf16), pltpu.VMEM((2048, HEAD), bf16),
                        pltpu.VMEM((2048, 2 * HEAD), bf16), pltpu.VMEM((CHAINS, 2 * FT, 2 * HEAD), bf16)],
        compiler_params=PARAMS,
        name="row_stats",
    )(lists, *qs, *gs, *kvs)


def grads_kernel(lists, s0, s1, s2, s3, q0, q1, q2, q3, g0, g1, g2, g3, k0, k1, k2, k3,
                 a0, a1, a2, a3, b0, b1, b2, b3, qall, gall, kvall, both, acc, dva, norm):
    fill_all((q0, q1, q2, q3), qall)
    fill_all((g0, g1, g2, g3), gall)
    fill_all((k0, k1, k2, k3), kvall)
    both[...] = jnp.zeros_like(both)
    dva[...] = jnp.zeros_like(dva)
    for t in range(4):
        rows = [slice(4 * ((t - d) % 4), 4 * ((t - d) % 4) + 4) for d in range(4)]
        stats = [ref[...] for ref in (s0, s1, s2, s3)]
        peaks = [stats[d][0:16][rows[d]] for d in range(4)]
        peak = jnp.maximum(jnp.maximum(peaks[0], peaks[1]), jnp.maximum(peaks[2], peaks[3]))
        total = jnp.zeros_like(peak)
        delta = jnp.zeros_like(peak)
        for d in range(4):
            fix = jnp.exp2(peaks[d] - peak)
            total += fix * stats[d][16:32][rows[d]]
            delta += fix * stats[d][32:48][rows[d]]
        norm[4 * t:4 * t + 4, :] = peak + jnp.log2(total)
        norm[16 + 4 * t:20 + 4 * t, :] = delta / total
    row = lax.broadcasted_iota(jnp.int32, (CHUNK, HEAD), 0)

    def frames(t, _):
        counts, chunks, most = start_frames(lists, t, qall, gall, both)
        lse = [norm[pl.ds(t * CHAINS + j, 1), :] for j in range(CHAINS)]
        delta = [norm[pl.ds(16 + t * CHAINS + j, 1), :] for j in range(CHAINS)]
        acc[...] = jnp.zeros_like(acc)

        def chunk(ch, _):
            at = [jnp.minimum(ch, chunks[j] - 1) * CB for j in range(CHAINS)]
            kvs = [load_chunk(lists, t * CHAINS + j, at[j], kvall) for j in range(CHAINS)]
            rs = [dot(kvs[j], both[j], 1, 1) for j in range(CHAINS)]
            lows, pairs = [], []
            for j in range(CHAINS):
                s = jnp.where(row < (counts[j] - ch * CB) * BLK, rs[j][:, :FT] * SCALE2, NEG)
                p = jnp.exp2(s - lse[j])
                low = p.astype(bf16)
                ds = (p * (rs[j][:, FT:] - delta[j]) * SCALE).astype(bf16)
                lows.append(low)
                pairs.append(jnp.concatenate([low, ds], axis=1))
            for j in range(CHAINS):
                product = dot(kvs[j], pairs[j], 0, 0)
                acc[j, 0] += product[HEAD:, :FT]
                acc[j, 1] += product[:HEAD, FT:]
            dvs = [dot(lows[j], both[j, FT:, HEAD:]) for j in range(CHAINS)]
            for i in range(CB):
                for j in range(CHAINS):
                    to = pl.multiple_of(lists[t * CHAINS + j, at[j] + i] * BLK, BLK)
                    dva[j, pl.ds(to, BLK), :] += dvs[j][i * BLK:(i + 1) * BLK, :]
            return 0

        lax.fori_loop(0, most, chunk, 0)
        for j in range(CHAINS):
            f = t * CHAINS + j
            at = pl.multiple_of(lax.rem(f, 4) * FT, FT)
            for d, a in enumerate((a0, a1, a2, a3)):
                def put():
                    a[pl.ds(at, FT), :HEAD] = acc[j, 0].T.astype(a.dtype)
                    a[pl.ds(at, FT), HEAD:] = acc[j, 1].T.astype(a.dtype)

                pl.when(f // 4 == d)(put)
        return 0

    lax.fori_loop(0, 16 // CHAINS, frames, 0)
    for d, b in enumerate((b0, b1, b2, b3)):
        total = dva[0, d * 512:(d + 1) * 512, :]
        for j in range(1, CHAINS):
            total += dva[j, d * 512:(d + 1) * 512, :]
        b[...] = total.astype(b.dtype)


def attention_grads(lists, stats, qs, gs, kvs):
    wire = [f32, WIRE, WIRE, WIRE]
    return pl.pallas_call(
        grads_kernel,
        in_specs=[SMEM] + [VMEM] * 16,
        out_specs=[VMEM] * 8,
        out_shape=[jax.ShapeDtypeStruct((512, 2 * HEAD), t) for t in wire]
        + [jax.ShapeDtypeStruct((512, HEAD), t) for t in wire],
        scratch_shapes=[pltpu.VMEM((2048, HEAD), bf16), pltpu.VMEM((2048, HEAD), bf16),
                        pltpu.VMEM((2048, 2 * HEAD), bf16), pltpu.VMEM((CHAINS, 2 * FT, 2 * HEAD), bf16),
                        pltpu.VMEM((CHAINS, 2, HEAD, FT), f32), pltpu.VMEM((CHAINS, 2048, HEAD), f32),
                        pltpu.VMEM((32, 128), f32)],
        compiler_params=PARAMS,
        name="attention_grads",
    )(lists, *stats, *qs, *gs, *kvs)


def finish_kernel(pos, a0, a1, a2, a3, b0, b1, b2, b3, rq_own, rq_other, rv_own, rv_other, uq, uv,
                  o_keep, o_send, rg_keep, rg_send, up):
    total = a0[...] + a1[...].astype(f32) + a2[...].astype(f32) + a3[...].astype(f32)
    out = total[:, :HEAD].astype(bf16)
    dq = total[:, HEAD:].astype(bf16)
    dv = (b0[...] + b1[...].astype(f32) + b2[...].astype(f32) + b3[...].astype(f32)).astype(bf16)
    o_keep[...] = out[:256]
    o_send[...] = out[256:]
    up[:, :HEAD] = dot(rq_own[...], dq[:256], 0, 0) + dot(rq_other[...], dq[256:], 0, 0)
    up[:, HEAD:] = dot(rv_own[...], dv[:256], 0, 0) + dot(rv_other[...], dv[256:], 0, 0)
    for c in range(2):
        @pl.when(pos[2] == c)
        def _():
            gq = dot(dq, uq[:, c * HEAD:(c + 1) * HEAD], 1, 1)
            gv = dot(dv, uv[:, c * HEAD:(c + 1) * HEAD], 1, 1)
            rg_keep[:, :RANK] = gq[:256]
            rg_keep[:, RANK:] = gv[:256]
            rg_send[:, :RANK] = gq[256:]
            rg_send[:, RANK:] = gv[256:]


def finish(pos, a, b, ranks, uq, uv):
    shapes = [((256, HEAD), bf16), ((256, HEAD), bf16), ((256, 256), f32), ((256, 256), f32), ((128, 256), f32)]
    return pl.pallas_call(
        finish_kernel,
        in_specs=[SMEM] + [VMEM] * 14,
        out_specs=[VMEM] * 5,
        out_shape=[jax.ShapeDtypeStruct(s, t) for s, t in shapes],
        compiler_params=PARAMS,
        name="finish",
    )(pos, *a, *b, *ranks, uq, uv)


def quarter_kernel(pos, keep, other, r0, r1, r2, r3):
    for d, out in enumerate((r0, r1, r2, r3)):
        at = pl.multiple_of(lax.rem(pos[3] + d, 4) * 64, 64)
        out[...] = keep[pl.ds(at, 64), :] + other[pl.ds(at, 64), :]


def quarters(pos, keep, other):
    return pl.pallas_call(
        quarter_kernel,
        in_specs=[SMEM, VMEM, VMEM],
        out_specs=[VMEM] * 4,
        out_shape=[jax.ShapeDtypeStruct((64, 256), f32)] * 4,
        compiler_params=PARAMS,
        name="quarters",
    )(pos, keep, other)


def down_kernel(pos, act_t, r0, r1, r2, r3, mine, theirs, rg):
    for d, r in enumerate((r0, r1, r2, r3)):
        at = pl.multiple_of(lax.rem(pos[3] + 4 - d, 4) * 64, 64)
        rg[pl.ds(at, 64), :] = r[...]
    rows = mine.shape[0]
    for c in range(2):
        @pl.when(pos[2] == c)
        def _():
            mine[...] = dot(act_t[c * rows:(c + 1) * rows, :], rg[...])
            theirs[...] = dot(act_t[(1 - c) * rows:(2 - c) * rows, :], rg[...])


def down_terms(pos, act_t, rgs):
    rows = act_t.shape[0] // 2
    return pl.pallas_call(
        down_kernel,
        in_specs=[SMEM] + [VMEM] * 5,
        out_specs=[VMEM] * 2,
        out_shape=[jax.ShapeDtypeStruct((rows, 256), f32)] * 2,
        scratch_shapes=[pltpu.VMEM((256, 256), bf16)],
        compiler_params=PARAMS,
        name="down_terms",
    )(pos, act_t, *rgs)


def pack_kernel(mine, theirs, up, out):
    for i in range(16):
        out[i, :40, :] = mine[i * 40:(i + 1) * 40, :] + theirs[i * 40:(i + 1) * 40, :]
        out[i, 40:, :] = up[i * 8:(i + 1) * 8, :]


def pack(mine, theirs, up):
    return pl.pallas_call(
        pack_kernel,
        in_specs=[VMEM] * 3,
        out_specs=VMEM,
        out_shape=jax.ShapeDtypeStruct((16, 48, 256), f32),
        compiler_params=PARAMS,
        name="pack",
    )(mine, theirs, up)


def emit_kernel(pos, own, other, o_keep, o_other, att, down_q, up_q, down_v, up_v):
    zz = pl.program_id(0)
    halves = [own, other]
    for c in range(2):
        @pl.when(pos[2] == c)
        def _():
            for cc in range(2):
                src = halves[(c + cc) % 2]
                for i in range(16):
                    part = src[zz * 16 + i].astype(f32)
                    at = cc * 640 + i * 40
                    down_q[at:at + 40, :] = part[:40, :RANK]
                    down_v[at:at + 40, :] = part[:40, RANK:]

            @pl.when(zz == 0)
            def _():
                outs = [o_keep, o_other]
                for cc in range(2):
                    src = halves[(c + cc) % 2]
                    att[:, cc * HEAD:(cc + 1) * HEAD] = outs[(c + cc) % 2][...]
                    for i in range(16):
                        part = src[pos[3] * 16 + i].astype(f32)
                        up_q[i * 8:(i + 1) * 8, cc * HEAD:(cc + 1) * HEAD] = part[40:, :HEAD]
                        up_v[i * 8:(i + 1) * 8, cc * HEAD:(cc + 1) * HEAD] = part[40:, HEAD:]


def emit(pos, own, other, o_keep, o_other):
    whole = lambda a: pl.BlockSpec(a, lambda k: (0,) * len(a))
    return pl.pallas_call(
        emit_kernel,
        grid=(4,),
        in_specs=[SMEM] + [whole(a.shape) for a in (own, other, o_keep, o_other)],
        out_specs=[whole((256, 256)), pl.BlockSpec((1280, RANK), lambda k: (k, 0)), whole((RANK, 256)),
                   pl.BlockSpec((1280, RANK), lambda k: (k, 0)), whole((RANK, 256))],
        out_shape=[jax.ShapeDtypeStruct((256, 256), bf16), jax.ShapeDtypeStruct((5120, RANK), f32),
                   jax.ShapeDtypeStruct((RANK, 256), f32), jax.ShapeDtypeStruct((5120, RANK), f32),
                   jax.ShapeDtypeStruct((RANK, 256), f32)],
        compiler_params=PARAMS,
        name="emit",
    )(pos, own, other, o_keep, o_other)


def ring(n, d):
    return [(i, (i + d) % n) for i in range(n)]


def swap(a):
    return lax.ppermute(a, "c", ring(2, 1))


def spread(a, axis):
    one, three, two = [lax.ppermute(a, axis, ring(4, d)) for d in (1, 3, 2)]
    return [a, one, two, three]


def collect(parts, axis):
    return [parts[0]] + [lax.ppermute(parts[d], axis, ring(4, -d)) for d in (1, 2, 3)]


def half(a, index, size):
    return lax.dynamic_slice_in_dim(a, index * size, size, axis=1)


def local(act, wq, wk, wv, dq, uq, dv, uv, grad_out, levels, order, slot):
    x, y, c, z = (lax.axis_index(n).astype(jnp.int32) for n in ("x", "y", "c", "z"))
    pos = jnp.stack([x, y, c, z])
    g_other = swap(half(grad_out, 1 - c, HEAD))
    lists = visible_lists(pos, slot, levels, order)
    g = jnp.concatenate([half(grad_out, c, HEAD), g_other], axis=0)
    gs = spread(g, "y")
    kv_keep, kv_send, rv = project_kv(pos, act, wk, wv, dv, uv, g, lists)
    kv = jnp.concatenate([kv_keep, swap(kv_send)], axis=0)
    kvs = spread(kv, "x")
    q_keep, q_send, rq = project_q(pos, act, wq, dq, uq, kv, *gs[1:])
    q = jnp.concatenate([q_keep, swap(q_send)], axis=0)
    qs = spread(q, "y")
    act_t = half(act, z, act.shape[1] // 4).T
    stats = spread(row_stats(lists, qs, gs, kvs), "y")
    parts = attention_grads(lists, stats, qs, gs, kvs)
    ranks = (rq, swap(rq), rv, swap(rv))
    a = collect(parts[:4], "y")
    b = collect(parts[4:], "x")
    o_keep, o_send, rg_keep, rg_send, up = finish(pos, a, b, ranks, uq, uv)
    q0, q1, q2, q3 = quarters(pos, rg_keep, swap(rg_send))
    mine = q0 + lax.ppermute(q1, "z", ring(4, 1)) + lax.ppermute(q2, "z", ring(4, 2)) + lax.ppermute(q3, "z", ring(4, 3))
    mine, theirs = down_terms(pos, act_t, spread(mine.astype(bf16), "z"))
    o_other = swap(o_send)
    down = lax.all_to_all(pack(mine, swap(theirs), up), ("x", "y"), 0, 0, tiled=True)
    down = jnp.sum(down, axis=0).astype(bf16)
    wide = jnp.broadcast_to(down[None], (64,) + down.shape)
    wide = lax.all_to_all(wide, ("z", "x", "y"), 0, 0, tiled=True)
    att, down_q, up_q, down_v, up_v = emit(pos, wide, swap(wide), o_keep, o_other)
    return att, down_q, up_q, down_v, up_v


def solution(mesh):
    torus = Mesh(mesh.devices.reshape(4, 4, 2, 4), ("x", "y", "c", "z"))
    tm = ("x", "y", "c")
    return jax.shard_map(
        local,
        mesh=torus,
        in_specs=(
            P(tm, None),
            P(None, "z"),
            P(None, "z"),
            P(None, "z"),
            P(),
            P(None, "z"),
            P(),
            P(None, "z"),
            P(tm, "z"),
            P(),
            P(),
            P(),
        ),
        out_specs=(P(tm, "z"), P(), P(None, "z"), P(), P(None, "z")),
        check_vma=False,
    )
```

```python
import math

import jax
import jax.numpy as jnp
from jax import lax
from jax.experimental import pallas as pl
from jax.experimental.pallas import tpu as pltpu
from jax.sharding import Mesh
from jax.sharding import PartitionSpec as P

HEAD = 128
FT = 128
BLK = 32
RANK = 128
CHUNK = 512
CB = CHUNK // BLK
CHAINS = 4
SCALE = HEAD ** -0.5
SCALE2 = SCALE * math.log2(math.e)
NEG = -1e30
f32 = jnp.float32
bf16 = jnp.bfloat16
WIRE = f32
KT = 1280
VMEM = pl.BlockSpec(memory_space=pltpu.VMEM)
SMEM = pl.BlockSpec(memory_space=pltpu.SMEM)
ANY = pl.BlockSpec(memory_space=pl.ANY)
WIDE = pltpu.CompilerParams(vmem_limit_bytes=60 * 1024 * 1024)
PARAMS = pltpu.CompilerParams(vmem_limit_bytes=48 * 1024 * 1024)


def dot(a, b, ca=1, cb=0):
    return lax.dot_general(a, b, (((ca,), (cb,)), ((), ())), preferred_element_type=f32)


def by_core(pos, put, keep, send):
    for c in range(2):
        @pl.when(pos[2] == c)
        def _():
            put(keep, c * HEAD)
            put(send, (1 - c) * HEAD)


def proj_kernel(pos, act, wq, wk, wv, down_q, down_v, up_q, up_v, keep, send, rank_q, rank_v, aq, ak, av, rq, rv):
    step = pl.program_id(0)
    last = pl.num_programs(0) - 1
    a = act[...]
    parts = [(ak, wk), (av, wv), (rv, down_v), (aq, wq), (rq, down_q)]

    @pl.when(step == 0)
    def _():
        for total, w in parts:
            total[...] = dot(a, w[...])

    @pl.when(step > 0)
    def _():
        for total, w in parts:
            total[...] += dot(a, w[...])

    @pl.when(step == last)
    def _():
        low_q = rq[...].astype(bf16)
        low_v = rv[...].astype(bf16)
        rank_q[...] = low_q
        rank_v[...] = low_v
        keys = ak[...].astype(bf16)
        values = (av[...] + dot(low_v, up_v[...])).astype(bf16)
        query = (aq[...] + dot(low_q, up_q[...])).astype(bf16)

        def put(ref, at):
            ref[:, :HEAD] = keys[:, at:at + HEAD]
            ref[:, HEAD:2 * HEAD] = values[:, at:at + HEAD]
            ref[:, 2 * HEAD:] = query[:, at:at + HEAD]

        by_core(pos, put, keep, send)


def project(pos, act, wq, wk, wv, down_q, down_v, up_q, up_v):
    rows, width = act.shape
    cols = wq.shape[1]
    whole = lambda shape: pl.BlockSpec(shape, lambda k: (0, 0))
    shapes = [(rows, 3 * HEAD), (rows, 3 * HEAD), (rows, RANK), (rows, RANK)]
    return pl.pallas_call(
        proj_kernel,
        grid=(width // KT,),
        in_specs=[SMEM, pl.BlockSpec((rows, KT), lambda k: (0, k))]
        + [pl.BlockSpec((KT, cols), lambda k: (k, 0))] * 3
        + [pl.BlockSpec((KT, RANK), lambda k: (k, 0))] * 2 + [whole(up_q.shape), whole(up_v.shape)],
        out_specs=[whole(s) for s in shapes],
        out_shape=[jax.ShapeDtypeStruct(s, bf16) for s in shapes],
        scratch_shapes=[pltpu.VMEM((rows, cols), f32)] * 3 + [pltpu.VMEM((rows, RANK), f32)] * 2,
        compiler_params=WIDE,
        cost_estimate=pl.CostEstimate(flops=2 * rows * width * (3 * cols + 2 * RANK),
                                      bytes_accessed=2 * width * (rows + 3 * cols + 2 * RANK), transcendentals=0),
        name="project",
    )(pos, act, wq, wk, wv, down_q, down_v, up_q, up_v)


def lists_kernel(pos, slot, packed, out):
    x, y, c = pos[0], pos[1], pos[2]

    def frame(xx, yy, local):
        core = c if local < 2 else 1 - c
        return slot[((xx * 4 + yy) * 2 + core) * 2 + local % 2]

    keys = [frame(lax.rem(x + 4 - k // 4, 4), y, k % 4) for k in range(16)]
    for q in range(16):
        out[17, q] = frame(x, lax.rem(y + 4 - q // 4, 4), q % 4)

    def one(q, _):
        f = out[17, q]
        n = 0
        for k in range(16):
            word = packed[f, keys[k]]
            for r in range(4):
                out[q, n + r] = k * 4 + ((word >> (2 * r)) & 3)
            n = n + (word >> 8)
        for r in range(CB):
            out[q, n + r] = 0
        out[16, q] = n
        return 0

    lax.fori_loop(0, 16, one, 0)


def visible_lists(pos, slot, levels, order):
    packed = levels * 256 + jnp.sum(order * jnp.array([1, 4, 16, 64], jnp.int32), axis=-1)
    return pl.pallas_call(
        lists_kernel,
        in_specs=[SMEM] * 3,
        out_specs=SMEM,
        out_shape=jax.ShapeDtypeStruct((24, 128), jnp.int32),
        name="lists",
    )(pos, slot, packed)


def fill_all(parts, whole):
    rows = parts[0].shape[0]
    for d, part in enumerate(parts):
        whole[d * rows:(d + 1) * rows, :] = part[...]


def fill_grads(pos, gathered, whole):
    for c in range(2):
        @pl.when(pos[2] == c)
        def _():
            for d in range(4):
                chip = lax.rem(pos[1] + 4 - d, 4)
                for i, core in enumerate((c, 1 - c)):
                    at = pl.multiple_of((chip * 2 + core) * 256, 256)
                    to = d * 512 + i * 256
                    whole[to:to + 256, :] = gathered[pl.ds(at, 256), c * HEAD:(c + 1) * HEAD]


def load_chunk(lists, f, at, kvall):
    blocks = [kvall[pl.ds(pl.multiple_of(lists[f, at + i] * BLK, BLK), BLK), :] for i in range(CB)]
    return jnp.concatenate(blocks, axis=0)


def start_frames(lists, t, qall, gall, both):
    counts = []
    for j in range(CHAINS):
        f = t * CHAINS + j
        at = pl.multiple_of(f * FT, FT)
        both[j, :FT, :HEAD] = qall[pl.ds(at, FT), :]
        both[j, FT:, HEAD:] = gall[pl.ds(at, FT), :]
        counts.append(lists[16, f])
    chunks = [(n + CB - 1) // CB for n in counts]
    most = chunks[0]
    for n in chunks[1:]:
        most = jnp.maximum(most, n)
    return counts, chunks, most


def stats_kernel(pos, lists, q0, q1, q2, q3, g, k0, k1, k2, k3, out, qall, gall, kvall, both):
    fill_all((q0, q1, q2, q3), qall)
    fill_grads(pos, g, gall)
    fill_all((k0, k1, k2, k3), kvall)
    both[...] = jnp.zeros_like(both)
    row = lax.broadcasted_iota(jnp.int32, (CHUNK, HEAD), 0)

    def frames(t, _):
        counts, chunks, most = start_frames(lists, t, qall, gall, both)

        def chunk(ch, carry):
            kvs = [load_chunk(lists, t * CHAINS + j, jnp.minimum(ch, chunks[j] - 1) * CB, kvall)
                   for j in range(CHAINS)]
            rs = [dot(kvs[j], both[j], 1, 1) for j in range(CHAINS)]
            after = []
            for j in range(CHAINS):
                peak, total, delta = carry[j]
                s = jnp.where(row < (counts[j] - ch * CB) * BLK, rs[j][:, :FT] * SCALE2, NEG)
                new = jnp.maximum(peak, jnp.max(s, axis=0, keepdims=True))
                p = jnp.exp2(s - new)
                fix = jnp.exp2(peak - new)
                total = total * fix + jnp.sum(p, axis=0, keepdims=True)
                delta = delta * fix + jnp.sum(p * rs[j][:, FT:], axis=0, keepdims=True)
                after.append((new, total, delta))
            return tuple(after)

        zero = jnp.zeros((1, FT), f32)
        carry = lax.fori_loop(0, most, chunk, ((zero + NEG, zero, zero),) * CHAINS)
        for j in range(CHAINS):
            for i in range(3):
                out[pl.ds(16 * i + t * CHAINS + j, 1), :] = carry[j][i]
        return 0

    lax.fori_loop(0, 16 // CHAINS, frames, 0)


def row_stats(pos, lists, qs, g, kvs):
    return pl.pallas_call(
        stats_kernel,
        in_specs=[SMEM, SMEM] + [VMEM] * 9,
        out_specs=VMEM,
        out_shape=jax.ShapeDtypeStruct((48, 128), f32),
        scratch_shapes=[pltpu.VMEM((2048, HEAD), bf16), pltpu.VMEM((2048, HEAD), bf16),
                        pltpu.VMEM((2048, 2 * HEAD), bf16), pltpu.VMEM((CHAINS, 2 * FT, 2 * HEAD), bf16)],
        compiler_params=PARAMS,
        name="row_stats",
    )(pos, lists, *qs, g, *kvs)


def grads_kernel(pos, lists, s0, s1, s2, s3, q0, q1, q2, q3, g, k0, k1, k2, k3,
                 o, a0, a1, a2, a3, b0, b1, b2, b3, qall, gall, kvall, both, acc, dva, norm):
    fill_all((q0, q1, q2, q3), qall)
    fill_grads(pos, g, gall)
    fill_all((k0, k1, k2, k3), kvall)
    both[...] = jnp.zeros_like(both)
    dva[...] = jnp.zeros_like(dva)
    for t in range(4):
        rows = [slice(4 * ((t - d) % 4), 4 * ((t - d) % 4) + 4) for d in range(4)]
        stats = [ref[...] for ref in (s0, s1, s2, s3)]
        peaks = [stats[d][0:16][rows[d]] for d in range(4)]
        peak = jnp.maximum(jnp.maximum(peaks[0], peaks[1]), jnp.maximum(peaks[2], peaks[3]))
        total = jnp.zeros_like(peak)
        delta = jnp.zeros_like(peak)
        for d in range(4):
            fix = jnp.exp2(peaks[d] - peak)
            total += fix * stats[d][16:32][rows[d]]
            delta += fix * stats[d][32:48][rows[d]]
        norm[4 * t:4 * t + 4, :] = peak + jnp.log2(total)
        norm[16 + 4 * t:20 + 4 * t, :] = delta / total
    row = lax.broadcasted_iota(jnp.int32, (CHUNK, HEAD), 0)

    def frames(t, _):
        counts, chunks, most = start_frames(lists, t, qall, gall, both)
        lse = [norm[pl.ds(t * CHAINS + j, 1), :] for j in range(CHAINS)]
        delta = [norm[pl.ds(16 + t * CHAINS + j, 1), :] for j in range(CHAINS)]
        acc[...] = jnp.zeros_like(acc)

        def chunk(ch, _):
            at = [jnp.minimum(ch, chunks[j] - 1) * CB for j in range(CHAINS)]
            kvs = [load_chunk(lists, t * CHAINS + j, at[j], kvall) for j in range(CHAINS)]
            rs = [dot(kvs[j], both[j], 1, 1) for j in range(CHAINS)]
            lows, pairs = [], []
            for j in range(CHAINS):
                s = jnp.where(row < (counts[j] - ch * CB) * BLK, rs[j][:, :FT] * SCALE2, NEG)
                p = jnp.exp2(s - lse[j])
                low = p.astype(bf16)
                ds = (p * (rs[j][:, FT:] - delta[j]) * SCALE).astype(bf16)
                lows.append(low)
                pairs.append(jnp.concatenate([low, ds], axis=1))
            for j in range(CHAINS):
                product = dot(kvs[j], pairs[j], 0, 0)
                acc[j, 0] += product[HEAD:, :FT]
                acc[j, 1] += product[:HEAD, FT:]
            dvs = [dot(lows[j], both[j, FT:, HEAD:]) for j in range(CHAINS)]
            for i in range(CB):
                for j in range(CHAINS):
                    to = pl.multiple_of(lists[t * CHAINS + j, at[j] + i] * BLK, BLK)
                    dva[j, pl.ds(to, BLK), :] += dvs[j][i * BLK:(i + 1) * BLK, :]
            return 0

        lax.fori_loop(0, most, chunk, 0)
        for j in range(CHAINS):
            f = t * CHAINS + j
            at = pl.multiple_of(lax.rem(f, 4) * FT, FT)
            chip = lax.rem(pos[1] + 4 - f // 4, 4)
            o[pl.ds(pl.multiple_of(chip * 512 + at, FT), FT), :] = acc[j, 0].T
            for d, a in enumerate((a0, a1, a2, a3)):
                @pl.when(f // 4 == d)
                def _():
                    a[pl.ds(at, FT), :] = acc[j, 1].T.astype(a.dtype)

        return 0

    lax.fori_loop(0, 16 // CHAINS, frames, 0)
    for d, b in enumerate((b0, b1, b2, b3)):
        total = dva[0, d * 512:(d + 1) * 512, :]
        for j in range(1, CHAINS):
            total += dva[j, d * 512:(d + 1) * 512, :]
        b[...] = total.astype(b.dtype)


def attention_grads(pos, lists, stats, qs, g, kvs):
    wire = [f32, WIRE, WIRE, WIRE]
    return pl.pallas_call(
        grads_kernel,
        in_specs=[SMEM, SMEM] + [VMEM] * 13,
        out_specs=[VMEM] * 9,
        out_shape=[jax.ShapeDtypeStruct((2048, HEAD), f32)]
        + [jax.ShapeDtypeStruct((512, HEAD), t) for t in wire + wire],
        scratch_shapes=[pltpu.VMEM((2048, HEAD), bf16), pltpu.VMEM((2048, HEAD), bf16),
                        pltpu.VMEM((2048, 2 * HEAD), bf16), pltpu.VMEM((CHAINS, 2 * FT, 2 * HEAD), bf16),
                        pltpu.VMEM((CHAINS, 2, HEAD, FT), f32), pltpu.VMEM((CHAINS, 2048, HEAD), f32),
                        pltpu.VMEM((32, 128), f32)],
        compiler_params=PARAMS,
        name="attention_grads",
    )(pos, lists, *stats, *qs, g, *kvs)


def finish_kernel(pos, a0, a1, a2, a3, b0, b1, b2, b3, rq_own, rq_other, rv_own, rv_other, uq, uv,
                  rg_keep, rg_send, up):
    dq = (a0[...] + a1[...].astype(f32) + a2[...].astype(f32) + a3[...].astype(f32)).astype(bf16)
    dv = (b0[...] + b1[...].astype(f32) + b2[...].astype(f32) + b3[...].astype(f32)).astype(bf16)
    for c in range(2):
        @pl.when(pos[2] == c)
        def _():
            gq = dot(dq, uq[:, c * HEAD:(c + 1) * HEAD], 1, 1)
            gv = dot(dv, uv[:, c * HEAD:(c + 1) * HEAD], 1, 1)
            rg_keep[:, :RANK] = gq[:256]
            rg_keep[:, RANK:] = gv[:256]
            rg_send[:, :RANK] = gq[256:]
            rg_send[:, RANK:] = gv[256:]
    up[:, :HEAD] = dot(rq_own[...], dq[:256], 0, 0) + dot(rq_other[...], dq[256:], 0, 0)
    up[:, HEAD:] = dot(rv_own[...], dv[:256], 0, 0) + dot(rv_other[...], dv[256:], 0, 0)


def finish(pos, a, b, ranks, uq, uv):
    return pl.pallas_call(
        finish_kernel,
        in_specs=[SMEM] + [VMEM] * 14,
        out_specs=[VMEM] * 3,
        out_shape=[jax.ShapeDtypeStruct((r, 256), f32) for r in (256, 256, 128)],
        compiler_params=PARAMS,
        name="finish",
    )(pos, *a, *b, *ranks, uq, uv)


def down_kernel(pos, act_t, own, r1, r2, r3, after, mine, theirs):
    rg = (own[...] + r1[...].astype(f32) + r2[...].astype(f32) + r3[...].astype(f32)).astype(bf16)
    rows = mine.shape[0]
    for c in range(2):
        @pl.when(pos[2] == c)
        def _():
            mine[...] = dot(act_t[c * rows:(c + 1) * rows, :], rg)
            theirs[...] = dot(act_t[(1 - c) * rows:(2 - c) * rows, :], rg)


def down_terms(pos, act_t, own, others, after):
    rows = act_t.shape[0] // 2
    return pl.pallas_call(
        down_kernel,
        in_specs=[SMEM] + [VMEM] * 5 + [ANY],
        out_specs=[VMEM] * 2,
        out_shape=[jax.ShapeDtypeStruct((rows, 256), f32)] * 2,
        compiler_params=PARAMS,
        name="down_terms",
    )(pos, act_t, own, *others, after)


def pack_kernel(mine, theirs, up, out):
    for i in range(16):
        part = mine[i * 40:(i + 1) * 40, :] + theirs[i * 40:(i + 1) * 40, :]
        out[i, :, :] = jnp.concatenate([part, up[i * 8:(i + 1) * 8, :]], axis=0).astype(out.dtype)


def pack(mine, theirs, up):
    return pl.pallas_call(
        pack_kernel,
        in_specs=[VMEM] * 3,
        out_specs=VMEM,
        out_shape=jax.ShapeDtypeStruct((16, 48, 256), bf16),
        compiler_params=PARAMS,
        name="pack",
    )(mine, theirs, up)


def emit_kernel(pos, own, other, o_keep, o_other, att, down_q, up_q, down_v, up_v):
    zz = pl.program_id(0)
    halves = [own, other]
    for c in range(2):
        @pl.when(pos[2] == c)
        def _():
            for cc in range(2):
                src = halves[(c + cc) % 2]
                for i in range(16):
                    part = src[zz * 16 + i].astype(f32)
                    at = cc * 640 + i * 40
                    down_q[at:at + 40, :] = part[:40, :RANK]
                    down_v[at:at + 40, :] = part[:40, RANK:]

            @pl.when(zz == 0)
            def _():
                outs = [o_keep, o_other]
                for cc in range(2):
                    src = halves[(c + cc) % 2]
                    att[:, cc * HEAD:(cc + 1) * HEAD] = outs[(c + cc) % 2][...]
                    for i in range(16):
                        part = src[pos[3] * 16 + i].astype(f32)
                        up_q[i * 8:(i + 1) * 8, cc * HEAD:(cc + 1) * HEAD] = part[40:, :HEAD]
                        up_v[i * 8:(i + 1) * 8, cc * HEAD:(cc + 1) * HEAD] = part[40:, HEAD:]


def emit(pos, own, other, o_keep, o_other):
    whole = lambda a: pl.BlockSpec(a, lambda k: (0,) * len(a))
    return pl.pallas_call(
        emit_kernel,
        grid=(4,),
        in_specs=[SMEM] + [whole(a.shape) for a in (own, other, o_keep, o_other)],
        out_specs=[whole((256, 256)), pl.BlockSpec((1280, RANK), lambda k: (k, 0)), whole((RANK, 256)),
                   pl.BlockSpec((1280, RANK), lambda k: (k, 0)), whole((RANK, 256))],
        out_shape=[jax.ShapeDtypeStruct((256, 256), bf16), jax.ShapeDtypeStruct((5120, RANK), f32),
                   jax.ShapeDtypeStruct((RANK, 256), f32), jax.ShapeDtypeStruct((5120, RANK), f32),
                   jax.ShapeDtypeStruct((RANK, 256), f32)],
        compiler_params=PARAMS,
        name="emit",
    )(pos, own, other, o_keep, o_other)


def total_kernel(parts, after, out):
    total = parts[0].astype(f32)
    for i in range(1, 16):
        total += parts[i].astype(f32)
    low = total.astype(bf16)
    for i in range(64):
        out[i, :, :] = low


def total_for_all(parts, after):
    return pl.pallas_call(
        total_kernel,
        in_specs=[VMEM, ANY],
        out_specs=VMEM,
        out_shape=jax.ShapeDtypeStruct((64, 48, 256), bf16),
        compiler_params=PARAMS,
        name="total_for_all",
    )(parts, after)


def ring(n, d):
    return [(i, (i + d) % n) for i in range(n)]


def swap(a):
    return lax.ppermute(a, "c", ring(2, 1))


def spread(a, axis):
    one, three, two = [lax.ppermute(a, axis, ring(4, d)) for d in (1, 3, 2)]
    return [a, one, two, three]


def collect(parts, axis):
    return [parts[0]] + [lax.ppermute(parts[d], axis, ring(4, -d)) for d in (1, 2, 3)]


def half(a, index, size):
    return lax.dynamic_slice_in_dim(a, index * size, size, axis=1)


def local(act, wq, wk, wv, dq, uq, dv, uv, grad_out, levels, order, slot):
    x, y, c, z = (lax.axis_index(n).astype(jnp.int32) for n in ("x", "y", "c", "z"))
    pos = jnp.stack([x, y, c, z])
    g = lax.all_gather(grad_out, ("y", "c"), axis=0, tiled=True)
    keep, send, rq, rv = project(pos, act, wq, wk, wv, dq, dv, uq, uv)
    lists = visible_lists(pos, slot, levels, order)
    whole = jnp.concatenate([keep, swap(send)], axis=0)
    kvs = spread(whole[:, :2 * HEAD], "x")
    qs = spread(whole[:, 2 * HEAD:], "y")
    act_t = half(act, z, act.shape[1] // 4).T
    stats = spread(row_stats(pos, lists, qs, g, kvs), "y")
    o, *parts = attention_grads(pos, lists, stats, qs, g, kvs)
    a = collect(parts[:4], "y")
    b = collect(parts[4:], "x")
    o = lax.psum_scatter(o, "y", scatter_dimension=0, tiled=True).astype(bf16)
    o_keep, o_other = o[:256], swap(o[256:])
    rg_keep, rg_send, up = finish(pos, a, b, (rq, swap(rq), rv, swap(rv)), uq, uv)
    rg = rg_keep + swap(rg_send)
    mine, theirs = down_terms(pos, act_t, rg, spread(rg.astype(bf16), "z")[1:], o)
    terms = lax.all_to_all(pack(mine, swap(theirs), up), ("x", "y"), 0, 0, tiled=True)
    wide = lax.all_to_all(total_for_all(terms, o_other), ("z", "x", "y"), 0, 0, tiled=True)
    att, down_q, up_q, down_v, up_v = emit(pos, wide, swap(wide), o_keep, o_other)
    return att, down_q, up_q, down_v, up_v


def solution(mesh):
    torus = Mesh(mesh.devices.reshape(4, 4, 2, 4), ("x", "y", "c", "z"))
    tm = ("x", "y", "c")
    return jax.shard_map(
        local,
        mesh=torus,
        in_specs=(
            P(tm, None),
            P(None, "z"),
            P(None, "z"),
            P(None, "z"),
            P(),
            P(None, "z"),
            P(),
            P(None, "z"),
            P(tm, "z"),
            P(),
            P(),
            P(),
        ),
        out_specs=(P(tm, "z"), P(), P(None, "z"), P(), P(None, "z")),
        check_vma=False,
    )
```

```python
import math

import jax
import jax.numpy as jnp
from jax import lax
from jax.experimental import pallas as pl
from jax.experimental.pallas import tpu as pltpu
from jax.sharding import Mesh
from jax.sharding import PartitionSpec as P

HEAD = 128
FT = 128
BLK = 32
RANK = 128
CHUNK = 512
CB = CHUNK // BLK
CHAINS = 4
SCALE = HEAD ** -0.5
SCALE2 = SCALE * math.log2(math.e)
NEG = -1e30
f32 = jnp.float32
bf16 = jnp.bfloat16
WIRE = f32
KT = 1280
VMEM = pl.BlockSpec(memory_space=pltpu.VMEM)
SMEM = pl.BlockSpec(memory_space=pltpu.SMEM)
ANY = pl.BlockSpec(memory_space=pl.ANY)
WIDE = pltpu.CompilerParams(vmem_limit_bytes=60 * 1024 * 1024)
PARAMS = pltpu.CompilerParams(vmem_limit_bytes=48 * 1024 * 1024)


def dot(a, b, ca=1, cb=0):
    return lax.dot_general(a, b, (((ca,), (cb,)), ((), ())), preferred_element_type=f32)


def by_core(put, keep, send):
    for c in range(2):
        @pl.when(lax.axis_index("c") == c)
        def _():
            put(keep, c * HEAD)
            put(send, (1 - c) * HEAD)


def proj_kernel(act, wq, wk, wv, down_q, down_v, up_q, up_v, grad, keep, send, rank, aq, ak, av, rq, rv):
    step = pl.program_id(0)
    last = pl.num_programs(0) - 1
    a = act[...]
    parts = [(ak, wk), (av, wv), (rv, down_v), (aq, wq), (rq, down_q)]

    @pl.when(step == 0)
    def _():
        for total, w in parts:
            total[...] = dot(a, w[...])

    @pl.when(step > 0)
    def _():
        for total, w in parts:
            total[...] += dot(a, w[...])

    @pl.when(step == last)
    def _():
        low_q = rq[...].astype(bf16)
        low_v = rv[...].astype(bf16)
        rank[:, :RANK] = low_q
        rank[:, RANK:] = low_v
        keys = ak[...].astype(bf16)
        values = (av[...] + dot(low_v, up_v[...])).astype(bf16)
        query = (aq[...] + dot(low_q, up_q[...])).astype(bf16)

        def put(ref, at):
            ref[:, :HEAD] = keys[:, at:at + HEAD]
            ref[:, HEAD:2 * HEAD] = values[:, at:at + HEAD]
            ref[:, 2 * HEAD:3 * HEAD] = query[:, at:at + HEAD]
            ref[:, 3 * HEAD:] = grad[:, at:at + HEAD]

        by_core(put, keep, send)


def project(act, wq, wk, wv, down_q, down_v, up_q, up_v, grad):
    rows, width = act.shape
    cols = wq.shape[1]
    whole = lambda shape: pl.BlockSpec(shape, lambda k: (0, 0))
    shapes = [(rows, 4 * HEAD), (rows, 4 * HEAD), (rows, 2 * RANK)]
    return pl.pallas_call(
        proj_kernel,
        grid=(width // KT,),
        in_specs=[pl.BlockSpec((rows, KT), lambda k: (0, k))]
        + [pl.BlockSpec((KT, cols), lambda k: (k, 0))] * 3
        + [pl.BlockSpec((KT, RANK), lambda k: (k, 0))] * 2 + [whole(up_q.shape), whole(up_v.shape), whole(grad.shape)],
        out_specs=[whole(s) for s in shapes],
        out_shape=[jax.ShapeDtypeStruct(s, bf16) for s in shapes],
        scratch_shapes=[pltpu.VMEM((rows, cols), f32)] * 3 + [pltpu.VMEM((rows, RANK), f32)] * 2,
        compiler_params=WIDE,
        cost_estimate=pl.CostEstimate(flops=2 * rows * width * (3 * cols + 2 * RANK),
                                      bytes_accessed=2 * width * (rows + 3 * cols + 2 * RANK), transcendentals=0),
        name="project",
    )(act, wq, wk, wv, down_q, down_v, up_q, up_v, grad)


def assemble_kernel(keep, other, kv, qg):
    kv[:256, :] = keep[:, :256]
    kv[256:, :] = other[:, :256]
    qg[:256, :] = keep[:, 256:]
    qg[256:, :] = other[:, 256:]


def assemble(keep, other):
    return pl.pallas_call(
        assemble_kernel,
        in_specs=[VMEM] * 2,
        out_specs=[VMEM] * 2,
        out_shape=[jax.ShapeDtypeStruct((512, 256), bf16)] * 2,
        name="assemble",
    )(keep, other)


def lists_kernel(slot, packed, out):
    x, y, c = (lax.axis_index(n) for n in ("x", "y", "c"))

    def frame(xx, yy, local):
        core = c if local < 2 else 1 - c
        return slot[((xx * 4 + yy) * 2 + core) * 2 + local % 2]

    keys = [frame(lax.rem(x + 4 - k // 4, 4), y, k % 4) for k in range(16)]
    for q in range(16):
        out[17, q] = frame(x, lax.rem(y + 4 - q // 4, 4), q % 4)

    def one(q, _):
        f = out[17, q]
        n = 0
        for k in range(16):
            word = packed[f, keys[k]]
            for r in range(4):
                out[q, n + r] = k * 4 + ((word >> (2 * r)) & 3)
            n = n + (word >> 8)
        for r in range(CB):
            out[q, n + r] = 0
        out[16, q] = n
        return 0

    lax.fori_loop(0, 16, one, 0)


def visible_lists(slot, levels, order):
    packed = levels * 256 + jnp.sum(order * jnp.array([1, 4, 16, 64], jnp.int32), axis=-1)
    return pl.pallas_call(
        lists_kernel,
        in_specs=[SMEM] * 2,
        out_specs=SMEM,
        out_shape=jax.ShapeDtypeStruct((24, 128), jnp.int32),
        name="lists",
    )(slot, packed)


def fill_all(parts, whole):
    rows = parts[0].shape[0]
    for d, part in enumerate(parts):
        whole[d * rows:(d + 1) * rows, :] = part[...]


def load_chunk(lists, f, at, kvall):
    blocks = [kvall[pl.ds(pl.multiple_of(lists[f, at + i] * BLK, BLK), BLK), :] for i in range(CB)]
    return jnp.concatenate(blocks, axis=0)


def start_frames(lists, t, qgall, both):
    counts = []
    for j in range(CHAINS):
        f = t * CHAINS + j
        at = pl.multiple_of(f * FT, FT)
        both[j, :FT, :HEAD] = qgall[pl.ds(at, FT), :HEAD]
        both[j, FT:, HEAD:] = qgall[pl.ds(at, FT), HEAD:]
        counts.append(lists[16, f])
    chunks = [(n + CB - 1) // CB for n in counts]
    most = chunks[0]
    for n in chunks[1:]:
        most = jnp.maximum(most, n)
    return counts, chunks, most


def stats_kernel(lists, q0, q1, q2, q3, k0, k1, k2, k3, out, qgall, kvall, both):
    fill_all((q0, q1, q2, q3), qgall)
    fill_all((k0, k1, k2, k3), kvall)
    both[...] = jnp.zeros_like(both)
    row = lax.broadcasted_iota(jnp.int32, (CHUNK, HEAD), 0)

    def frames(t, _):
        counts, chunks, most = start_frames(lists, t, qgall, both)

        def chunk(ch, carry):
            kvs = [load_chunk(lists, t * CHAINS + j, jnp.minimum(ch, chunks[j] - 1) * CB, kvall)
                   for j in range(CHAINS)]
            rs = [dot(kvs[j], both[j], 1, 1) for j in range(CHAINS)]
            after = []
            for j in range(CHAINS):
                peak, total, delta = carry[j]
                s = jnp.where(row < (counts[j] - ch * CB) * BLK, rs[j][:, :FT] * SCALE2, NEG)
                new = jnp.maximum(peak, jnp.max(s, axis=0, keepdims=True))
                p = jnp.exp2(s - new)
                fix = jnp.exp2(peak - new)
                total = total * fix + jnp.sum(p, axis=0, keepdims=True)
                delta = delta * fix + jnp.sum(p * rs[j][:, FT:], axis=0, keepdims=True)
                after.append((new, total, delta))
            return tuple(after)

        zero = jnp.zeros((1, FT), f32)
        carry = lax.fori_loop(0, most, chunk, ((zero + NEG, zero, zero),) * CHAINS)
        for j in range(CHAINS):
            for i in range(3):
                out[pl.ds(16 * i + t * CHAINS + j, 1), :] = carry[j][i]
        return 0

    lax.fori_loop(0, 16 // CHAINS, frames, 0)


def row_stats(lists, qgs, kvs):
    return pl.pallas_call(
        stats_kernel,
        in_specs=[SMEM] + [VMEM] * 8,
        out_specs=VMEM,
        out_shape=jax.ShapeDtypeStruct((48, 128), f32),
        scratch_shapes=[pltpu.VMEM((2048, 2 * HEAD), bf16), pltpu.VMEM((2048, 2 * HEAD), bf16),
                        pltpu.VMEM((CHAINS, 2 * FT, 2 * HEAD), bf16)],
        compiler_params=PARAMS,
        name="row_stats",
    )(lists, *qgs, *kvs)


def grads_kernel(lists, s0, s1, s2, s3, q0, q1, q2, q3, k0, k1, k2, k3,
                 o0, o1, o2, o3, a0, a1, a2, a3, b0, b1, b2, b3, qgall, kvall, both, acc, dva, norm):
    fill_all((q0, q1, q2, q3), qgall)
    fill_all((k0, k1, k2, k3), kvall)
    both[...] = jnp.zeros_like(both)
    dva[...] = jnp.zeros_like(dva)
    for t in range(4):
        rows = [slice(4 * ((t - d) % 4), 4 * ((t - d) % 4) + 4) for d in range(4)]
        stats = [ref[...] for ref in (s0, s1, s2, s3)]
        peaks = [stats[d][0:16][rows[d]] for d in range(4)]
        peak = jnp.maximum(jnp.maximum(peaks[0], peaks[1]), jnp.maximum(peaks[2], peaks[3]))
        total = jnp.zeros_like(peak)
        delta = jnp.zeros_like(peak)
        for d in range(4):
            fix = jnp.exp2(peaks[d] - peak)
            total += fix * stats[d][16:32][rows[d]]
            delta += fix * stats[d][32:48][rows[d]]
        norm[4 * t:4 * t + 4, :] = peak + jnp.log2(total)
        norm[16 + 4 * t:20 + 4 * t, :] = delta / total
    row = lax.broadcasted_iota(jnp.int32, (CHUNK, HEAD), 0)

    def frames(t, _):
        counts, chunks, most = start_frames(lists, t, qgall, both)
        lse = [norm[pl.ds(t * CHAINS + j, 1), :] for j in range(CHAINS)]
        delta = [norm[pl.ds(16 + t * CHAINS + j, 1), :] for j in range(CHAINS)]
        acc[...] = jnp.zeros_like(acc)

        def chunk(ch, _):
            at = [jnp.minimum(ch, chunks[j] - 1) * CB for j in range(CHAINS)]
            kvs = [load_chunk(lists, t * CHAINS + j, at[j], kvall) for j in range(CHAINS)]
            rs = [dot(kvs[j], both[j], 1, 1) for j in range(CHAINS)]
            lows, pairs = [], []
            for j in range(CHAINS):
                s = jnp.where(row < (counts[j] - ch * CB) * BLK, rs[j][:, :FT] * SCALE2, NEG)
                p = jnp.exp2(s - lse[j])
                low = p.astype(bf16)
                ds = (p * (rs[j][:, FT:] - delta[j]) * SCALE).astype(bf16)
                lows.append(low)
                pairs.append(jnp.concatenate([low, ds], axis=1))
            for j in range(CHAINS):
                product = dot(kvs[j], pairs[j], 0, 0)
                acc[j, 0] += product[HEAD:, :FT]
                acc[j, 1] += product[:HEAD, FT:]
            dvs = [dot(lows[j], both[j, FT:, HEAD:]) for j in range(CHAINS)]
            for i in range(CB):
                for j in range(CHAINS):
                    to = pl.multiple_of(lists[t * CHAINS + j, at[j] + i] * BLK, BLK)
                    dva[j, pl.ds(to, BLK), :] += dvs[j][i * BLK:(i + 1) * BLK, :]
            return 0

        lax.fori_loop(0, most, chunk, 0)
        for j in range(CHAINS):
            f = t * CHAINS + j
            at = pl.multiple_of(lax.rem(f, 4) * FT, FT)
            for d, (o, a) in enumerate(zip((o0, o1, o2, o3), (a0, a1, a2, a3))):
                @pl.when(f // 4 == d)
                def _():
                    o[pl.ds(at, FT), :] = acc[j, 0].T.astype(o.dtype)
                    a[pl.ds(at, FT), :] = acc[j, 1].T.astype(a.dtype)

        return 0

    lax.fori_loop(0, 16 // CHAINS, frames, 0)
    for d, b in enumerate((b0, b1, b2, b3)):
        total = dva[0, d * 512:(d + 1) * 512, :]
        for j in range(1, CHAINS):
            total += dva[j, d * 512:(d + 1) * 512, :]
        b[...] = total.astype(b.dtype)


def attention_grads(lists, stats, qgs, kvs):
    wire = [f32, bf16, bf16, bf16] + [WIRE] * 8
    return pl.pallas_call(
        grads_kernel,
        in_specs=[SMEM] + [VMEM] * 12,
        out_specs=[VMEM] * 12,
        out_shape=[jax.ShapeDtypeStruct((512, HEAD), t) for t in wire],
        scratch_shapes=[pltpu.VMEM((2048, 2 * HEAD), bf16), pltpu.VMEM((2048, 2 * HEAD), bf16),
                        pltpu.VMEM((CHAINS, 2 * FT, 2 * HEAD), bf16),
                        pltpu.VMEM((CHAINS, 2, HEAD, FT), f32), pltpu.VMEM((CHAINS, 2048, HEAD), f32),
                        pltpu.VMEM((32, 128), f32)],
        compiler_params=PARAMS,
        name="attention_grads",
    )(lists, *stats, *qgs, *kvs)


def finish_kernel(a0, a1, a2, a3, b0, b1, b2, b3, own, other, uq, uv, after,
                  rg_keep, rg_send, up):
    dq = (a0[...] + a1[...].astype(f32) + a2[...].astype(f32) + a3[...].astype(f32)).astype(bf16)
    dv = (b0[...] + b1[...].astype(f32) + b2[...].astype(f32) + b3[...].astype(f32)).astype(bf16)
    for c in range(2):
        @pl.when(lax.axis_index("c") == c)
        def _():
            gq = dot(dq, uq[:, c * HEAD:(c + 1) * HEAD], 1, 1)
            gv = dot(dv, uv[:, c * HEAD:(c + 1) * HEAD], 1, 1)
            rg_keep[:, :RANK] = gq[:256]
            rg_keep[:, RANK:] = gv[:256]
            rg_send[:, :RANK] = gq[256:]
            rg_send[:, RANK:] = gv[256:]
    up[:, :HEAD] = dot(own[:, :RANK], dq[:256], 0, 0) + dot(other[:, :RANK], dq[256:], 0, 0)
    up[:, HEAD:] = dot(own[:, RANK:], dv[:256], 0, 0) + dot(other[:, RANK:], dv[256:], 0, 0)


def finish(a, b, own, other, uq, uv, after):
    return pl.pallas_call(
        finish_kernel,
        in_specs=[VMEM] * 12 + [ANY],
        out_specs=[VMEM] * 3,
        out_shape=[jax.ShapeDtypeStruct((r, 256), f32) for r in (256, 256, 128)],
        compiler_params=PARAMS,
        name="finish",
    )(*a, *b, own, other, uq, uv, after)


def down_kernel(act_t, own, r1, r2, r3, after, mine, theirs):
    rg = (own[...] + r1[...].astype(f32) + r2[...].astype(f32) + r3[...].astype(f32)).astype(bf16)
    rows = mine.shape[0]
    for c in range(2):
        @pl.when(lax.axis_index("c") == c)
        def _():
            mine[...] = dot(act_t[c * rows:(c + 1) * rows, :], rg)
            theirs[...] = dot(act_t[(1 - c) * rows:(2 - c) * rows, :], rg)


def down_terms(act_t, own, others, after):
    rows = act_t.shape[0] // 2
    return pl.pallas_call(
        down_kernel,
        in_specs=[VMEM] * 5 + [ANY],
        out_specs=[VMEM] * 2,
        out_shape=[jax.ShapeDtypeStruct((rows, 256), f32)] * 2,
        compiler_params=PARAMS,
        name="down_terms",
    )(act_t, own, *others, after)


def pack_kernel(mine, theirs, up, out):
    for i in range(16):
        part = mine[i * 40:(i + 1) * 40, :] + theirs[i * 40:(i + 1) * 40, :]
        out[i, :, :] = jnp.concatenate([part, up[i * 8:(i + 1) * 8, :]], axis=0).astype(out.dtype)


def pack(mine, theirs, up):
    return pl.pallas_call(
        pack_kernel,
        in_specs=[VMEM] * 3,
        out_specs=VMEM,
        out_shape=jax.ShapeDtypeStruct((16, 48, 256), bf16),
        compiler_params=PARAMS,
        name="pack",
    )(mine, theirs, up)


def emit_kernel(own, other, o_keep, o_other, att, down_q, up_q, down_v, up_v):
    zz = pl.program_id(0)
    halves = [own, other]
    for c in range(2):
        @pl.when(lax.axis_index("c") == c)
        def _():
            for cc in range(2):
                src = halves[(c + cc) % 2]
                for i in range(16):
                    part = src[zz * 16 + i].astype(f32)
                    at = cc * 640 + i * 40
                    down_q[at:at + 40, :] = part[:40, :RANK]
                    down_v[at:at + 40, :] = part[:40, RANK:]

            @pl.when(zz == 0)
            def _():
                outs = [o_keep, o_other]
                for cc in range(2):
                    src = halves[(c + cc) % 2]
                    att[:, cc * HEAD:(cc + 1) * HEAD] = outs[(c + cc) % 2][...]
                    for i in range(16):
                        part = src[lax.axis_index("z") * 16 + i].astype(f32)
                        up_q[i * 8:(i + 1) * 8, cc * HEAD:(cc + 1) * HEAD] = part[40:, :HEAD]
                        up_v[i * 8:(i + 1) * 8, cc * HEAD:(cc + 1) * HEAD] = part[40:, HEAD:]


def emit(own, other, o_keep, o_other):
    whole = lambda a: pl.BlockSpec(a, lambda k: (0,) * len(a))
    return pl.pallas_call(
        emit_kernel,
        grid=(4,),
        in_specs=[whole(a.shape) for a in (own, other, o_keep, o_other)],
        out_specs=[whole((256, 256)), pl.BlockSpec((1280, RANK), lambda k: (k, 0)), whole((RANK, 256)),
                   pl.BlockSpec((1280, RANK), lambda k: (k, 0)), whole((RANK, 256))],
        out_shape=[jax.ShapeDtypeStruct((256, 256), bf16), jax.ShapeDtypeStruct((5120, RANK), f32),
                   jax.ShapeDtypeStruct((RANK, 256), f32), jax.ShapeDtypeStruct((5120, RANK), f32),
                   jax.ShapeDtypeStruct((RANK, 256), f32)],
        compiler_params=PARAMS,
        name="emit",
    )(own, other, o_keep, o_other)


def total_kernel(parts, after, out):
    total = parts[0].astype(f32)
    for i in range(1, 16):
        total += parts[i].astype(f32)
    low = total.astype(bf16)
    for i in range(64):
        out[i, :, :] = low


def total_for_all(parts, after):
    return pl.pallas_call(
        total_kernel,
        in_specs=[VMEM, ANY],
        out_specs=VMEM,
        out_shape=jax.ShapeDtypeStruct((64, 48, 256), bf16),
        compiler_params=PARAMS,
        name="total_for_all",
    )(parts, after)


def ring(n, d):
    return [(i, (i + d) % n) for i in range(n)]


def swap(a):
    return lax.ppermute(a, "c", ring(2, 1))


def spread(a, axis):
    one, three, two = [lax.ppermute(a, axis, ring(4, d)) for d in (1, 3, 2)]
    return [a, one, two, three]


def collect(parts, axis):
    return [parts[0]] + [lax.ppermute(parts[d], axis, ring(4, -d)) for d in (1, 2, 3)]


def half(a, index, size):
    return lax.dynamic_slice_in_dim(a, index * size, size, axis=1)


def local(act, wq, wk, wv, dq, uq, dv, uv, grad_out, levels, order, slot):
    z = lax.axis_index("z")
    keep, send, rank = project(act, wq, wk, wv, dq, dv, uq, uv, grad_out)
    kv, qg = assemble(keep, swap(send))
    kvs = spread(kv, "x")
    qgs = spread(qg, "y")
    lists = visible_lists(slot, levels, order)
    act_t = half(act, z, act.shape[1] // 4).T
    stats = spread(row_stats(lists, qgs, kvs), "y")
    parts = attention_grads(lists, stats, qgs, kvs)
    a = collect(parts[4:8], "y")
    b = collect(parts[8:], "x")
    o0, o1, o2, o3 = collect(parts[:4], "y")
    o = (o0 + o1.astype(f32) + o2.astype(f32) + o3.astype(f32)).astype(bf16)
    o_keep, o_other = o[:256], swap(o[256:])
    rg_keep, rg_send, up = finish(a, b, rank, swap(rank), uq, uv, act_t)
    rg = rg_keep + swap(rg_send)
    mine, theirs = down_terms(act_t, rg, spread(rg.astype(bf16), "z")[1:], o)
    terms = lax.all_to_all(pack(mine, swap(theirs), up), ("x", "y"), 0, 0, tiled=True)
    wide = lax.all_to_all(total_for_all(terms, o_other), ("z", "x", "y"), 0, 0, tiled=True)
    att, down_q, up_q, down_v, up_v = emit(wide, swap(wide), o_keep, o_other)
    return att, down_q, up_q, down_v, up_v


def solution(mesh):
    torus = Mesh(mesh.devices.reshape(4, 4, 2, 4), ("x", "y", "c", "z"))
    tm = ("x", "y", "c")
    return jax.shard_map(
        local,
        mesh=torus,
        in_specs=(
            P(tm, None),
            P(None, "z"),
            P(None, "z"),
            P(None, "z"),
            P(),
            P(None, "z"),
            P(),
            P(None, "z"),
            P(tm, "z"),
            P(),
            P(),
            P(),
        ),
        out_specs=(P(tm, "z"), P(), P(None, "z"), P(), P(None, "z")),
        check_vma=False,
    )
```

```python
import math

import jax
import jax.numpy as jnp
from jax import lax
from jax.experimental import pallas as pl
from jax.experimental.pallas import tpu as pltpu
from jax.sharding import Mesh
from jax.sharding import PartitionSpec as P

HEAD = 128
FT = 128
BLK = 32
RANK = 128
CHUNK = 512
CB = CHUNK // BLK
CHAINS = 4
SCALE = HEAD ** -0.5
SCALE2 = SCALE * math.log2(math.e)
NEG = -1e30
f32 = jnp.float32
bf16 = jnp.bfloat16
WIRE = f32
KT = 1280
VMEM = pl.BlockSpec(memory_space=pltpu.VMEM)
SMEM = pl.BlockSpec(memory_space=pltpu.SMEM)
ANY = pl.BlockSpec(memory_space=pl.ANY)
WIDE = pltpu.CompilerParams(vmem_limit_bytes=60 * 1024 * 1024)
PARAMS = pltpu.CompilerParams(vmem_limit_bytes=20 * 1024 * 1024)


def dot(a, b, ca=1, cb=0):
    return lax.dot_general(a, b, (((ca,), (cb,)), ((), ())), preferred_element_type=f32)


def by_core(put, keep, send):
    for c in range(2):
        @pl.when(lax.axis_index("c") == c)
        def _():
            put(keep, c * HEAD)
            put(send, (1 - c) * HEAD)


def proj_kernel(act, wq, wk, wv, down_q, down_v, up_q, up_v, grad, keep, send, rank, aq, ak, av, rq, rv):
    step = pl.program_id(0)
    last = pl.num_programs(0) - 1
    a = act[...]
    parts = [(ak, wk), (av, wv), (rv, down_v), (aq, wq), (rq, down_q)]

    @pl.when(step == 0)
    def _():
        for total, w in parts:
            total[...] = dot(a, w[...])

    @pl.when(step > 0)
    def _():
        for total, w in parts:
            total[...] += dot(a, w[...])

    @pl.when(step == last)
    def _():
        low_q = rq[...].astype(bf16)
        low_v = rv[...].astype(bf16)
        rank[:, :RANK] = low_q
        rank[:, RANK:] = low_v
        keys = ak[...].astype(bf16)
        values = (av[...] + dot(low_v, up_v[...])).astype(bf16)
        query = (aq[...] + dot(low_q, up_q[...])).astype(bf16)

        def put(ref, at):
            ref[:, :HEAD] = keys[:, at:at + HEAD]
            ref[:, HEAD:2 * HEAD] = values[:, at:at + HEAD]
            ref[:, 2 * HEAD:3 * HEAD] = query[:, at:at + HEAD]
            ref[:, 3 * HEAD:] = grad[:, at:at + HEAD]

        by_core(put, keep, send)


def project(act, wq, wk, wv, down_q, down_v, up_q, up_v, grad):
    rows, width = act.shape
    cols = wq.shape[1]
    whole = lambda shape: pl.BlockSpec(shape, lambda k: (0, 0))
    shapes = [(rows, 4 * HEAD), (rows, 4 * HEAD), (rows, 2 * RANK)]
    return pl.pallas_call(
        proj_kernel,
        grid=(width // KT,),
        in_specs=[pl.BlockSpec((rows, KT), lambda k: (0, k))]
        + [pl.BlockSpec((KT, cols), lambda k: (k, 0))] * 3
        + [pl.BlockSpec((KT, RANK), lambda k: (k, 0))] * 2 + [whole(up_q.shape), whole(up_v.shape), whole(grad.shape)],
        out_specs=[whole(s) for s in shapes],
        out_shape=[jax.ShapeDtypeStruct(s, bf16) for s in shapes],
        scratch_shapes=[pltpu.VMEM((rows, cols), f32)] * 3 + [pltpu.VMEM((rows, RANK), f32)] * 2,
        compiler_params=WIDE,
        cost_estimate=pl.CostEstimate(flops=2 * rows * width * (3 * cols + 2 * RANK),
                                      bytes_accessed=2 * width * (rows + 3 * cols + 2 * RANK), transcendentals=0),
        name="project",
    )(act, wq, wk, wv, down_q, down_v, up_q, up_v, grad)


def assemble_kernel(keep, other, kv, qg):
    kv[:256, :] = keep[:, :256]
    kv[256:, :] = other[:, :256]
    qg[:256, :] = keep[:, 256:]
    qg[256:, :] = other[:, 256:]


def assemble(keep, other):
    return pl.pallas_call(
        assemble_kernel,
        in_specs=[VMEM] * 2,
        out_specs=[VMEM] * 2,
        out_shape=[jax.ShapeDtypeStruct((512, 256), bf16)] * 2,
        compiler_params=PARAMS,
        name="assemble",
    )(keep, other)


def lists_kernel(slot, packed, out):
    x, y, c = (lax.axis_index(n) for n in ("x", "y", "c"))

    def frame(xx, yy, local):
        core = c if local < 2 else 1 - c
        return slot[((xx * 4 + yy) * 2 + core) * 2 + local % 2]

    keys = [frame(lax.rem(x + 4 - k // 4, 4), y, k % 4) for k in range(16)]
    for q in range(16):
        out[17, q] = frame(x, lax.rem(y + 4 - q // 4, 4), q % 4)

    def one(q, _):
        f = out[17, q]
        words = [packed[f, keys[k]] for k in range(16)]
        n = 0
        for k, word in enumerate(words):
            for r in range(4):
                out[q, n + r] = k * 4 + ((word >> (2 * r)) & 3)
            n = n + (word >> 8)
        for r in range(CB):
            out[q, n + r] = 0
        out[16, q] = n
        return 0

    lax.fori_loop(0, 16, one, 0)


def visible_lists(slot, levels, order):
    packed = levels * 256 + jnp.sum(order * jnp.array([1, 4, 16, 64], jnp.int32), axis=-1)
    return pl.pallas_call(
        lists_kernel,
        in_specs=[SMEM] * 2,
        out_specs=SMEM,
        out_shape=jax.ShapeDtypeStruct((24, 128), jnp.int32),
        compiler_params=PARAMS,
        name="lists",
    )(slot, packed)


def fill_all(parts, whole):
    rows = parts[0].shape[0]
    for d, part in enumerate(parts):
        whole[d * rows:(d + 1) * rows, :] = part[...]


def load_chunk(lists, f, at, kvall):
    blocks = [kvall[pl.ds(pl.multiple_of(lists[f, at + i] * BLK, BLK), BLK), :] for i in range(CB)]
    return jnp.concatenate(blocks, axis=0)


def start_frames(lists, t, qgall, both):
    counts = []
    for j in range(CHAINS):
        f = t * CHAINS + j
        at = pl.multiple_of(f * FT, FT)
        both[j, :FT, :HEAD] = qgall[pl.ds(at, FT), :HEAD]
        both[j, FT:, HEAD:] = qgall[pl.ds(at, FT), HEAD:]
        counts.append(lists[16, f])
    chunks = [(n + CB - 1) // CB for n in counts]
    most = chunks[0]
    for n in chunks[1:]:
        most = jnp.maximum(most, n)
    return counts, chunks, most


def stats_kernel(lists, q0, q1, q2, q3, k0, k1, k2, k3, out, qgall, kvall, both):
    fill_all((q0, q1, q2, q3), qgall)
    fill_all((k0, k1, k2, k3), kvall)
    both[...] = jnp.zeros_like(both)
    row = lax.broadcasted_iota(jnp.int32, (CHUNK, HEAD), 0)

    def frames(t, _):
        counts, chunks, most = start_frames(lists, t, qgall, both)

        def chunk(ch, carry):
            kvs = [load_chunk(lists, t * CHAINS + j, jnp.minimum(ch, chunks[j] - 1) * CB, kvall)
                   for j in range(CHAINS)]
            rs = [dot(kvs[j], both[j], 1, 1) for j in range(CHAINS)]
            after = []
            for j in range(CHAINS):
                peak, total, delta = carry[j]
                s = jnp.where(row < (counts[j] - ch * CB) * BLK, rs[j][:, :FT] * SCALE2, NEG)
                new = jnp.maximum(peak, jnp.max(s, axis=0, keepdims=True))
                p = jnp.exp2(s - new)
                fix = jnp.exp2(peak - new)
                total = total * fix + jnp.sum(p, axis=0, keepdims=True)
                delta = delta * fix + jnp.sum(p * rs[j][:, FT:], axis=0, keepdims=True)
                after.append((new, total, delta))
            return tuple(after)

        zero = jnp.zeros((1, FT), f32)
        carry = lax.fori_loop(0, most, chunk, ((zero + NEG, zero, zero),) * CHAINS)
        for j in range(CHAINS):
            for i in range(3):
                out[pl.ds(16 * i + t * CHAINS + j, 1), :] = carry[j][i]
        return 0

    lax.fori_loop(0, 16 // CHAINS, frames, 0)


def row_stats(lists, qgs, kvs):
    return pl.pallas_call(
        stats_kernel,
        in_specs=[SMEM] + [VMEM] * 8,
        out_specs=VMEM,
        out_shape=jax.ShapeDtypeStruct((48, 128), f32),
        scratch_shapes=[pltpu.VMEM((2048, 2 * HEAD), bf16), pltpu.VMEM((2048, 2 * HEAD), bf16),
                        pltpu.VMEM((CHAINS, 2 * FT, 2 * HEAD), bf16)],
        compiler_params=PARAMS,
        name="row_stats",
    )(lists, *qgs, *kvs)


def grads_kernel(lists, s0, s1, s2, s3, q0, q1, q2, q3, k0, k1, k2, k3,
                 o0, o1, o2, o3, a0, a1, a2, a3, b0, b1, b2, b3, qgall, kvall, both, acc, dva, norm):
    fill_all((q0, q1, q2, q3), qgall)
    fill_all((k0, k1, k2, k3), kvall)
    both[...] = jnp.zeros_like(both)
    dva[...] = jnp.zeros_like(dva)
    for t in range(4):
        rows = [slice(4 * ((t - d) % 4), 4 * ((t - d) % 4) + 4) for d in range(4)]
        stats = [ref[...] for ref in (s0, s1, s2, s3)]
        peaks = [stats[d][0:16][rows[d]] for d in range(4)]
        peak = jnp.maximum(jnp.maximum(peaks[0], peaks[1]), jnp.maximum(peaks[2], peaks[3]))
        total = jnp.zeros_like(peak)
        delta = jnp.zeros_like(peak)
        for d in range(4):
            fix = jnp.exp2(peaks[d] - peak)
            total += fix * stats[d][16:32][rows[d]]
            delta += fix * stats[d][32:48][rows[d]]
        norm[4 * t:4 * t + 4, :] = peak + jnp.log2(total)
        norm[16 + 4 * t:20 + 4 * t, :] = delta / total
    row = lax.broadcasted_iota(jnp.int32, (CHUNK, HEAD), 0)

    def frames(t, _):
        counts, chunks, most = start_frames(lists, t, qgall, both)
        lse = [norm[pl.ds(t * CHAINS + j, 1), :] for j in range(CHAINS)]
        delta = [norm[pl.ds(16 + t * CHAINS + j, 1), :] for j in range(CHAINS)]
        acc[...] = jnp.zeros_like(acc)

        def chunk(ch, _):
            at = [jnp.minimum(ch, chunks[j] - 1) * CB for j in range(CHAINS)]
            kvs = [load_chunk(lists, t * CHAINS + j, at[j], kvall) for j in range(CHAINS)]
            rs = [dot(kvs[j], both[j], 1, 1) for j in range(CHAINS)]
            lows, pairs = [], []
            for j in range(CHAINS):
                s = jnp.where(row < (counts[j] - ch * CB) * BLK, rs[j][:, :FT] * SCALE2, NEG)
                p = jnp.exp2(s - lse[j])
                low = p.astype(bf16)
                ds = (p * (rs[j][:, FT:] - delta[j]) * SCALE).astype(bf16)
                lows.append(low)
                pairs.append(jnp.concatenate([low, ds], axis=1))
            for j in range(CHAINS):
                product = dot(kvs[j], pairs[j], 0, 0)
                acc[j, 0] += product[HEAD:, :FT]
                acc[j, 1] += product[:HEAD, FT:]
            dvs = [dot(lows[j], both[j, FT:, HEAD:]) for j in range(CHAINS)]
            for i in range(CB):
                for j in range(CHAINS):
                    to = pl.multiple_of(lists[t * CHAINS + j, at[j] + i] * BLK, BLK)
                    dva[j, pl.ds(to, BLK), :] += dvs[j][i * BLK:(i + 1) * BLK, :]
            return 0

        lax.fori_loop(0, most, chunk, 0)
        for j in range(CHAINS):
            f = t * CHAINS + j
            at = pl.multiple_of(lax.rem(f, 4) * FT, FT)
            for d, (o, a) in enumerate(zip((o0, o1, o2, o3), (a0, a1, a2, a3))):
                @pl.when(f // 4 == d)
                def _():
                    o[pl.ds(at, FT), :] = acc[j, 0].T.astype(o.dtype)
                    a[pl.ds(at, FT), :] = acc[j, 1].T.astype(a.dtype)

        return 0

    lax.fori_loop(0, 16 // CHAINS, frames, 0)
    for d, b in enumerate((b0, b1, b2, b3)):
        total = dva[0, d * 512:(d + 1) * 512, :]
        for j in range(1, CHAINS):
            total += dva[j, d * 512:(d + 1) * 512, :]
        b[...] = total.astype(b.dtype)


def attention_grads(lists, stats, qgs, kvs):
    wire = [f32, bf16, bf16, bf16] + [WIRE] * 8
    return pl.pallas_call(
        grads_kernel,
        in_specs=[SMEM] + [VMEM] * 12,
        out_specs=[VMEM] * 12,
        out_shape=[jax.ShapeDtypeStruct((512, HEAD), t) for t in wire],
        scratch_shapes=[pltpu.VMEM((2048, 2 * HEAD), bf16), pltpu.VMEM((2048, 2 * HEAD), bf16),
                        pltpu.VMEM((CHAINS, 2 * FT, 2 * HEAD), bf16),
                        pltpu.VMEM((CHAINS, 2, HEAD, FT), f32), pltpu.VMEM((CHAINS, 2048, HEAD), f32),
                        pltpu.VMEM((32, 128), f32)],
        compiler_params=PARAMS,
        name="attention_grads",
    )(lists, *stats, *qgs, *kvs)


def finish_kernel(a0, a1, a2, a3, b0, b1, b2, b3, own, other, uq, uv, after,
                  rg_keep, rg_send, up):
    dq = (a0[...] + a1[...].astype(f32) + a2[...].astype(f32) + a3[...].astype(f32)).astype(bf16)
    dv = (b0[...] + b1[...].astype(f32) + b2[...].astype(f32) + b3[...].astype(f32)).astype(bf16)
    for c in range(2):
        @pl.when(lax.axis_index("c") == c)
        def _():
            gq = dot(dq, uq[:, c * HEAD:(c + 1) * HEAD], 1, 1)
            gv = dot(dv, uv[:, c * HEAD:(c + 1) * HEAD], 1, 1)
            rg_keep[:, :RANK] = gq[:256]
            rg_keep[:, RANK:] = gv[:256]
            rg_send[:, :RANK] = gq[256:]
            rg_send[:, RANK:] = gv[256:]
    up[:, :HEAD] = dot(own[:, :RANK], dq[:256], 0, 0) + dot(other[:, :RANK], dq[256:], 0, 0)
    up[:, HEAD:] = dot(own[:, RANK:], dv[:256], 0, 0) + dot(other[:, RANK:], dv[256:], 0, 0)


def finish(a, b, own, other, uq, uv, after):
    return pl.pallas_call(
        finish_kernel,
        in_specs=[VMEM] * 12 + [ANY],
        out_specs=[VMEM] * 3,
        out_shape=[jax.ShapeDtypeStruct((r, 256), f32) for r in (256, 256, 128)],
        compiler_params=PARAMS,
        name="finish",
    )(*a, *b, own, other, uq, uv, after)


def down_kernel(act_t, own, r1, r2, r3, after, mine, theirs):
    rg = (own[...] + r1[...].astype(f32) + r2[...].astype(f32) + r3[...].astype(f32)).astype(bf16)
    rows = mine.shape[0]
    for c in range(2):
        @pl.when(lax.axis_index("c") == c)
        def _():
            mine[...] = dot(act_t[c * rows:(c + 1) * rows, :], rg)
            theirs[...] = dot(act_t[(1 - c) * rows:(2 - c) * rows, :], rg)


def down_terms(act_t, own, others, after):
    rows = act_t.shape[0] // 2
    return pl.pallas_call(
        down_kernel,
        in_specs=[VMEM] * 5 + [ANY],
        out_specs=[VMEM] * 2,
        out_shape=[jax.ShapeDtypeStruct((rows, 256), f32)] * 2,
        compiler_params=PARAMS,
        name="down_terms",
    )(act_t, own, *others, after)


def pack_kernel(mine, theirs, up, out):
    for i in range(16):
        part = mine[i * 40:(i + 1) * 40, :] + theirs[i * 40:(i + 1) * 40, :]
        out[i, :, :] = jnp.concatenate([part, up[i * 8:(i + 1) * 8, :]], axis=0).astype(out.dtype)


def pack(mine, theirs, up):
    return pl.pallas_call(
        pack_kernel,
        in_specs=[VMEM] * 3,
        out_specs=VMEM,
        out_shape=jax.ShapeDtypeStruct((16, 48, 256), bf16),
        compiler_params=PARAMS,
        name="pack",
    )(mine, theirs, up)


def emit_kernel(own, other, o_keep, o_other, att, down_q, up_q, down_v, up_v):
    zz = pl.program_id(0)
    halves = [own, other]
    for c in range(2):
        @pl.when(lax.axis_index("c") == c)
        def _():
            for cc in range(2):
                src = halves[(c + cc) % 2]
                for i in range(16):
                    part = src[i, pl.ds(pl.multiple_of(zz * 48, 16), 48), :].astype(f32)
                    at = cc * 640 + i * 40
                    down_q[at:at + 40, :] = part[:40, :RANK]
                    down_v[at:at + 40, :] = part[:40, RANK:]

            @pl.when(zz == 0)
            def _():
                outs = [o_keep, o_other]
                for cc in range(2):
                    src = halves[(c + cc) % 2]
                    att[:, cc * HEAD:(cc + 1) * HEAD] = outs[(c + cc) % 2][...]
                    for i in range(16):
                        part = src[i, pl.ds(pl.multiple_of(lax.axis_index("z") * 48, 16), 48), :].astype(f32)
                        up_q[i * 8:(i + 1) * 8, cc * HEAD:(cc + 1) * HEAD] = part[40:, :HEAD]
                        up_v[i * 8:(i + 1) * 8, cc * HEAD:(cc + 1) * HEAD] = part[40:, HEAD:]


def emit(own, other, o_keep, o_other):
    whole = lambda a: pl.BlockSpec(a, lambda k: (0,) * len(a))
    return pl.pallas_call(
        emit_kernel,
        grid=(4,),
        in_specs=[whole(a.shape) for a in (own, other, o_keep, o_other)],
        out_specs=[whole((256, 256)), pl.BlockSpec((1280, RANK), lambda k: (k, 0)), whole((RANK, 256)),
                   pl.BlockSpec((1280, RANK), lambda k: (k, 0)), whole((RANK, 256))],
        out_shape=[jax.ShapeDtypeStruct((256, 256), bf16), jax.ShapeDtypeStruct((5120, RANK), f32),
                   jax.ShapeDtypeStruct((RANK, 256), f32), jax.ShapeDtypeStruct((5120, RANK), f32),
                   jax.ShapeDtypeStruct((RANK, 256), f32)],
        compiler_params=PARAMS,
        name="emit",
    )(own, other, o_keep, o_other)


def total_kernel(parts, after, out):
    total = parts[0].astype(f32)
    for i in range(1, 16):
        total += parts[i].astype(f32)
    out[...] = total.astype(bf16)


def add_up(parts, after):
    return pl.pallas_call(
        total_kernel,
        in_specs=[VMEM, ANY],
        out_specs=VMEM,
        out_shape=jax.ShapeDtypeStruct((48, 256), bf16),
        compiler_params=PARAMS,
        name="add_up",
    )(parts, after)


def copies_kernel(p0, p1, p2, p3, out):
    for d, part in enumerate((p0, p1, p2, p3)):
        at = pl.multiple_of(lax.rem(lax.axis_index("z") + 4 - d, 4) * 48, 16)
        for i in range(16):
            out[i, pl.ds(at, 48), :] = part[...]


def copies(parts):
    return pl.pallas_call(
        copies_kernel,
        in_specs=[VMEM] * 4,
        out_specs=VMEM,
        out_shape=jax.ShapeDtypeStruct((16, 192, 256), bf16),
        compiler_params=PARAMS,
        name="copies",
    )(*parts)


def ring(n, d):
    return [(i, (i + d) % n) for i in range(n)]


def swap(a):
    return lax.ppermute(a, "c", ring(2, 1))


def spread(a, axis):
    one, three, two = [lax.ppermute(a, axis, ring(4, d)) for d in (1, 3, 2)]
    return [a, one, two, three]


def collect(parts, axis):
    return [parts[0]] + [lax.ppermute(parts[d], axis, ring(4, -d)) for d in (1, 2, 3)]


def half(a, index, size):
    return lax.dynamic_slice_in_dim(a, index * size, size, axis=1)


def local(act, wq, wk, wv, dq, uq, dv, uv, grad_out, levels, order, slot):
    z = lax.axis_index("z")
    keep, send, rank = project(act, wq, wk, wv, dq, dv, uq, uv, grad_out)
    kv, qg = assemble(keep, swap(send))
    kvs = spread(kv, "x")
    qgs = spread(qg, "y")
    lists = visible_lists(slot, levels, order)
    act_t = half(act, z, act.shape[1] // 4).T
    stats = spread(row_stats(lists, qgs, kvs), "y")
    parts = attention_grads(lists, stats, qgs, kvs)
    a = collect(parts[4:8], "y")
    b = collect(parts[8:], "x")
    o0, o1, o2, o3 = collect(parts[:4], "y")
    o = (o0 + o1.astype(f32) + o2.astype(f32) + o3.astype(f32)).astype(bf16)
    o_keep, o_other = o[:256], swap(o[256:])
    rg_keep, rg_send, up = finish(a, b, rank, swap(rank), uq, uv, act_t)
    rg = rg_keep + swap(rg_send)
    mine, theirs = down_terms(act_t, rg, spread(rg.astype(bf16), "z")[1:], o)
    terms = lax.all_to_all(pack(mine, swap(theirs), up), ("x", "y"), 0, 0, tiled=True)
    wide = copies(spread(add_up(terms, o_other), "z"))
    wide = lax.all_to_all(wide, ("x", "y"), 0, 0, tiled=True)
    att, down_q, up_q, down_v, up_v = emit(wide, swap(wide), o_keep, o_other)
    return att, down_q, up_q, down_v, up_v


def solution(mesh):
    torus = Mesh(mesh.devices.reshape(4, 4, 2, 4), ("x", "y", "c", "z"))
    tm = ("x", "y", "c")
    return jax.shard_map(
        local,
        mesh=torus,
        in_specs=(
            P(tm, None),
            P(None, "z"),
            P(None, "z"),
            P(None, "z"),
            P(),
            P(None, "z"),
            P(),
            P(None, "z"),
            P(tm, "z"),
            P(),
            P(),
            P(),
        ),
        out_specs=(P(tm, "z"), P(), P(None, "z"), P(), P(None, "z")),
        check_vma=False,
    )
```

```python
import math

import jax
import jax.numpy as jnp
from jax import lax
from jax.experimental import pallas as pl
from jax.experimental.pallas import tpu as pltpu
from jax.sharding import Mesh
from jax.sharding import PartitionSpec as P

HEAD = 128
FT = 128
BLK = 32
RANK = 128
CHUNK = 512
CB = CHUNK // BLK
CHAINS = 4
SCALE = HEAD ** -0.5
SCALE2 = SCALE * math.log2(math.e)
NEG = -1e30
f32 = jnp.float32
bf16 = jnp.bfloat16
WIRE = f32
WIRE2 = bf16
KT = 1280
VMEM = pl.BlockSpec(memory_space=pltpu.VMEM)
SMEM = pl.BlockSpec(memory_space=pltpu.SMEM)
ANY = pl.BlockSpec(memory_space=pl.ANY)
WIDE = pltpu.CompilerParams(vmem_limit_bytes=60 * 1024 * 1024)
PARAMS = pltpu.CompilerParams(vmem_limit_bytes=20 * 1024 * 1024)


def dot(a, b, ca=1, cb=0):
    return lax.dot_general(a, b, (((ca,), (cb,)), ((), ())), preferred_element_type=f32)


def by_core(put, keep, send):
    for c in range(2):
        @pl.when(lax.axis_index("c") == c)
        def _():
            put(keep, c * HEAD)
            put(send, (1 - c) * HEAD)


def proj_kernel(act, wq, wk, wv, down_q, down_v, up_q, up_v, grad, keep, send, rank, aq, ak, av, rq, rv):
    step = pl.program_id(0)
    last = pl.num_programs(0) - 1
    a = act[...]
    parts = [(ak, wk), (av, wv), (rv, down_v), (aq, wq), (rq, down_q)]

    @pl.when(step == 0)
    def _():
        for total, w in parts:
            total[...] = dot(a, w[...])

    @pl.when(step > 0)
    def _():
        for total, w in parts:
            total[...] += dot(a, w[...])

    @pl.when(step == last)
    def _():
        low_q = rq[...].astype(bf16)
        low_v = rv[...].astype(bf16)
        rank[:, :RANK] = low_q
        rank[:, RANK:] = low_v
        keys = ak[...].astype(bf16)
        values = (av[...] + dot(low_v, up_v[...])).astype(bf16)
        query = (aq[...] + dot(low_q, up_q[...])).astype(bf16)

        def put(ref, at):
            ref[:, :HEAD] = keys[:, at:at + HEAD]
            ref[:, HEAD:2 * HEAD] = values[:, at:at + HEAD]
            ref[:, 2 * HEAD:3 * HEAD] = query[:, at:at + HEAD]
            ref[:, 3 * HEAD:] = grad[:, at:at + HEAD]

        by_core(put, keep, send)


def project(act, wq, wk, wv, down_q, down_v, up_q, up_v, grad):
    rows, width = act.shape
    cols = wq.shape[1]
    whole = lambda shape: pl.BlockSpec(shape, lambda k: (0, 0))
    shapes = [(rows, 4 * HEAD), (rows, 4 * HEAD), (rows, 2 * RANK)]
    return pl.pallas_call(
        proj_kernel,
        grid=(width // KT,),
        in_specs=[pl.BlockSpec((rows, KT), lambda k: (0, k))]
        + [pl.BlockSpec((KT, cols), lambda k: (k, 0))] * 3
        + [pl.BlockSpec((KT, RANK), lambda k: (k, 0))] * 2 + [whole(up_q.shape), whole(up_v.shape), whole(grad.shape)],
        out_specs=[whole(s) for s in shapes],
        out_shape=[jax.ShapeDtypeStruct(s, bf16) for s in shapes],
        scratch_shapes=[pltpu.VMEM((rows, cols), f32)] * 3 + [pltpu.VMEM((rows, RANK), f32)] * 2,
        compiler_params=WIDE,
        cost_estimate=pl.CostEstimate(flops=2 * rows * width * (3 * cols + 2 * RANK),
                                      bytes_accessed=2 * width * (rows + 3 * cols + 2 * RANK), transcendentals=0),
        name="project",
    )(act, wq, wk, wv, down_q, down_v, up_q, up_v, grad)


def assemble_kernel(keep, other, kv, qg):
    kv[:256, :] = keep[:, :256]
    kv[256:, :] = other[:, :256]
    qg[:256, :] = keep[:, 256:]
    qg[256:, :] = other[:, 256:]


def assemble(keep, other):
    return pl.pallas_call(
        assemble_kernel,
        in_specs=[VMEM] * 2,
        out_specs=[VMEM] * 2,
        out_shape=[jax.ShapeDtypeStruct((512, 256), bf16)] * 2,
        compiler_params=PARAMS,
        name="assemble",
    )(keep, other)


def lists_kernel(slot, packed, out):
    x, y, c = (lax.axis_index(n) for n in ("x", "y", "c"))

    def frame(xx, yy, local):
        core = c if local < 2 else 1 - c
        return slot[((xx * 4 + yy) * 2 + core) * 2 + local % 2]

    keys = [frame(lax.rem(x + 4 - k // 4, 4), y, k % 4) for k in range(16)]
    for q in range(16):
        out[17, q] = frame(x, lax.rem(y + 4 - q // 4, 4), q % 4)

    def one(q, _):
        f = out[17, q]
        words = [packed[f, keys[k]] for k in range(16)]
        n = 0
        for k, word in enumerate(words):
            for r in range(4):
                out[q, n + r] = k * 4 + ((word >> (2 * r)) & 3)
            n = n + (word >> 8)
        for r in range(CB):
            out[q, n + r] = 0
        out[16, q] = n
        return 0

    lax.fori_loop(0, 16, one, 0)


def visible_lists(slot, levels, order):
    packed = levels * 256 + jnp.sum(order * jnp.array([1, 4, 16, 64], jnp.int32), axis=-1)
    return pl.pallas_call(
        lists_kernel,
        in_specs=[SMEM] * 2,
        out_specs=SMEM,
        out_shape=jax.ShapeDtypeStruct((24, 128), jnp.int32),
        compiler_params=PARAMS,
        name="lists",
    )(slot, packed)


def fill_all(parts, whole):
    rows = parts[0].shape[0]
    for d, part in enumerate(parts):
        whole[d * rows:(d + 1) * rows, :] = part[...]


def load_chunk(lists, f, at, kvall):
    blocks = [kvall[pl.ds(pl.multiple_of(lists[f, at + i] * BLK, BLK), BLK), :] for i in range(CB)]
    return jnp.concatenate(blocks, axis=0)


def start_frames(lists, t, qgall, both):
    counts = []
    for j in range(CHAINS):
        f = t * CHAINS + j
        at = pl.multiple_of(f * FT, FT)
        both[j, :FT, :HEAD] = qgall[pl.ds(at, FT), :HEAD]
        both[j, FT:, HEAD:] = qgall[pl.ds(at, FT), HEAD:]
        counts.append(lists[16, f])
    chunks = [(n + CB - 1) // CB for n in counts]
    most = chunks[0]
    for n in chunks[1:]:
        most = jnp.maximum(most, n)
    return counts, chunks, most


def stats_kernel(lists, q0, q1, q2, q3, k0, k1, k2, k3, out, qgall, kvall, both):
    fill_all((q0, q1, q2, q3), qgall)
    fill_all((k0, k1, k2, k3), kvall)
    both[...] = jnp.zeros_like(both)
    row = lax.broadcasted_iota(jnp.int32, (CHUNK, HEAD), 0)

    def frames(t, _):
        counts, chunks, most = start_frames(lists, t, qgall, both)

        def chunk(ch, carry):
            kvs = [load_chunk(lists, t * CHAINS + j, jnp.minimum(ch, chunks[j] - 1) * CB, kvall)
                   for j in range(CHAINS)]
            rs = [dot(kvs[j], both[j], 1, 1) for j in range(CHAINS)]
            after = []
            for j in range(CHAINS):
                peak, total, delta = carry[j]
                s = jnp.where(row < (counts[j] - ch * CB) * BLK, rs[j][:, :FT] * SCALE2, NEG)
                new = jnp.maximum(peak, jnp.max(s, axis=0, keepdims=True))
                p = jnp.exp2(s - new)
                fix = jnp.exp2(peak - new)
                total = total * fix + jnp.sum(p, axis=0, keepdims=True)
                delta = delta * fix + jnp.sum(p * rs[j][:, FT:], axis=0, keepdims=True)
                after.append((new, total, delta))
            return tuple(after)

        zero = jnp.zeros((1, FT), f32)
        carry = lax.fori_loop(0, most, chunk, ((zero + NEG, zero, zero),) * CHAINS)
        for j in range(CHAINS):
            for i in range(3):
                out[pl.ds(16 * i + t * CHAINS + j, 1), :] = carry[j][i]
        return 0

    lax.fori_loop(0, 16 // CHAINS, frames, 0)


def row_stats(lists, qgs, kvs):
    return pl.pallas_call(
        stats_kernel,
        in_specs=[SMEM] + [VMEM] * 8,
        out_specs=VMEM,
        out_shape=jax.ShapeDtypeStruct((48, 128), f32),
        scratch_shapes=[pltpu.VMEM((2048, 2 * HEAD), bf16), pltpu.VMEM((2048, 2 * HEAD), bf16),
                        pltpu.VMEM((CHAINS, 2 * FT, 2 * HEAD), bf16)],
        compiler_params=PARAMS,
        name="row_stats",
    )(lists, *qgs, *kvs)


def merge_stats(stats, norm):
    for t in range(4):
        rows = [slice(4 * ((t - d) % 4), 4 * ((t - d) % 4) + 4) for d in range(4)]
        peaks = [stats[d][0:16][rows[d]] for d in range(4)]
        peak = jnp.maximum(jnp.maximum(peaks[0], peaks[1]), jnp.maximum(peaks[2], peaks[3]))
        total = jnp.zeros_like(peak)
        delta = jnp.zeros_like(peak)
        for d in range(4):
            fix = jnp.exp2(peaks[d] - peak)
            total += fix * stats[d][16:32][rows[d]]
            delta += fix * stats[d][32:48][rows[d]]
        norm[4 * t:4 * t + 4, :] = peak + jnp.log2(total)
        norm[16 + 4 * t:20 + 4 * t, :] = delta / total


def slot_grads(lists, t, qgall, kvall, both, acc, dva, norm):
    row = lax.broadcasted_iota(jnp.int32, (CHUNK, HEAD), 0)
    counts, chunks, most = start_frames(lists, t, qgall, both)
    lse = [norm[pl.ds(t * CHAINS + j, 1), :] for j in range(CHAINS)]
    delta = [norm[pl.ds(16 + t * CHAINS + j, 1), :] for j in range(CHAINS)]
    acc[...] = jnp.zeros_like(acc)

    def chunk(ch, _):
        at = [jnp.minimum(ch, chunks[j] - 1) * CB for j in range(CHAINS)]
        kvs = [load_chunk(lists, t * CHAINS + j, at[j], kvall) for j in range(CHAINS)]
        rs = [dot(kvs[j], both[j], 1, 1) for j in range(CHAINS)]
        lows, pairs = [], []
        for j in range(CHAINS):
            s = jnp.where(row < (counts[j] - ch * CB) * BLK, rs[j][:, :FT] * SCALE2, NEG)
            p = jnp.exp2(s - lse[j])
            low = p.astype(bf16)
            ds = (p * (rs[j][:, FT:] - delta[j]) * SCALE).astype(bf16)
            lows.append(low)
            pairs.append(jnp.concatenate([low, ds], axis=1))
        for j in range(CHAINS):
            product = dot(kvs[j], pairs[j], 0, 0)
            acc[j, 0] += product[HEAD:, :FT]
            acc[j, 1] += product[:HEAD, FT:]
        dvs = [dot(lows[j], both[j, FT:, HEAD:]) for j in range(CHAINS)]
        for i in range(CB):
            for j in range(CHAINS):
                to = pl.multiple_of(lists[t * CHAINS + j, at[j] + i] * BLK, BLK)
                dva[j, pl.ds(to, BLK), :] += dvs[j][i * BLK:(i + 1) * BLK, :]
        return 0

    lax.fori_loop(0, most, chunk, 0)


def put_slot(acc, a):
    for j in range(CHAINS):
        dq = acc[j, 1].T
        high = dq.astype(bf16)
        rows = slice(j * FT, (j + 1) * FT)
        a[rows, :HEAD] = acc[j, 0].T.astype(a.dtype)
        if a.dtype == bf16:
            a[rows, HEAD:2 * HEAD] = high
            a[rows, 2 * HEAD:] = (dq - high.astype(f32)).astype(bf16)
        else:
            a[rows, HEAD:] = dq


def grads_kernel(lists, s0, s1, s2, s3, q0, q1, q2, q3, k0, k1, k2, k3,
                 a0, a1, a2, a3, b0, b1, b2, b3, qgall, kvall, both, acc, dva, norm):
    fill_all((q0, q1, q2, q3), qgall)
    fill_all((k0, k1, k2, k3), kvall)
    both[...] = jnp.zeros_like(both)
    dva[...] = jnp.zeros_like(dva)
    merge_stats([ref[...] for ref in (s0, s1, s2, s3)], norm)

    def slot(t, _):
        slot_grads(lists, t, qgall, kvall, both, acc, dva, norm)
        for d, a in enumerate((a0, a1, a2, a3)):
            pl.when(t == d)(lambda a=a: put_slot(acc, a))
        return 0

    lax.fori_loop(0, 4, slot, 0)
    for d, b in enumerate((b0, b1, b2, b3)):
        total = dva[0, d * 512:(d + 1) * 512, :]
        for j in range(1, CHAINS):
            total += dva[j, d * 512:(d + 1) * 512, :]
        b[...] = total.astype(b.dtype)


def attention_grads(lists, stats, qgs, kvs):
    outs = [(2 * HEAD, f32)] + [(3 * HEAD, bf16)] * 3 + [(HEAD, t) for t in (f32, WIRE, WIRE2, WIRE)]
    keys = pltpu.VMEM((2048, 2 * HEAD), bf16)
    return pl.pallas_call(
        grads_kernel,
        in_specs=[SMEM] + [VMEM] * 12,
        out_specs=[VMEM] * 8,
        out_shape=[jax.ShapeDtypeStruct((512, lanes), t) for lanes, t in outs],
        scratch_shapes=[keys, keys, pltpu.VMEM((CHAINS, 2 * FT, 2 * HEAD), bf16),
                        pltpu.VMEM((CHAINS, 2, HEAD, FT), f32), pltpu.VMEM((CHAINS, 2048, HEAD), f32),
                        pltpu.VMEM((32, 128), f32)],
        compiler_params=PARAMS,
        name="attention_grads",
    )(lists, *stats, *qgs, *kvs)


def finish_kernel(b0, b1, b2, b3, a0, a1, a2, a3, own, other, uq, uv, after,
                  o_keep, o_send, rg_keep, rg_send, up):
    out, dq, dv = a0[:, :HEAD], a0[:, HEAD:], b0[...]
    for a, b in ((a1, b1), (a2, b2), (a3, b3)):
        out += a[:, :HEAD].astype(f32)
        dq += a[:, HEAD:2 * HEAD].astype(f32) + a[:, 2 * HEAD:].astype(f32)
        dv += b[...].astype(f32)
    out, dq, dv = out.astype(bf16), dq.astype(bf16), dv.astype(bf16)
    o_keep[...] = out[:256]
    o_send[...] = out[256:]
    for c in range(2):
        @pl.when(lax.axis_index("c") == c)
        def _():
            gq = dot(dq, uq[:, c * HEAD:(c + 1) * HEAD], 1, 1)
            gv = dot(dv, uv[:, c * HEAD:(c + 1) * HEAD], 1, 1)
            rg_keep[:, :RANK] = gq[:256]
            rg_keep[:, RANK:] = gv[:256]
            rg_send[:, :RANK] = gq[256:]
            rg_send[:, RANK:] = gv[256:]
    up[:, :HEAD] = dot(own[:, :RANK], dq[:256], 0, 0) + dot(other[:, :RANK], dq[256:], 0, 0)
    up[:, HEAD:] = dot(own[:, RANK:], dv[:256], 0, 0) + dot(other[:, RANK:], dv[256:], 0, 0)


def finish(b, a, own, other, uq, uv, after):
    return pl.pallas_call(
        finish_kernel,
        in_specs=[VMEM] * 12 + [ANY],
        out_specs=[VMEM] * 5,
        out_shape=[jax.ShapeDtypeStruct((256, HEAD), bf16)] * 2
        + [jax.ShapeDtypeStruct((r, 256), f32) for r in (256, 256, 128)],
        compiler_params=PARAMS,
        name="finish",
    )(*b, *a, own, other, uq, uv, after)


def down_kernel(act_t, own, r1, r2, r3, mine, theirs):
    rg = (own[...] + r1[...].astype(f32) + r2[...].astype(f32) + r3[...].astype(f32)).astype(bf16)
    rows = mine.shape[0]
    for c in range(2):
        @pl.when(lax.axis_index("c") == c)
        def _():
            mine[...] = dot(act_t[c * rows:(c + 1) * rows, :], rg)
            theirs[...] = dot(act_t[(1 - c) * rows:(2 - c) * rows, :], rg)


def down_terms(act_t, own, others):
    rows = act_t.shape[0] // 2
    return pl.pallas_call(
        down_kernel,
        in_specs=[VMEM] * 5,
        out_specs=[VMEM] * 2,
        out_shape=[jax.ShapeDtypeStruct((rows, 256), f32)] * 2,
        compiler_params=PARAMS,
        name="down_terms",
    )(act_t, own, *others)


def pack_kernel(mine, theirs, up, out):
    for i in range(16):
        part = mine[i * 40:(i + 1) * 40, :] + theirs[i * 40:(i + 1) * 40, :]
        out[i, :, :] = jnp.concatenate([part, up[i * 8:(i + 1) * 8, :]], axis=0).astype(out.dtype)


def pack(mine, theirs, up):
    return pl.pallas_call(
        pack_kernel,
        in_specs=[VMEM] * 3,
        out_specs=VMEM,
        out_shape=jax.ShapeDtypeStruct((16, 48, 256), bf16),
        compiler_params=PARAMS,
        name="pack",
    )(mine, theirs, up)


def emit_kernel(own, other, o_keep, o_other, att, down_q, up_q, down_v, up_v):
    zz = pl.program_id(0)
    halves = [own, other]
    for c in range(2):
        @pl.when(lax.axis_index("c") == c)
        def _():
            for cc in range(2):
                src = halves[(c + cc) % 2]
                for i in range(16):
                    part = src[zz * 16 + i].astype(f32)
                    at = cc * 640 + i * 40
                    down_q[at:at + 40, :] = part[:40, :RANK]
                    down_v[at:at + 40, :] = part[:40, RANK:]

            @pl.when(zz == 0)
            def _():
                outs = [o_keep, o_other]
                for cc in range(2):
                    src = halves[(c + cc) % 2]
                    att[:, cc * HEAD:(cc + 1) * HEAD] = outs[(c + cc) % 2][...]
                    for i in range(16):
                        part = src[lax.axis_index("z") * 16 + i].astype(f32)
                        up_q[i * 8:(i + 1) * 8, cc * HEAD:(cc + 1) * HEAD] = part[40:, :HEAD]
                        up_v[i * 8:(i + 1) * 8, cc * HEAD:(cc + 1) * HEAD] = part[40:, HEAD:]


def emit(own, other, o_keep, o_other):
    whole = lambda a: pl.BlockSpec(a, lambda k: (0,) * len(a))
    return pl.pallas_call(
        emit_kernel,
        grid=(4,),
        in_specs=[whole(a.shape) for a in (own, other, o_keep, o_other)],
        out_specs=[whole((256, 256)), pl.BlockSpec((1280, RANK), lambda k: (k, 0)), whole((RANK, 256)),
                   pl.BlockSpec((1280, RANK), lambda k: (k, 0)), whole((RANK, 256))],
        out_shape=[jax.ShapeDtypeStruct((256, 256), bf16), jax.ShapeDtypeStruct((5120, RANK), f32),
                   jax.ShapeDtypeStruct((RANK, 256), f32), jax.ShapeDtypeStruct((5120, RANK), f32),
                   jax.ShapeDtypeStruct((RANK, 256), f32)],
        compiler_params=PARAMS,
        name="emit",
    )(own, other, o_keep, o_other)


def total_kernel(parts, after, out):
    total = parts[0].astype(f32)
    for i in range(1, 16):
        total += parts[i].astype(f32)
    low = total.astype(bf16)
    for i in range(64):
        out[i, :, :] = low


def total_for_all(parts, after):
    return pl.pallas_call(
        total_kernel,
        in_specs=[VMEM, ANY],
        out_specs=VMEM,
        out_shape=jax.ShapeDtypeStruct((64, 48, 256), bf16),
        compiler_params=PARAMS,
        name="total_for_all",
    )(parts, after)


def ring(n, d):
    return [(i, (i + d) % n) for i in range(n)]


def swap(a):
    return lax.ppermute(a, "c", ring(2, 1))


def spread(a, axis):
    one, three, two = [lax.ppermute(a, axis, ring(4, d)) for d in (1, 3, 2)]
    return [a, one, two, three]


def collect(parts, axis):
    return [parts[0]] + [lax.ppermute(parts[d], axis, ring(4, -d)) for d in (1, 2, 3)]


def half(a, index, size):
    return lax.dynamic_slice_in_dim(a, index * size, size, axis=1)


def local(act, wq, wk, wv, dq, uq, dv, uv, grad_out, levels, order, slot):
    z = lax.axis_index("z")
    keep, send, rank = project(act, wq, wk, wv, dq, dv, uq, uv, grad_out)
    kv, qg = assemble(keep, swap(send))
    kvs = spread(kv, "x")
    qgs = spread(qg, "y")
    lists = visible_lists(slot, levels, order)
    act_t = half(act, z, act.shape[1] // 4).T
    stats = spread(row_stats(lists, qgs, kvs), "y")
    parts = attention_grads(lists, stats, qgs, kvs)
    a = collect(parts[:4], "y")
    b = collect(parts[4:], "x")
    o_keep, o_send, rg_keep, rg_send, up = finish(b, a, rank, swap(rank), uq, uv, act_t)
    o_other = swap(o_send)
    rg = rg_keep + swap(rg_send)
    mine, theirs = down_terms(act_t, rg, spread(rg.astype(bf16), "z")[1:])
    terms = lax.all_to_all(pack(mine, swap(theirs), up), ("x", "y"), 0, 0, tiled=True)
    wide = lax.all_to_all(total_for_all(terms, o_other), ("z", "x", "y"), 0, 0, tiled=True)
    att, down_q, up_q, down_v, up_v = emit(wide, swap(wide), o_keep, o_other)
    return att, down_q, up_q, down_v, up_v


def solution(mesh):
    torus = Mesh(mesh.devices.reshape(4, 4, 2, 4), ("x", "y", "c", "z"))
    tm = ("x", "y", "c")
    return jax.shard_map(
        local,
        mesh=torus,
        in_specs=(
            P(tm, None),
            P(None, "z"),
            P(None, "z"),
            P(None, "z"),
            P(),
            P(None, "z"),
            P(),
            P(None, "z"),
            P(tm, "z"),
            P(),
            P(),
            P(),
        ),
        out_specs=(P(tm, "z"), P(), P(None, "z"), P(), P(None, "z")),
        check_vma=False,
    )
```

```python
import math

import jax
import jax.numpy as jnp
from jax import lax
from jax.experimental import pallas as pl
from jax.experimental.pallas import tpu as pltpu
from jax.sharding import Mesh
from jax.sharding import PartitionSpec as P

HEAD = 128
FT = 128
BLK = 32
RANK = 128
CHUNK = 512
CB = CHUNK // BLK
CHAINS = 4
STAT_CHAINS = 8
SCALE = HEAD ** -0.5
SCALE2 = SCALE * math.log2(math.e)
NEG = -1e30
f32 = jnp.float32
bf16 = jnp.bfloat16
WIRE = f32
WIRE2 = bf16
KT = 1280
VMEM = pl.BlockSpec(memory_space=pltpu.VMEM)
SMEM = pl.BlockSpec(memory_space=pltpu.SMEM)
ANY = pl.BlockSpec(memory_space=pl.ANY)
WIDE = pltpu.CompilerParams(vmem_limit_bytes=60 * 1024 * 1024)
PARAMS = pltpu.CompilerParams(vmem_limit_bytes=20 * 1024 * 1024)


def dot(a, b, ca=1, cb=0):
    return lax.dot_general(a, b, (((ca,), (cb,)), ((), ())), preferred_element_type=f32)


def by_core(put, keep, send):
    for c in range(2):
        @pl.when(lax.axis_index("c") == c)
        def _():
            put(keep, c * HEAD)
            put(send, (1 - c) * HEAD)


def proj_kernel(act, wq, wk, wv, down_q, down_v, up_q, up_v, grad, keep, send, rank, aq, ak, av, rq, rv):
    step = pl.program_id(0)
    last = pl.num_programs(0) - 1
    a = act[...]
    parts = [(ak, wk), (av, wv), (rv, down_v), (aq, wq), (rq, down_q)]

    @pl.when(step == 0)
    def _():
        for total, w in parts:
            total[...] = dot(a, w[...])

    @pl.when(step > 0)
    def _():
        for total, w in parts:
            total[...] += dot(a, w[...])

    @pl.when(step == last)
    def _():
        low_q = rq[...].astype(bf16)
        low_v = rv[...].astype(bf16)
        rank[:, :RANK] = low_q
        rank[:, RANK:] = low_v
        keys = ak[...].astype(bf16)
        values = (av[...] + dot(low_v, up_v[...])).astype(bf16)
        query = (aq[...] + dot(low_q, up_q[...])).astype(bf16)

        def put(ref, at):
            ref[:, :HEAD] = keys[:, at:at + HEAD]
            ref[:, HEAD:2 * HEAD] = values[:, at:at + HEAD]
            ref[:, 2 * HEAD:3 * HEAD] = query[:, at:at + HEAD]
            ref[:, 3 * HEAD:] = grad[:, at:at + HEAD]

        by_core(put, keep, send)


def project(act, wq, wk, wv, down_q, down_v, up_q, up_v, grad):
    rows, width = act.shape
    cols = wq.shape[1]
    whole = lambda shape: pl.BlockSpec(shape, lambda k: (0, 0))
    shapes = [(rows, 4 * HEAD), (rows, 4 * HEAD), (rows, 2 * RANK)]
    return pl.pallas_call(
        proj_kernel,
        grid=(width // KT,),
        in_specs=[pl.BlockSpec((rows, KT), lambda k: (0, k))]
        + [pl.BlockSpec((KT, cols), lambda k: (k, 0))] * 3
        + [pl.BlockSpec((KT, RANK), lambda k: (k, 0))] * 2 + [whole(up_q.shape), whole(up_v.shape), whole(grad.shape)],
        out_specs=[whole(s) for s in shapes],
        out_shape=[jax.ShapeDtypeStruct(s, bf16) for s in shapes],
        scratch_shapes=[pltpu.VMEM((rows, cols), f32)] * 3 + [pltpu.VMEM((rows, RANK), f32)] * 2,
        compiler_params=WIDE,
        cost_estimate=pl.CostEstimate(flops=2 * rows * width * (3 * cols + 2 * RANK),
                                      bytes_accessed=2 * width * (rows + 3 * cols + 2 * RANK), transcendentals=0),
        name="project",
    )(act, wq, wk, wv, down_q, down_v, up_q, up_v, grad)


def assemble_kernel(keep, other, kv, qg):
    kv[:256, :] = keep[:, :256]
    kv[256:, :] = other[:, :256]
    qg[:256, :] = keep[:, 256:]
    qg[256:, :] = other[:, 256:]


def assemble(keep, other):
    return pl.pallas_call(
        assemble_kernel,
        in_specs=[VMEM] * 2,
        out_specs=[VMEM] * 2,
        out_shape=[jax.ShapeDtypeStruct((512, 256), bf16)] * 2,
        compiler_params=PARAMS,
        name="assemble",
    )(keep, other)


def lists_kernel(slot, packed, out):
    x, y, c = (lax.axis_index(n) for n in ("x", "y", "c"))

    def frame(xx, yy, local):
        core = c if local < 2 else 1 - c
        return slot[((xx * 4 + yy) * 2 + core) * 2 + local % 2]

    keys = [frame(lax.rem(x + 4 - k // 4, 4), y, k % 4) for k in range(16)]
    for q in range(16):
        out[17, q] = frame(x, lax.rem(y + 4 - q // 4, 4), q % 4)

    def one(q, _):
        f = out[17, q]
        words = [packed[f, keys[k]] for k in range(16)]
        n = 0
        for k, word in enumerate(words):
            for r in range(4):
                out[q, n + r] = k * 4 + ((word >> (2 * r)) & 3)
            n = n + (word >> 8)
        for r in range(CB):
            out[q, n + r] = 0
        out[16, q] = n
        return 0

    lax.fori_loop(0, 16, one, 0)


def visible_lists(slot, levels, order):
    packed = levels * 256 + jnp.sum(order * jnp.array([1, 4, 16, 64], jnp.int32), axis=-1)
    return pl.pallas_call(
        lists_kernel,
        in_specs=[SMEM] * 2,
        out_specs=SMEM,
        out_shape=jax.ShapeDtypeStruct((24, 128), jnp.int32),
        compiler_params=PARAMS,
        name="lists",
    )(slot, packed)


def fill_all(parts, whole):
    rows = parts[0].shape[0]
    for d, part in enumerate(parts):
        whole[d * rows:(d + 1) * rows, :] = part[...]


def load_chunk(lists, f, at, kvall):
    blocks = [kvall[pl.ds(pl.multiple_of(lists[f, at + i] * BLK, BLK), BLK), :] for i in range(CB)]
    return jnp.concatenate(blocks, axis=0)


def start_frames(lists, t, qgall, both):
    chains = both.shape[0]
    counts = []
    for j in range(chains):
        f = t * chains + j
        at = pl.multiple_of(f * FT, FT)
        both[j, :FT, :HEAD] = qgall[pl.ds(at, FT), :HEAD]
        both[j, FT:, HEAD:] = qgall[pl.ds(at, FT), HEAD:]
        counts.append(lists[16, f])
    chunks = [(n + CB - 1) // CB for n in counts]
    most = chunks[0]
    for n in chunks[1:]:
        most = jnp.maximum(most, n)
    return counts, chunks, most


def stats_kernel(lists, q0, q1, q2, q3, k0, k1, k2, k3, out, qgall, kvall, both):
    fill_all((q0, q1, q2, q3), qgall)
    fill_all((k0, k1, k2, k3), kvall)
    both[...] = jnp.zeros_like(both)
    row = lax.broadcasted_iota(jnp.int32, (CHUNK, HEAD), 0)

    def frames(t, _):
        counts, chunks, most = start_frames(lists, t, qgall, both)

        def chunk(ch, carry):
            kvs = [load_chunk(lists, t * STAT_CHAINS + j, jnp.minimum(ch, chunks[j] - 1) * CB, kvall)
                   for j in range(STAT_CHAINS)]
            rs = [dot(kvs[j], both[j], 1, 1) for j in range(STAT_CHAINS)]
            after = []
            for j in range(STAT_CHAINS):
                peak, total, delta = carry[j]
                s = jnp.where(row < (counts[j] - ch * CB) * BLK, rs[j][:, :FT] * SCALE2, NEG)
                new = jnp.maximum(peak, jnp.max(s, axis=0, keepdims=True))
                p = jnp.exp2(s - new)
                fix = jnp.exp2(peak - new)
                total = total * fix + jnp.sum(p, axis=0, keepdims=True)
                delta = delta * fix + jnp.sum(p * rs[j][:, FT:], axis=0, keepdims=True)
                after.append((new, total, delta))
            return tuple(after)

        zero = jnp.zeros((1, FT), f32)
        carry = lax.fori_loop(0, most, chunk, ((zero + NEG, zero, zero),) * STAT_CHAINS)
        for j in range(STAT_CHAINS):
            for i in range(3):
                out[pl.ds(16 * i + t * STAT_CHAINS + j, 1), :] = carry[j][i]
        return 0

    lax.fori_loop(0, 16 // STAT_CHAINS, frames, 0)


def row_stats(lists, qgs, kvs):
    return pl.pallas_call(
        stats_kernel,
        in_specs=[SMEM] + [VMEM] * 8,
        out_specs=VMEM,
        out_shape=jax.ShapeDtypeStruct((48, 128), f32),
        scratch_shapes=[pltpu.VMEM((2048, 2 * HEAD), bf16), pltpu.VMEM((2048, 2 * HEAD), bf16),
                        pltpu.VMEM((STAT_CHAINS, 2 * FT, 2 * HEAD), bf16)],
        compiler_params=PARAMS,
        name="row_stats",
    )(lists, *qgs, *kvs)


def merge_stats(stats, norm):
    for t in range(4):
        rows = [slice(4 * ((t - d) % 4), 4 * ((t - d) % 4) + 4) for d in range(4)]
        peaks = [stats[d][0:16][rows[d]] for d in range(4)]
        peak = jnp.maximum(jnp.maximum(peaks[0], peaks[1]), jnp.maximum(peaks[2], peaks[3]))
        total = jnp.zeros_like(peak)
        delta = jnp.zeros_like(peak)
        for d in range(4):
            fix = jnp.exp2(peaks[d] - peak)
            total += fix * stats[d][16:32][rows[d]]
            delta += fix * stats[d][32:48][rows[d]]
        norm[4 * t:4 * t + 4, :] = peak + jnp.log2(total)
        norm[16 + 4 * t:20 + 4 * t, :] = delta / total


def slot_grads(lists, t, qgall, kvall, both, acc, dva, norm):
    row = lax.broadcasted_iota(jnp.int32, (CHUNK, HEAD), 0)
    counts, chunks, most = start_frames(lists, t, qgall, both)
    lse = [norm[pl.ds(t * CHAINS + j, 1), :] for j in range(CHAINS)]
    delta = [norm[pl.ds(16 + t * CHAINS + j, 1), :] for j in range(CHAINS)]
    acc[...] = jnp.zeros_like(acc)

    def chunk(ch, _):
        at = [jnp.minimum(ch, chunks[j] - 1) * CB for j in range(CHAINS)]
        kvs = [load_chunk(lists, t * CHAINS + j, at[j], kvall) for j in range(CHAINS)]
        rs = [dot(kvs[j], both[j], 1, 1) for j in range(CHAINS)]
        lows, pairs = [], []
        for j in range(CHAINS):
            s = jnp.where(row < (counts[j] - ch * CB) * BLK, rs[j][:, :FT] * SCALE2, NEG)
            p = jnp.exp2(s - lse[j])
            low = p.astype(bf16)
            ds = (p * (rs[j][:, FT:] - delta[j]) * SCALE).astype(bf16)
            lows.append(low)
            pairs.append(jnp.concatenate([low, ds], axis=1))
        for j in range(CHAINS):
            product = dot(kvs[j], pairs[j], 0, 0)
            acc[j, 0] += product[HEAD:, :FT]
            acc[j, 1] += product[:HEAD, FT:]
        dvs = [dot(lows[j], both[j, FT:, HEAD:]) for j in range(CHAINS)]
        for i in range(CB):
            for j in range(CHAINS):
                to = pl.multiple_of(lists[t * CHAINS + j, at[j] + i] * BLK, BLK)
                dva[j, pl.ds(to, BLK), :] += dvs[j][i * BLK:(i + 1) * BLK, :]
        return 0

    lax.fori_loop(0, most, chunk, 0)


def put_slot(acc, a):
    for j in range(CHAINS):
        dq = acc[j, 1].T
        high = dq.astype(bf16)
        rows = slice(j * FT, (j + 1) * FT)
        a[rows, :HEAD] = acc[j, 0].T.astype(a.dtype)
        if a.dtype == bf16:
            a[rows, HEAD:2 * HEAD] = high
            a[rows, 2 * HEAD:] = (dq - high.astype(f32)).astype(bf16)
        else:
            a[rows, HEAD:] = dq


def grads_kernel(lists, s0, s1, s2, s3, q0, q1, q2, q3, k0, k1, k2, k3,
                 a0, a1, a2, a3, b0, b1, b2, b3, qgall, kvall, both, acc, dva, norm):
    fill_all((q0, q1, q2, q3), qgall)
    fill_all((k0, k1, k2, k3), kvall)
    both[...] = jnp.zeros_like(both)
    dva[...] = jnp.zeros_like(dva)
    merge_stats([ref[...] for ref in (s0, s1, s2, s3)], norm)

    def slot(t, _):
        slot_grads(lists, t, qgall, kvall, both, acc, dva, norm)
        for d, a in enumerate((a0, a1, a2, a3)):
            pl.when(t == d)(lambda a=a: put_slot(acc, a))
        return 0

    lax.fori_loop(0, 4, slot, 0)
    for d, b in enumerate((b0, b1, b2, b3)):
        total = dva[0, d * 512:(d + 1) * 512, :]
        for j in range(1, CHAINS):
            total += dva[j, d * 512:(d + 1) * 512, :]
        b[...] = total.astype(b.dtype)


def attention_grads(lists, stats, qgs, kvs):
    outs = [(2 * HEAD, f32)] + [(3 * HEAD, bf16)] * 3 + [(HEAD, t) for t in (f32, WIRE, WIRE2, WIRE)]
    keys = pltpu.VMEM((2048, 2 * HEAD), bf16)
    return pl.pallas_call(
        grads_kernel,
        in_specs=[SMEM] + [VMEM] * 12,
        out_specs=[VMEM] * 8,
        out_shape=[jax.ShapeDtypeStruct((512, lanes), t) for lanes, t in outs],
        scratch_shapes=[keys, keys, pltpu.VMEM((CHAINS, 2 * FT, 2 * HEAD), bf16),
                        pltpu.VMEM((CHAINS, 2, HEAD, FT), f32), pltpu.VMEM((CHAINS, 2048, HEAD), f32),
                        pltpu.VMEM((32, 128), f32)],
        compiler_params=PARAMS,
        name="attention_grads",
    )(lists, *stats, *qgs, *kvs)


def finish_kernel(b0, b1, b2, b3, a0, a1, a2, a3, own, other, uq, uv, after,
                  o_keep, o_send, rg_keep, rg_send, up):
    out, dq, dv = a0[:, :HEAD], a0[:, HEAD:], b0[...]
    for a, b in ((a1, b1), (a2, b2), (a3, b3)):
        out += a[:, :HEAD].astype(f32)
        dq += a[:, HEAD:2 * HEAD].astype(f32) + a[:, 2 * HEAD:].astype(f32)
        dv += b[...].astype(f32)
    out, dq, dv = out.astype(bf16), dq.astype(bf16), dv.astype(bf16)
    o_keep[...] = out[:256]
    o_send[...] = out[256:]
    for c in range(2):
        @pl.when(lax.axis_index("c") == c)
        def _():
            gq = dot(dq, uq[:, c * HEAD:(c + 1) * HEAD], 1, 1)
            gv = dot(dv, uv[:, c * HEAD:(c + 1) * HEAD], 1, 1)
            rg_keep[:, :RANK] = gq[:256]
            rg_keep[:, RANK:] = gv[:256]
            rg_send[:, :RANK] = gq[256:]
            rg_send[:, RANK:] = gv[256:]
    up[:, :HEAD] = dot(own[:, :RANK], dq[:256], 0, 0) + dot(other[:, :RANK], dq[256:], 0, 0)
    up[:, HEAD:] = dot(own[:, RANK:], dv[:256], 0, 0) + dot(other[:, RANK:], dv[256:], 0, 0)


def finish(b, a, own, other, uq, uv, after):
    return pl.pallas_call(
        finish_kernel,
        in_specs=[VMEM] * 12 + [ANY],
        out_specs=[VMEM] * 5,
        out_shape=[jax.ShapeDtypeStruct((256, HEAD), bf16)] * 2
        + [jax.ShapeDtypeStruct((r, 256), f32) for r in (256, 256, 128)],
        compiler_params=PARAMS,
        name="finish",
    )(*b, *a, own, other, uq, uv, after)


def columns_kernel(act, out, rows, sem):
    width = rows.shape[1]
    at = pl.multiple_of(lax.axis_index("z") * width, 128)
    copy = pltpu.make_async_copy(act.at[:, pl.ds(at, width)], rows, sem)
    copy.start()
    copy.wait()
    for i in range(width // 256):
        out[i * 256:(i + 1) * 256, :] = rows[:, i * 256:(i + 1) * 256].T


def columns(act, after):
    rows, width = act.shape[0], act.shape[1] // 4

    def kernel(act, after, out, part, sem):
        columns_kernel(act, out, part, sem)

    return pl.pallas_call(
        kernel,
        in_specs=[ANY, ANY],
        out_specs=VMEM,
        out_shape=jax.ShapeDtypeStruct((width, rows), bf16),
        scratch_shapes=[pltpu.VMEM((rows, width), bf16), pltpu.SemaphoreType.DMA(())],
        compiler_params=PARAMS,
        name="columns",
    )(act, after)


def cores_kernel(keep, other, total, low):
    rg = keep[...] + other[...]
    total[...] = rg
    low[...] = rg.astype(bf16)


def add_cores(keep, other):
    return pl.pallas_call(
        cores_kernel,
        in_specs=[VMEM] * 2,
        out_specs=[VMEM] * 2,
        out_shape=[jax.ShapeDtypeStruct((256, 256), t) for t in (f32, bf16)],
        compiler_params=PARAMS,
        name="add_cores",
    )(keep, other)


def down_kernel(act_t, own, r1, r2, r3, mine, theirs):
    rg = (own[...] + r1[...].astype(f32) + r2[...].astype(f32) + r3[...].astype(f32)).astype(bf16)
    rows = mine.shape[0]
    for c in range(2):
        @pl.when(lax.axis_index("c") == c)
        def _():
            mine[...] = dot(act_t[c * rows:(c + 1) * rows, :], rg)
            theirs[...] = dot(act_t[(1 - c) * rows:(2 - c) * rows, :], rg)


def down_terms(act_t, own, others):
    rows = act_t.shape[0] // 2
    return pl.pallas_call(
        down_kernel,
        in_specs=[VMEM] * 5,
        out_specs=[VMEM] * 2,
        out_shape=[jax.ShapeDtypeStruct((rows, 256), f32)] * 2,
        compiler_params=PARAMS,
        name="down_terms",
    )(act_t, own, *others)


def pack_kernel(mine, theirs, up, out):
    for i in range(16):
        part = mine[i * 40:(i + 1) * 40, :] + theirs[i * 40:(i + 1) * 40, :]
        out[i, :, :] = jnp.concatenate([part, up[i * 8:(i + 1) * 8, :]], axis=0).astype(out.dtype)


def pack(mine, theirs, up):
    return pl.pallas_call(
        pack_kernel,
        in_specs=[VMEM] * 3,
        out_specs=VMEM,
        out_shape=jax.ShapeDtypeStruct((16, 48, 256), bf16),
        compiler_params=PARAMS,
        name="pack",
    )(mine, theirs, up)


def emit_kernel(own, other, o_keep, o_other, att, down_q, up_q, down_v, up_v):
    zz = pl.program_id(0)
    halves = [own, other]
    for c in range(2):
        @pl.when(lax.axis_index("c") == c)
        def _():
            for cc in range(2):
                src = halves[(c + cc) % 2]
                for i in range(16):
                    part = src[zz * 16 + i].astype(f32)
                    at = cc * 640 + i * 40
                    down_q[at:at + 40, :] = part[:40, :RANK]
                    down_v[at:at + 40, :] = part[:40, RANK:]

            @pl.when(zz == 0)
            def _():
                outs = [o_keep, o_other]
                for cc in range(2):
                    src = halves[(c + cc) % 2]
                    att[:, cc * HEAD:(cc + 1) * HEAD] = outs[(c + cc) % 2][...]
                    for i in range(16):
                        part = src[lax.axis_index("z") * 16 + i].astype(f32)
                        up_q[i * 8:(i + 1) * 8, cc * HEAD:(cc + 1) * HEAD] = part[40:, :HEAD]
                        up_v[i * 8:(i + 1) * 8, cc * HEAD:(cc + 1) * HEAD] = part[40:, HEAD:]


def emit(own, other, o_keep, o_other):
    whole = lambda a: pl.BlockSpec(a, lambda k: (0,) * len(a))
    return pl.pallas_call(
        emit_kernel,
        grid=(4,),
        in_specs=[whole(a.shape) for a in (own, other, o_keep, o_other)],
        out_specs=[whole((256, 256)), pl.BlockSpec((1280, RANK), lambda k: (k, 0)), whole((RANK, 256)),
                   pl.BlockSpec((1280, RANK), lambda k: (k, 0)), whole((RANK, 256))],
        out_shape=[jax.ShapeDtypeStruct((256, 256), bf16), jax.ShapeDtypeStruct((5120, RANK), f32),
                   jax.ShapeDtypeStruct((RANK, 256), f32), jax.ShapeDtypeStruct((5120, RANK), f32),
                   jax.ShapeDtypeStruct((RANK, 256), f32)],
        compiler_params=PARAMS,
        name="emit",
    )(own, other, o_keep, o_other)


def total_kernel(parts, after, out):
    total = parts[0].astype(f32)
    for i in range(1, 16):
        total += parts[i].astype(f32)
    low = total.astype(bf16)
    for i in range(64):
        out[i, :, :] = low


def total_for_all(parts, after):
    return pl.pallas_call(
        total_kernel,
        in_specs=[VMEM, ANY],
        out_specs=VMEM,
        out_shape=jax.ShapeDtypeStruct((64, 48, 256), bf16),
        compiler_params=PARAMS,
        name="total_for_all",
    )(parts, after)


def ring(n, d):
    return [(i, (i + d) % n) for i in range(n)]


def swap(a):
    return lax.ppermute(a, "c", ring(2, 1))


def spread(a, axis):
    one, three, two = [lax.ppermute(a, axis, ring(4, d)) for d in (1, 3, 2)]
    return [a, one, two, three]


def relay(a, axis):
    one, three = [lax.ppermute(a, axis, ring(4, d)) for d in (1, 3)]
    return [a, one, lax.ppermute(one, axis, ring(4, 1)), three]


def collect(parts, axis):
    return [parts[0]] + [lax.ppermute(parts[d], axis, ring(4, -d)) for d in (1, 2, 3)]


def local(act, wq, wk, wv, dq, uq, dv, uv, grad_out, levels, order, slot):
    keep, send, rank = project(act, wq, wk, wv, dq, dv, uq, uv, grad_out)
    kv, qg = assemble(keep, swap(send))
    kvs = relay(kv, "x")
    qgs = relay(qg, "y")
    lists = visible_lists(slot, levels, order)
    stats = spread(row_stats(lists, qgs, kvs), "y")
    parts = attention_grads(lists, stats, qgs, kvs)
    act_t = columns(act, parts[0])
    a = collect(parts[:4], "y")
    b = collect(parts[4:], "x")
    o_keep, o_send, rg_keep, rg_send, up = finish(b, a, rank, swap(rank), uq, uv, act_t)
    o_other = swap(o_send)
    rg, low = add_cores(rg_keep, swap(rg_send))
    mine, theirs = down_terms(act_t, rg, spread(low, "z")[1:])
    terms = lax.all_to_all(pack(mine, swap(theirs), up), ("x", "y"), 0, 0, tiled=True)
    wide = lax.all_to_all(total_for_all(terms, o_other), ("z", "x", "y"), 0, 0, tiled=True)
    att, down_q, up_q, down_v, up_v = emit(wide, swap(wide), o_keep, o_other)
    return att, down_q, up_q, down_v, up_v


def solution(mesh):
    torus = Mesh(mesh.devices.reshape(4, 4, 2, 4), ("x", "y", "c", "z"))
    tm = ("x", "y", "c")
    return jax.shard_map(
        local,
        mesh=torus,
        in_specs=(
            P(tm, None),
            P(None, "z"),
            P(None, "z"),
            P(None, "z"),
            P(),
            P(None, "z"),
            P(),
            P(None, "z"),
            P(tm, "z"),
            P(),
            P(),
            P(),
        ),
        out_specs=(P(tm, "z"), P(), P(None, "z"), P(), P(None, "z")),
        check_vma=False,
    )
```

```python
import math

import jax
import jax.numpy as jnp
from jax import lax
from jax.experimental import pallas as pl
from jax.experimental.pallas import tpu as pltpu
from jax.sharding import Mesh
from jax.sharding import PartitionSpec as P

HEAD = 128
FT = 128
BLK = 32
RANK = 128
CHUNK = 512
CB = CHUNK // BLK
CHAINS = 4
STAT_CHAINS = 4
SCALE = HEAD ** -0.5
SCALE2 = SCALE * math.log2(math.e)
NEG = -1e30
f32 = jnp.float32
bf16 = jnp.bfloat16
WIRE = f32
WIRE2 = bf16
KT = 1280
VMEM = pl.BlockSpec(memory_space=pltpu.VMEM)
SMEM = pl.BlockSpec(memory_space=pltpu.SMEM)
ANY = pl.BlockSpec(memory_space=pl.ANY)
WIDE = pltpu.CompilerParams(vmem_limit_bytes=60 * 1024 * 1024)
PARAMS = pltpu.CompilerParams(vmem_limit_bytes=20 * 1024 * 1024)


def dot(a, b, ca=1, cb=0):
    return lax.dot_general(a, b, (((ca,), (cb,)), ((), ())), preferred_element_type=f32)


def by_core(put, keep, send):
    for c in range(2):
        @pl.when(lax.axis_index("c") == c)
        def _():
            put(keep, c * HEAD)
            put(send, (1 - c) * HEAD)


def proj_kernel(act, wq, wk, wv, down_q, down_v, up_q, up_v, grad, keep, send, rank, aq, ak, av, rq, rv):
    step = pl.program_id(0)
    last = pl.num_programs(0) - 1
    a = act[...]
    parts = [(ak, wk), (av, wv), (rv, down_v), (aq, wq), (rq, down_q)]

    @pl.when(step == 0)
    def _():
        for total, w in parts:
            total[...] = dot(a, w[...])

    @pl.when(step > 0)
    def _():
        for total, w in parts:
            total[...] += dot(a, w[...])

    @pl.when(step == last)
    def _():
        low_q = rq[...].astype(bf16)
        low_v = rv[...].astype(bf16)
        rank[:, :RANK] = low_q
        rank[:, RANK:] = low_v
        keys = ak[...].astype(bf16)
        values = (av[...] + dot(low_v, up_v[...])).astype(bf16)
        query = (aq[...] + dot(low_q, up_q[...])).astype(bf16)

        def put(ref, at):
            ref[:, :HEAD] = keys[:, at:at + HEAD]
            ref[:, HEAD:2 * HEAD] = values[:, at:at + HEAD]
            ref[:, 2 * HEAD:3 * HEAD] = query[:, at:at + HEAD]
            ref[:, 3 * HEAD:] = grad[:, at:at + HEAD]

        by_core(put, keep, send)


def project(act, wq, wk, wv, down_q, down_v, up_q, up_v, grad):
    rows, width = act.shape
    cols = wq.shape[1]
    whole = lambda shape: pl.BlockSpec(shape, lambda k: (0, 0))
    shapes = [(rows, 4 * HEAD), (rows, 4 * HEAD), (rows, 2 * RANK)]
    return pl.pallas_call(
        proj_kernel,
        grid=(width // KT,),
        in_specs=[pl.BlockSpec((rows, KT), lambda k: (0, k))]
        + [pl.BlockSpec((KT, cols), lambda k: (k, 0))] * 3
        + [pl.BlockSpec((KT, RANK), lambda k: (k, 0))] * 2 + [whole(up_q.shape), whole(up_v.shape), whole(grad.shape)],
        out_specs=[whole(s) for s in shapes],
        out_shape=[jax.ShapeDtypeStruct(s, bf16) for s in shapes],
        scratch_shapes=[pltpu.VMEM((rows, cols), f32)] * 3 + [pltpu.VMEM((rows, RANK), f32)] * 2,
        compiler_params=WIDE,
        cost_estimate=pl.CostEstimate(flops=2 * rows * width * (3 * cols + 2 * RANK),
                                      bytes_accessed=2 * width * (rows + 3 * cols + 2 * RANK), transcendentals=0),
        name="project",
    )(act, wq, wk, wv, down_q, down_v, up_q, up_v, grad)


def assemble_kernel(keep, other, kv, qg):
    kv[:256, :] = keep[:, :256]
    kv[256:, :] = other[:, :256]
    qg[:256, :] = keep[:, 256:]
    qg[256:, :] = other[:, 256:]


def assemble(keep, other):
    return pl.pallas_call(
        assemble_kernel,
        in_specs=[VMEM] * 2,
        out_specs=[VMEM] * 2,
        out_shape=[jax.ShapeDtypeStruct((512, 256), bf16)] * 2,
        compiler_params=PARAMS,
        name="assemble",
    )(keep, other)


def lists_kernel(slot, packed, out):
    x, y, c = (lax.axis_index(n) for n in ("x", "y", "c"))

    def frame(xx, yy, local):
        core = c if local < 2 else 1 - c
        return slot[((xx * 4 + yy) * 2 + core) * 2 + local % 2]

    keys = [frame(lax.rem(x + 4 - k // 4, 4), y, k % 4) for k in range(16)]
    for q in range(16):
        out[17, q] = frame(x, lax.rem(y + 4 - q // 4, 4), q % 4)

    def one(q, _):
        f = out[17, q]
        words = [packed[f, keys[k]] for k in range(16)]
        n = 0
        for k, word in enumerate(words):
            for r in range(4):
                out[q, n + r] = k * 4 + ((word >> (2 * r)) & 3)
            n = n + (word >> 8)
        for r in range(CB):
            out[q, n + r] = 0
        out[16, q] = n
        return 0

    lax.fori_loop(0, 16, one, 0)


def visible_lists(slot, levels, order):
    packed = levels * 256 + jnp.sum(order * jnp.array([1, 4, 16, 64], jnp.int32), axis=-1)
    return pl.pallas_call(
        lists_kernel,
        in_specs=[SMEM] * 2,
        out_specs=SMEM,
        out_shape=jax.ShapeDtypeStruct((24, 128), jnp.int32),
        compiler_params=PARAMS,
        name="lists",
    )(slot, packed)


def fill_all(parts, whole):
    rows = parts[0].shape[0]
    for d, part in enumerate(parts):
        whole[d * rows:(d + 1) * rows, :] = part[...]


def load_chunk(lists, f, at, kvall):
    blocks = [kvall[pl.ds(pl.multiple_of(lists[f, at + i] * BLK, BLK), BLK), :] for i in range(CB)]
    return jnp.concatenate(blocks, axis=0)


def start_frames(lists, t, qgall, both):
    chains = both.shape[0]
    counts = []
    for j in range(chains):
        f = t * chains + j
        at = pl.multiple_of(f * FT, FT)
        both[j, :FT, :HEAD] = qgall[pl.ds(at, FT), :HEAD]
        both[j, FT:, HEAD:] = qgall[pl.ds(at, FT), HEAD:]
        counts.append(lists[16, f])
    chunks = [(n + CB - 1) // CB for n in counts]
    most = chunks[0]
    for n in chunks[1:]:
        most = jnp.maximum(most, n)
    return counts, chunks, most


def stats_kernel(lists, q0, q1, q2, q3, k0, k1, k2, k3, out, qgall, kvall, both):
    fill_all((q0, q1, q2, q3), qgall)
    fill_all((k0, k1, k2, k3), kvall)
    both[...] = jnp.zeros_like(both)
    row = lax.broadcasted_iota(jnp.int32, (CHUNK, HEAD), 0)

    def frames(t, _):
        counts, chunks, most = start_frames(lists, t, qgall, both)

        def chunk(ch, carry):
            kvs = [load_chunk(lists, t * STAT_CHAINS + j, jnp.minimum(ch, chunks[j] - 1) * CB, kvall)
                   for j in range(STAT_CHAINS)]
            rs = [dot(kvs[j], both[j], 1, 1) for j in range(STAT_CHAINS)]
            after = []
            for j in range(STAT_CHAINS):
                peak, total, delta = carry[j]
                s = jnp.where(row < (counts[j] - ch * CB) * BLK, rs[j][:, :FT] * SCALE2, NEG)
                new = jnp.maximum(peak, jnp.max(s, axis=0, keepdims=True))
                p = jnp.exp2(s - new)
                fix = jnp.exp2(peak - new)
                total = total * fix + jnp.sum(p, axis=0, keepdims=True)
                delta = delta * fix + jnp.sum(p * rs[j][:, FT:], axis=0, keepdims=True)
                after.append((new, total, delta))
            return tuple(after)

        zero = jnp.zeros((1, FT), f32)
        carry = lax.fori_loop(0, most, chunk, ((zero + NEG, zero, zero),) * STAT_CHAINS)
        for j in range(STAT_CHAINS):
            for i in range(3):
                out[pl.ds(16 * i + t * STAT_CHAINS + j, 1), :] = carry[j][i]
        return 0

    lax.fori_loop(0, 16 // STAT_CHAINS, frames, 0)


def row_stats(lists, qgs, kvs):
    return pl.pallas_call(
        stats_kernel,
        in_specs=[SMEM] + [VMEM] * 8,
        out_specs=VMEM,
        out_shape=jax.ShapeDtypeStruct((48, 128), f32),
        scratch_shapes=[pltpu.VMEM((2048, 2 * HEAD), bf16), pltpu.VMEM((2048, 2 * HEAD), bf16),
                        pltpu.VMEM((STAT_CHAINS, 2 * FT, 2 * HEAD), bf16)],
        compiler_params=PARAMS,
        name="row_stats",
    )(lists, *qgs, *kvs)


def merge_stats(stats, norm):
    for t in range(4):
        rows = [slice(4 * ((t - d) % 4), 4 * ((t - d) % 4) + 4) for d in range(4)]
        peaks = [stats[d][0:16][rows[d]] for d in range(4)]
        peak = jnp.maximum(jnp.maximum(peaks[0], peaks[1]), jnp.maximum(peaks[2], peaks[3]))
        total = jnp.zeros_like(peak)
        delta = jnp.zeros_like(peak)
        for d in range(4):
            fix = jnp.exp2(peaks[d] - peak)
            total += fix * stats[d][16:32][rows[d]]
            delta += fix * stats[d][32:48][rows[d]]
        norm[4 * t:4 * t + 4, :] = peak + jnp.log2(total)
        norm[16 + 4 * t:20 + 4 * t, :] = delta / total


def slot_grads(lists, t, qgall, kvall, both, acc, dva, norm):
    row = lax.broadcasted_iota(jnp.int32, (CHUNK, HEAD), 0)
    counts, chunks, most = start_frames(lists, t, qgall, both)
    lse = [norm[pl.ds(t * CHAINS + j, 1), :] for j in range(CHAINS)]
    delta = [norm[pl.ds(16 + t * CHAINS + j, 1), :] for j in range(CHAINS)]
    acc[...] = jnp.zeros_like(acc)

    def chunk(ch, _):
        at = [jnp.minimum(ch, chunks[j] - 1) * CB for j in range(CHAINS)]
        kvs = [load_chunk(lists, t * CHAINS + j, at[j], kvall) for j in range(CHAINS)]
        rs = [dot(kvs[j], both[j], 1, 1) for j in range(CHAINS)]
        lows, pairs = [], []
        for j in range(CHAINS):
            s = jnp.where(row < (counts[j] - ch * CB) * BLK, rs[j][:, :FT] * SCALE2, NEG)
            p = jnp.exp2(s - lse[j])
            low = p.astype(bf16)
            ds = (p * (rs[j][:, FT:] - delta[j]) * SCALE).astype(bf16)
            lows.append(low)
            pairs.append(jnp.concatenate([low, ds], axis=1))
        for j in range(CHAINS):
            product = dot(kvs[j], pairs[j], 0, 0)
            acc[j, 0] += product[HEAD:, :FT]
            acc[j, 1] += product[:HEAD, FT:]
        dvs = [dot(lows[j], both[j, FT:, HEAD:]) for j in range(CHAINS)]
        for i in range(CB):
            for j in range(CHAINS):
                to = pl.multiple_of(lists[t * CHAINS + j, at[j] + i] * BLK, BLK)
                dva[j, pl.ds(to, BLK), :] += dvs[j][i * BLK:(i + 1) * BLK, :]
        return 0

    lax.fori_loop(0, most, chunk, 0)


def put_slot(acc, a):
    for j in range(CHAINS):
        dq = acc[j, 1].T
        high = dq.astype(bf16)
        rows = slice(j * FT, (j + 1) * FT)
        a[rows, :HEAD] = acc[j, 0].T.astype(a.dtype)
        if a.dtype == bf16:
            a[rows, HEAD:2 * HEAD] = high
            a[rows, 2 * HEAD:] = (dq - high.astype(f32)).astype(bf16)
        else:
            a[rows, HEAD:] = dq


def grads_kernel(lists, s0, s1, s2, s3, q0, q1, q2, q3, k0, k1, k2, k3,
                 a0, a1, a2, a3, b0, b1, b2, b3, qgall, kvall, both, acc, dva, norm):
    fill_all((q0, q1, q2, q3), qgall)
    fill_all((k0, k1, k2, k3), kvall)
    both[...] = jnp.zeros_like(both)
    dva[...] = jnp.zeros_like(dva)
    merge_stats([ref[...] for ref in (s0, s1, s2, s3)], norm)

    def slot(t, _):
        slot_grads(lists, t, qgall, kvall, both, acc, dva, norm)
        for d, a in enumerate((a0, a1, a2, a3)):
            pl.when(t == d)(lambda a=a: put_slot(acc, a))
        return 0

    lax.fori_loop(0, 4, slot, 0)
    for d, b in enumerate((b0, b1, b2, b3)):
        total = dva[0, d * 512:(d + 1) * 512, :]
        for j in range(1, CHAINS):
            total += dva[j, d * 512:(d + 1) * 512, :]
        b[...] = total.astype(b.dtype)


def attention_grads(lists, stats, qgs, kvs):
    outs = [(2 * HEAD, f32)] + [(3 * HEAD, bf16)] * 3 + [(HEAD, t) for t in (f32, WIRE, WIRE2, WIRE)]
    keys = pltpu.VMEM((2048, 2 * HEAD), bf16)
    return pl.pallas_call(
        grads_kernel,
        in_specs=[SMEM] + [VMEM] * 12,
        out_specs=[VMEM] * 8,
        out_shape=[jax.ShapeDtypeStruct((512, lanes), t) for lanes, t in outs],
        scratch_shapes=[keys, keys, pltpu.VMEM((CHAINS, 2 * FT, 2 * HEAD), bf16),
                        pltpu.VMEM((CHAINS, 2, HEAD, FT), f32), pltpu.VMEM((CHAINS, 2048, HEAD), f32),
                        pltpu.VMEM((32, 128), f32)],
        compiler_params=PARAMS,
        name="attention_grads",
    )(lists, *stats, *qgs, *kvs)


def finish_kernel(b0, b1, b2, b3, a0, a1, a2, a3, own, other, uq, uv, after,
                  o_keep, o_send, rg_keep, rg_send, up):
    out, dq, dv = a0[:, :HEAD], a0[:, HEAD:], b0[...]
    for a, b in ((a1, b1), (a2, b2), (a3, b3)):
        out += a[:, :HEAD].astype(f32)
        dq += a[:, HEAD:2 * HEAD].astype(f32) + a[:, 2 * HEAD:].astype(f32)
        dv += b[...].astype(f32)
    out, dq, dv = out.astype(bf16), dq.astype(bf16), dv.astype(bf16)
    o_keep[...] = out[:256]
    o_send[...] = out[256:]
    for c in range(2):
        @pl.when(lax.axis_index("c") == c)
        def _():
            gq = dot(dq, uq[:, c * HEAD:(c + 1) * HEAD], 1, 1)
            gv = dot(dv, uv[:, c * HEAD:(c + 1) * HEAD], 1, 1)
            rg_keep[:, :RANK] = gq[:256]
            rg_keep[:, RANK:] = gv[:256]
            rg_send[:, :RANK] = gq[256:]
            rg_send[:, RANK:] = gv[256:]
    up[:, :HEAD] = dot(own[:, :RANK], dq[:256], 0, 0) + dot(other[:, :RANK], dq[256:], 0, 0)
    up[:, HEAD:] = dot(own[:, RANK:], dv[:256], 0, 0) + dot(other[:, RANK:], dv[256:], 0, 0)


def finish(b, a, own, other, uq, uv, after):
    return pl.pallas_call(
        finish_kernel,
        in_specs=[VMEM] * 12 + [ANY],
        out_specs=[VMEM] * 5,
        out_shape=[jax.ShapeDtypeStruct((256, HEAD), bf16)] * 2
        + [jax.ShapeDtypeStruct((r, 256), f32) for r in (256, 256, 128)],
        compiler_params=PARAMS,
        name="finish",
    )(*b, *a, own, other, uq, uv, after)


def columns_kernel(act, out, rows, sem):
    width = rows.shape[1]
    at = pl.multiple_of(lax.axis_index("z") * width, 128)
    copy = pltpu.make_async_copy(act.at[:, pl.ds(at, width)], rows, sem)
    copy.start()
    copy.wait()
    for i in range(width // 256):
        out[i * 256:(i + 1) * 256, :] = rows[:, i * 256:(i + 1) * 256].T


def columns(act, after):
    rows, width = act.shape[0], act.shape[1] // 4

    def kernel(act, after, out, part, sem):
        columns_kernel(act, out, part, sem)

    return pl.pallas_call(
        kernel,
        in_specs=[ANY, ANY],
        out_specs=VMEM,
        out_shape=jax.ShapeDtypeStruct((width, rows), bf16),
        scratch_shapes=[pltpu.VMEM((rows, width), bf16), pltpu.SemaphoreType.DMA(())],
        compiler_params=PARAMS,
        name="columns",
    )(act, after)


def cores_kernel(keep, other, total, low):
    rg = keep[...] + other[...]
    total[...] = rg
    low[...] = rg.astype(bf16)


def add_cores(keep, other):
    return pl.pallas_call(
        cores_kernel,
        in_specs=[VMEM] * 2,
        out_specs=[VMEM] * 2,
        out_shape=[jax.ShapeDtypeStruct((256, 256), t) for t in (f32, bf16)],
        compiler_params=PARAMS,
        name="add_cores",
    )(keep, other)


def down_kernel(act_t, own, r1, r2, r3, mine, theirs):
    rg = (own[...] + r1[...].astype(f32) + r2[...].astype(f32) + r3[...].astype(f32)).astype(bf16)
    rows = mine.shape[0]
    for c in range(2):
        @pl.when(lax.axis_index("c") == c)
        def _():
            mine[...] = dot(act_t[c * rows:(c + 1) * rows, :], rg)
            theirs[...] = dot(act_t[(1 - c) * rows:(2 - c) * rows, :], rg)


def down_terms(act_t, own, others):
    rows = act_t.shape[0] // 2
    return pl.pallas_call(
        down_kernel,
        in_specs=[VMEM] * 5,
        out_specs=[VMEM] * 2,
        out_shape=[jax.ShapeDtypeStruct((rows, 256), f32)] * 2,
        compiler_params=PARAMS,
        name="down_terms",
    )(act_t, own, *others)


def pack_kernel(mine, theirs, up, out):
    for i in range(16):
        part = mine[i * 40:(i + 1) * 40, :] + theirs[i * 40:(i + 1) * 40, :]
        out[i, :, :] = jnp.concatenate([part, up[i * 8:(i + 1) * 8, :]], axis=0).astype(out.dtype)


def pack(mine, theirs, up):
    return pl.pallas_call(
        pack_kernel,
        in_specs=[VMEM] * 3,
        out_specs=VMEM,
        out_shape=jax.ShapeDtypeStruct((16, 48, 256), bf16),
        compiler_params=PARAMS,
        name="pack",
    )(mine, theirs, up)


def emit_kernel(own, other, o_keep, o_other, att, down_q, up_q, down_v, up_v):
    zz = pl.program_id(0)
    halves = [own, other]
    for c in range(2):
        @pl.when(lax.axis_index("c") == c)
        def _():
            for cc in range(2):
                src = halves[(c + cc) % 2]
                for i in range(16):
                    part = src[zz * 16 + i].astype(f32)
                    at = cc * 640 + i * 40
                    down_q[at:at + 40, :] = part[:40, :RANK]
                    down_v[at:at + 40, :] = part[:40, RANK:]

            @pl.when(zz == 0)
            def _():
                outs = [o_keep, o_other]
                for cc in range(2):
                    src = halves[(c + cc) % 2]
                    att[:, cc * HEAD:(cc + 1) * HEAD] = outs[(c + cc) % 2][...]
                    for i in range(16):
                        part = src[lax.axis_index("z") * 16 + i].astype(f32)
                        up_q[i * 8:(i + 1) * 8, cc * HEAD:(cc + 1) * HEAD] = part[40:, :HEAD]
                        up_v[i * 8:(i + 1) * 8, cc * HEAD:(cc + 1) * HEAD] = part[40:, HEAD:]


def emit(own, other, o_keep, o_other):
    whole = lambda a: pl.BlockSpec(a, lambda k: (0,) * len(a))
    return pl.pallas_call(
        emit_kernel,
        grid=(4,),
        in_specs=[whole(a.shape) for a in (own, other, o_keep, o_other)],
        out_specs=[whole((256, 256)), pl.BlockSpec((1280, RANK), lambda k: (k, 0)), whole((RANK, 256)),
                   pl.BlockSpec((1280, RANK), lambda k: (k, 0)), whole((RANK, 256))],
        out_shape=[jax.ShapeDtypeStruct((256, 256), bf16), jax.ShapeDtypeStruct((5120, RANK), f32),
                   jax.ShapeDtypeStruct((RANK, 256), f32), jax.ShapeDtypeStruct((5120, RANK), f32),
                   jax.ShapeDtypeStruct((RANK, 256), f32)],
        compiler_params=PARAMS,
        name="emit",
    )(own, other, o_keep, o_other)


def total_kernel(parts, after, out):
    total = parts[0].astype(f32)
    for i in range(1, 16):
        total += parts[i].astype(f32)
    low = total.astype(bf16)
    for i in range(64):
        out[i, :, :] = low


def total_for_all(parts, after):
    return pl.pallas_call(
        total_kernel,
        in_specs=[VMEM, ANY],
        out_specs=VMEM,
        out_shape=jax.ShapeDtypeStruct((64, 48, 256), bf16),
        compiler_params=PARAMS,
        name="total_for_all",
    )(parts, after)


def ring(n, d):
    return [(i, (i + d) % n) for i in range(n)]


def swap(a):
    return lax.ppermute(a, "c", ring(2, 1))


def spread(a, axis):
    one, three, two = [lax.ppermute(a, axis, ring(4, d)) for d in (1, 3, 2)]
    return [a, one, two, three]


def relay(a, axis):
    one, three = [lax.ppermute(a, axis, ring(4, d)) for d in (1, 3)]
    return [a, one, lax.ppermute(one, axis, ring(4, 1)), three]


def collect(parts, axis):
    return [parts[0]] + [lax.ppermute(parts[d], axis, ring(4, -d)) for d in (1, 2, 3)]


def local(act, wq, wk, wv, dq, uq, dv, uv, grad_out, levels, order, slot):
    keep, send, rank = project(act, wq, wk, wv, dq, dv, uq, uv, grad_out)
    kv, qg = assemble(keep, swap(send))
    kvs = relay(kv, "x")
    qgs = relay(qg, "y")
    lists = visible_lists(slot, levels, order)
    stats = spread(row_stats(lists, qgs, kvs), "y")
    parts = attention_grads(lists, stats, qgs, kvs)
    act_t = columns(act, parts[0])
    a = collect(parts[:4], "y")
    b = collect(parts[4:], "x")
    o_keep, o_send, rg_keep, rg_send, up = finish(b, a, rank, swap(rank), uq, uv, act_t)
    o_other = swap(o_send)
    rg, low = add_cores(rg_keep, swap(rg_send))
    mine, theirs = down_terms(act_t, rg, relay(low, "z")[1:])
    terms = lax.all_to_all(pack(mine, swap(theirs), up), ("x", "y"), 0, 0, tiled=True)
    wide = lax.all_to_all(total_for_all(terms, o_other), ("z", "x", "y"), 0, 0, tiled=True)
    att, down_q, up_q, down_v, up_v = emit(wide, swap(wide), o_keep, o_other)
    return att, down_q, up_q, down_v, up_v


def solution(mesh):
    torus = Mesh(mesh.devices.reshape(4, 4, 2, 4), ("x", "y", "c", "z"))
    tm = ("x", "y", "c")
    return jax.shard_map(
        local,
        mesh=torus,
        in_specs=(
            P(tm, None),
            P(None, "z"),
            P(None, "z"),
            P(None, "z"),
            P(),
            P(None, "z"),
            P(),
            P(None, "z"),
            P(tm, "z"),
            P(),
            P(),
            P(),
        ),
        out_specs=(P(tm, "z"), P(), P(None, "z"), P(), P(None, "z")),
        check_vma=False,
    )
```

```python
import math

import jax
import jax.numpy as jnp
from jax import lax
from jax.experimental import pallas as pl
from jax.experimental.pallas import tpu as pltpu
from jax.sharding import Mesh
from jax.sharding import PartitionSpec as P

HEAD = 128
FT = 128
BLK = 32
RANK = 128
CHUNK = 512
CB = CHUNK // BLK
CHAINS = 4
STAT_CHAINS = 4
SCALE = HEAD ** -0.5
SCALE2 = SCALE * math.log2(math.e)
NEG = -1e30
f32 = jnp.float32
bf16 = jnp.bfloat16
WIRE = f32
WIRE2 = bf16
KT = 2560
VMEM = pl.BlockSpec(memory_space=pltpu.VMEM)
SMEM = pl.BlockSpec(memory_space=pltpu.SMEM)
ANY = pl.BlockSpec(memory_space=pl.ANY)
WIDE = pltpu.CompilerParams(vmem_limit_bytes=60 * 1024 * 1024)
PARAMS = pltpu.CompilerParams(vmem_limit_bytes=20 * 1024 * 1024)


def dot(a, b, ca=1, cb=0):
    return lax.dot_general(a, b, (((ca,), (cb,)), ((), ())), preferred_element_type=f32)


def by_core(put, keep, send):
    for c in range(2):
        @pl.when(lax.axis_index("c") == c)
        def _():
            put(keep, c * HEAD)
            put(send, (1 - c) * HEAD)


def proj_kernel(act, wq, wk, wv, down_q, down_v, up_q, up_v, grad, keep, send, rank, aq, ak, av, rq, rv):
    step = pl.program_id(0)
    last = pl.num_programs(0) - 1
    a = act[...]
    parts = [(ak, wk), (av, wv), (rv, down_v), (aq, wq), (rq, down_q)]

    @pl.when(step == 0)
    def _():
        for total, w in parts:
            total[...] = dot(a, w[...])

    @pl.when(step > 0)
    def _():
        for total, w in parts:
            total[...] += dot(a, w[...])

    @pl.when(step == last)
    def _():
        low_q = rq[...].astype(bf16)
        low_v = rv[...].astype(bf16)
        rank[:, :RANK] = low_q
        rank[:, RANK:] = low_v
        keys = ak[...].astype(bf16)
        values = (av[...] + dot(low_v, up_v[...])).astype(bf16)
        query = (aq[...] + dot(low_q, up_q[...])).astype(bf16)

        def put(ref, at):
            ref[:, :HEAD] = keys[:, at:at + HEAD]
            ref[:, HEAD:2 * HEAD] = values[:, at:at + HEAD]
            ref[:, 2 * HEAD:3 * HEAD] = query[:, at:at + HEAD]
            ref[:, 3 * HEAD:] = grad[:, at:at + HEAD]

        by_core(put, keep, send)


def project(act, wq, wk, wv, down_q, down_v, up_q, up_v, grad):
    rows, width = act.shape
    cols = wq.shape[1]
    whole = lambda shape: pl.BlockSpec(shape, lambda k: (0, 0))
    shapes = [(rows, 4 * HEAD), (rows, 4 * HEAD), (rows, 2 * RANK)]
    return pl.pallas_call(
        proj_kernel,
        grid=(width // KT,),
        in_specs=[pl.BlockSpec((rows, KT), lambda k: (0, k))]
        + [pl.BlockSpec((KT, cols), lambda k: (k, 0))] * 3
        + [pl.BlockSpec((KT, RANK), lambda k: (k, 0))] * 2 + [whole(up_q.shape), whole(up_v.shape), whole(grad.shape)],
        out_specs=[whole(s) for s in shapes],
        out_shape=[jax.ShapeDtypeStruct(s, bf16) for s in shapes],
        scratch_shapes=[pltpu.VMEM((rows, cols), f32)] * 3 + [pltpu.VMEM((rows, RANK), f32)] * 2,
        compiler_params=WIDE,
        cost_estimate=pl.CostEstimate(flops=2 * rows * width * (3 * cols + 2 * RANK),
                                      bytes_accessed=2 * width * (rows + 3 * cols + 2 * RANK), transcendentals=0),
        name="project",
    )(act, wq, wk, wv, down_q, down_v, up_q, up_v, grad)


def assemble_kernel(keep, other, kv, qg):
    kv[:256, :] = keep[:, :256]
    kv[256:, :] = other[:, :256]
    qg[:256, :] = keep[:, 256:]
    qg[256:, :] = other[:, 256:]


def assemble(keep, other):
    return pl.pallas_call(
        assemble_kernel,
        in_specs=[VMEM] * 2,
        out_specs=[VMEM] * 2,
        out_shape=[jax.ShapeDtypeStruct((512, 256), bf16)] * 2,
        compiler_params=PARAMS,
        name="assemble",
    )(keep, other)


def lists_kernel(slot, packed, out):
    x, y, c = (lax.axis_index(n) for n in ("x", "y", "c"))

    def frame(xx, yy, local):
        core = c if local < 2 else 1 - c
        return slot[((xx * 4 + yy) * 2 + core) * 2 + local % 2]

    keys = [frame(lax.rem(x + 4 - k // 4, 4), y, k % 4) for k in range(16)]
    for q in range(16):
        out[17, q] = frame(x, lax.rem(y + 4 - q // 4, 4), q % 4)

    def one(q, _):
        f = out[17, q]
        words = [packed[f, keys[k]] for k in range(16)]
        n = 0
        for k, word in enumerate(words):
            for r in range(4):
                out[q, n + r] = k * 4 + ((word >> (2 * r)) & 3)
            n = n + (word >> 8)
        for r in range(CB):
            out[q, n + r] = 0
        out[16, q] = n
        return 0

    lax.fori_loop(0, 16, one, 0)


def visible_lists(slot, levels, order):
    packed = levels * 256 + jnp.sum(order * jnp.array([1, 4, 16, 64], jnp.int32), axis=-1)
    return pl.pallas_call(
        lists_kernel,
        in_specs=[SMEM] * 2,
        out_specs=SMEM,
        out_shape=jax.ShapeDtypeStruct((24, 128), jnp.int32),
        compiler_params=PARAMS,
        name="lists",
    )(slot, packed)


def fill_all(parts, whole):
    rows = parts[0].shape[0]
    for d, part in enumerate(parts):
        whole[d * rows:(d + 1) * rows, :] = part[...]


def load_chunk(lists, f, at, kvall):
    blocks = [kvall[pl.ds(pl.multiple_of(lists[f, at + i] * BLK, BLK), BLK), :] for i in range(CB)]
    return jnp.concatenate(blocks, axis=0)


def start_frames(lists, t, qgall, both):
    chains = both.shape[0]
    counts = []
    for j in range(chains):
        f = t * chains + j
        at = pl.multiple_of(f * FT, FT)
        both[j, :FT, :HEAD] = qgall[pl.ds(at, FT), :HEAD]
        both[j, FT:, HEAD:] = qgall[pl.ds(at, FT), HEAD:]
        counts.append(lists[16, f])
    chunks = [(n + CB - 1) // CB for n in counts]
    most = chunks[0]
    for n in chunks[1:]:
        most = jnp.maximum(most, n)
    return counts, chunks, most


def stats_kernel(lists, q0, q1, q2, q3, k0, k1, k2, k3, out, qgall, kvall, both):
    fill_all((q0, q1, q2, q3), qgall)
    fill_all((k0, k1, k2, k3), kvall)
    both[...] = jnp.zeros_like(both)
    row = lax.broadcasted_iota(jnp.int32, (CHUNK, HEAD), 0)

    def frames(t, _):
        counts, chunks, most = start_frames(lists, t, qgall, both)

        def chunk(ch, carry):
            kvs = [load_chunk(lists, t * STAT_CHAINS + j, jnp.minimum(ch, chunks[j] - 1) * CB, kvall)
                   for j in range(STAT_CHAINS)]
            rs = [dot(kvs[j], both[j], 1, 1) for j in range(STAT_CHAINS)]
            after = []
            for j in range(STAT_CHAINS):
                peak, total, delta = carry[j]
                s = jnp.where(row < (counts[j] - ch * CB) * BLK, rs[j][:, :FT] * SCALE2, NEG)
                new = jnp.maximum(peak, jnp.max(s, axis=0, keepdims=True))
                p = jnp.exp2(s - new)
                fix = jnp.exp2(peak - new)
                total = total * fix + jnp.sum(p, axis=0, keepdims=True)
                delta = delta * fix + jnp.sum(p * rs[j][:, FT:], axis=0, keepdims=True)
                after.append((new, total, delta))
            return tuple(after)

        zero = jnp.zeros((1, FT), f32)
        carry = lax.fori_loop(0, most, chunk, ((zero + NEG, zero, zero),) * STAT_CHAINS)
        for j in range(STAT_CHAINS):
            for i in range(3):
                out[pl.ds(16 * i + t * STAT_CHAINS + j, 1), :] = carry[j][i]
        return 0

    lax.fori_loop(0, 16 // STAT_CHAINS, frames, 0)


def row_stats(lists, qgs, kvs):
    return pl.pallas_call(
        stats_kernel,
        in_specs=[SMEM] + [VMEM] * 8,
        out_specs=VMEM,
        out_shape=jax.ShapeDtypeStruct((48, 128), f32),
        scratch_shapes=[pltpu.VMEM((2048, 2 * HEAD), bf16), pltpu.VMEM((2048, 2 * HEAD), bf16),
                        pltpu.VMEM((STAT_CHAINS, 2 * FT, 2 * HEAD), bf16)],
        compiler_params=PARAMS,
        name="row_stats",
    )(lists, *qgs, *kvs)


def merge_stats(stats, norm):
    for t in range(4):
        rows = [slice(4 * ((t - d) % 4), 4 * ((t - d) % 4) + 4) for d in range(4)]
        peaks = [stats[d][0:16][rows[d]] for d in range(4)]
        peak = jnp.maximum(jnp.maximum(peaks[0], peaks[1]), jnp.maximum(peaks[2], peaks[3]))
        total = jnp.zeros_like(peak)
        delta = jnp.zeros_like(peak)
        for d in range(4):
            fix = jnp.exp2(peaks[d] - peak)
            total += fix * stats[d][16:32][rows[d]]
            delta += fix * stats[d][32:48][rows[d]]
        norm[4 * t:4 * t + 4, :] = peak + jnp.log2(total)
        norm[16 + 4 * t:20 + 4 * t, :] = delta / total


def slot_grads(lists, t, qgall, kvall, both, acc, dva, norm):
    row = lax.broadcasted_iota(jnp.int32, (CHUNK, HEAD), 0)
    counts, chunks, most = start_frames(lists, t, qgall, both)
    lse = [norm[pl.ds(t * CHAINS + j, 1), :] for j in range(CHAINS)]
    delta = [norm[pl.ds(16 + t * CHAINS + j, 1), :] for j in range(CHAINS)]
    acc[...] = jnp.zeros_like(acc)

    def chunk(ch, _):
        at = [jnp.minimum(ch, chunks[j] - 1) * CB for j in range(CHAINS)]
        kvs = [load_chunk(lists, t * CHAINS + j, at[j], kvall) for j in range(CHAINS)]
        rs = [dot(kvs[j], both[j], 1, 1) for j in range(CHAINS)]
        lows, pairs = [], []
        for j in range(CHAINS):
            s = jnp.where(row < (counts[j] - ch * CB) * BLK, rs[j][:, :FT] * SCALE2, NEG)
            p = jnp.exp2(s - lse[j])
            low = p.astype(bf16)
            ds = (p * (rs[j][:, FT:] - delta[j]) * SCALE).astype(bf16)
            lows.append(low)
            pairs.append(jnp.concatenate([low, ds], axis=1))
        for j in range(CHAINS):
            product = dot(kvs[j], pairs[j], 0, 0)
            acc[j, 0] += product[HEAD:, :FT]
            acc[j, 1] += product[:HEAD, FT:]
        dvs = [dot(lows[j], both[j, FT:, HEAD:]) for j in range(CHAINS)]
        for i in range(CB):
            for j in range(CHAINS):
                to = pl.multiple_of(lists[t * CHAINS + j, at[j] + i] * BLK, BLK)
                dva[j, pl.ds(to, BLK), :] += dvs[j][i * BLK:(i + 1) * BLK, :]
        return 0

    lax.fori_loop(0, most, chunk, 0)


def put_slot(acc, a):
    for j in range(CHAINS):
        dq = acc[j, 1].T
        high = dq.astype(bf16)
        rows = slice(j * FT, (j + 1) * FT)
        a[rows, :HEAD] = acc[j, 0].T.astype(a.dtype)
        if a.dtype == bf16:
            a[rows, HEAD:2 * HEAD] = high
            a[rows, 2 * HEAD:] = (dq - high.astype(f32)).astype(bf16)
        else:
            a[rows, HEAD:] = dq


def grads_kernel(lists, s0, s1, s2, s3, q0, q1, q2, q3, k0, k1, k2, k3,
                 a0, a1, a2, a3, b0, b1, b2, b3, qgall, kvall, both, acc, dva, norm):
    fill_all((q0, q1, q2, q3), qgall)
    fill_all((k0, k1, k2, k3), kvall)
    both[...] = jnp.zeros_like(both)
    dva[...] = jnp.zeros_like(dva)
    merge_stats([ref[...] for ref in (s0, s1, s2, s3)], norm)

    def slot(t, _):
        slot_grads(lists, t, qgall, kvall, both, acc, dva, norm)
        for d, a in enumerate((a0, a1, a2, a3)):
            pl.when(t == d)(lambda a=a: put_slot(acc, a))
        return 0

    lax.fori_loop(0, 4, slot, 0)
    for d, b in enumerate((b0, b1, b2, b3)):
        total = dva[0, d * 512:(d + 1) * 512, :]
        for j in range(1, CHAINS):
            total += dva[j, d * 512:(d + 1) * 512, :]
        b[...] = total.astype(b.dtype)


def attention_grads(lists, stats, qgs, kvs):
    outs = [(2 * HEAD, f32)] + [(3 * HEAD, bf16)] * 3 + [(HEAD, t) for t in (f32, WIRE, WIRE2, WIRE)]
    keys = pltpu.VMEM((2048, 2 * HEAD), bf16)
    return pl.pallas_call(
        grads_kernel,
        in_specs=[SMEM] + [VMEM] * 12,
        out_specs=[VMEM] * 8,
        out_shape=[jax.ShapeDtypeStruct((512, lanes), t) for lanes, t in outs],
        scratch_shapes=[keys, keys, pltpu.VMEM((CHAINS, 2 * FT, 2 * HEAD), bf16),
                        pltpu.VMEM((CHAINS, 2, HEAD, FT), f32), pltpu.VMEM((CHAINS, 2048, HEAD), f32),
                        pltpu.VMEM((32, 128), f32)],
        compiler_params=PARAMS,
        name="attention_grads",
    )(lists, *stats, *qgs, *kvs)


def finish_kernel(b0, b1, b2, b3, a0, a1, a2, a3, own, other, uq, uv, after,
                  o_keep, o_send, rg_keep, rg_send, up):
    out, dq, dv = a0[:, :HEAD], a0[:, HEAD:], b0[...]
    for a, b in ((a1, b1), (a2, b2), (a3, b3)):
        out += a[:, :HEAD].astype(f32)
        dq += a[:, HEAD:2 * HEAD].astype(f32) + a[:, 2 * HEAD:].astype(f32)
        dv += b[...].astype(f32)
    out, dq, dv = out.astype(bf16), dq.astype(bf16), dv.astype(bf16)
    o_keep[...] = out[:256]
    o_send[...] = out[256:]
    for c in range(2):
        @pl.when(lax.axis_index("c") == c)
        def _():
            gq = dot(dq, uq[:, c * HEAD:(c + 1) * HEAD], 1, 1)
            gv = dot(dv, uv[:, c * HEAD:(c + 1) * HEAD], 1, 1)
            rg_keep[:, :RANK] = gq[:256]
            rg_keep[:, RANK:] = gv[:256]
            rg_send[:, :RANK] = gq[256:]
            rg_send[:, RANK:] = gv[256:]
    up[:, :HEAD] = dot(own[:, :RANK], dq[:256], 0, 0) + dot(other[:, :RANK], dq[256:], 0, 0)
    up[:, HEAD:] = dot(own[:, RANK:], dv[:256], 0, 0) + dot(other[:, RANK:], dv[256:], 0, 0)


def finish(b, a, own, other, uq, uv, after):
    return pl.pallas_call(
        finish_kernel,
        in_specs=[VMEM] * 12 + [ANY],
        out_specs=[VMEM] * 5,
        out_shape=[jax.ShapeDtypeStruct((256, HEAD), bf16)] * 2
        + [jax.ShapeDtypeStruct((r, 256), f32) for r in (256, 256, 128)],
        compiler_params=PARAMS,
        name="finish",
    )(*b, *a, own, other, uq, uv, after)


def columns_kernel(act, out, rows, sem):
    width = rows.shape[1]
    at = pl.multiple_of(lax.axis_index("z") * width, 128)
    copy = pltpu.make_async_copy(act.at[:, pl.ds(at, width)], rows, sem)
    copy.start()
    copy.wait()
    for i in range(width // 256):
        out[i * 256:(i + 1) * 256, :] = rows[:, i * 256:(i + 1) * 256].T


def columns(act, after):
    rows, width = act.shape[0], act.shape[1] // 4

    def kernel(act, after, out, part, sem):
        columns_kernel(act, out, part, sem)

    return pl.pallas_call(
        kernel,
        in_specs=[ANY, ANY],
        out_specs=VMEM,
        out_shape=jax.ShapeDtypeStruct((width, rows), bf16),
        scratch_shapes=[pltpu.VMEM((rows, width), bf16), pltpu.SemaphoreType.DMA(())],
        compiler_params=PARAMS,
        name="columns",
    )(act, after)


def cores_kernel(keep, other, total, low):
    rg = keep[...] + other[...]
    total[...] = rg
    low[...] = rg.astype(bf16)


def add_cores(keep, other):
    return pl.pallas_call(
        cores_kernel,
        in_specs=[VMEM] * 2,
        out_specs=[VMEM] * 2,
        out_shape=[jax.ShapeDtypeStruct((256, 256), t) for t in (f32, bf16)],
        compiler_params=PARAMS,
        name="add_cores",
    )(keep, other)


def down_kernel(act_t, own, r1, r2, r3, mine, theirs):
    rg = (own[...] + r1[...].astype(f32) + r2[...].astype(f32) + r3[...].astype(f32)).astype(bf16)
    rows = mine.shape[0]
    for c in range(2):
        @pl.when(lax.axis_index("c") == c)
        def _():
            mine[...] = dot(act_t[c * rows:(c + 1) * rows, :], rg)
            theirs[...] = dot(act_t[(1 - c) * rows:(2 - c) * rows, :], rg)


def down_terms(act_t, own, others):
    rows = act_t.shape[0] // 2
    return pl.pallas_call(
        down_kernel,
        in_specs=[VMEM] * 5,
        out_specs=[VMEM] * 2,
        out_shape=[jax.ShapeDtypeStruct((rows, 256), f32)] * 2,
        compiler_params=PARAMS,
        name="down_terms",
    )(act_t, own, *others)


def pack_kernel(mine, theirs, up, out):
    for i in range(16):
        part = mine[i * 40:(i + 1) * 40, :] + theirs[i * 40:(i + 1) * 40, :]
        out[i, :, :] = jnp.concatenate([part, up[i * 8:(i + 1) * 8, :]], axis=0).astype(out.dtype)


def pack(mine, theirs, up):
    return pl.pallas_call(
        pack_kernel,
        in_specs=[VMEM] * 3,
        out_specs=VMEM,
        out_shape=jax.ShapeDtypeStruct((16, 48, 256), bf16),
        compiler_params=PARAMS,
        name="pack",
    )(mine, theirs, up)


def half_kernel(src, down_q, down_v, up):
    for i in range(16):
        part = src[pl.program_id(0) * 16 + i].astype(f32)
        down_q[i * 40:(i + 1) * 40, :] = part[:40, :RANK]
        down_v[i * 40:(i + 1) * 40, :] = part[:40, RANK:]

    @pl.when(pl.program_id(0) == 0)
    def _():
        for i in range(16):
            up[i * 8:(i + 1) * 8, :] = src[lax.axis_index("z") * 16 + i].astype(f32)[40:, :]


def own_kernel(src, down_q, down_v, up):
    half_kernel(src, down_q, down_v, up)


def other_kernel(src, own_up, o_keep, o_other, q_in, v_in, att, down_q, up_q, down_v, up_v, other_up):
    half_kernel(src, down_q, down_v, other_up)

    @pl.when(pl.program_id(0) == 0)
    def _():
        ups, outs = [own_up, other_up], [o_keep, o_other]
        for c in range(2):
            @pl.when(lax.axis_index("c") == c)
            def _():
                for cc in range(2):
                    lanes = slice(cc * HEAD, (cc + 1) * HEAD)
                    att[:, lanes] = outs[(c + cc) % 2][...]
                    up_q[:, lanes] = ups[(c + cc) % 2][:, :RANK]
                    up_v[:, lanes] = ups[(c + cc) % 2][:, RANK:]


def whole_block(shape):
    return pl.BlockSpec(shape, lambda k: (0,) * len(shape))


def emit_own(own):
    mine = pl.BlockSpec((640, RANK), lambda k: (k * 2 + lax.axis_index("c"), 0))
    down = jax.ShapeDtypeStruct((5120, RANK), f32)
    return pl.pallas_call(
        own_kernel,
        grid=(4,),
        in_specs=[whole_block(own.shape)],
        out_specs=[mine, mine, whole_block((RANK, 256))],
        out_shape=[down, down, jax.ShapeDtypeStruct((RANK, 256), f32)],
        compiler_params=PARAMS,
        name="emit_own",
    )(own)


def emit_other(other, own_up, o_keep, o_other, down_q, down_v):
    theirs = pl.BlockSpec((640, RANK), lambda k: (k * 2 + 1 - lax.axis_index("c"), 0))
    down = jax.ShapeDtypeStruct((5120, RANK), f32)
    up = jax.ShapeDtypeStruct((RANK, 256), f32)
    return pl.pallas_call(
        other_kernel,
        grid=(4,),
        in_specs=[whole_block(a.shape) for a in (other, own_up, o_keep, o_other)] + [ANY, ANY],
        out_specs=[whole_block((256, 256)), theirs, whole_block((RANK, 256)), theirs, whole_block((RANK, 256))],
        out_shape=[jax.ShapeDtypeStruct((256, 256), bf16), down, up, down, up],
        input_output_aliases={4: 1, 5: 3},
        scratch_shapes=[pltpu.VMEM((RANK, 256), f32)],
        compiler_params=PARAMS,
        name="emit_other",
    )(other, own_up, o_keep, o_other, down_q, down_v)


def total_kernel(parts, after, out):
    total = parts[0].astype(f32)
    for i in range(1, 16):
        total += parts[i].astype(f32)
    low = total.astype(bf16)
    for i in range(64):
        out[i, :, :] = low


def total_for_all(parts, after):
    return pl.pallas_call(
        total_kernel,
        in_specs=[VMEM, ANY],
        out_specs=VMEM,
        out_shape=jax.ShapeDtypeStruct((64, 48, 256), bf16),
        compiler_params=PARAMS,
        name="total_for_all",
    )(parts, after)


def ring(n, d):
    return [(i, (i + d) % n) for i in range(n)]


def swap(a):
    return lax.ppermute(a, "c", ring(2, 1))


def spread(a, axis):
    one, three, two = [lax.ppermute(a, axis, ring(4, d)) for d in (1, 3, 2)]
    return [a, one, two, three]


def relay(a, axis):
    one, three = [lax.ppermute(a, axis, ring(4, d)) for d in (1, 3)]
    return [a, one, lax.ppermute(one, axis, ring(4, 1)), three]


def collect(parts, axis):
    return [parts[0]] + [lax.ppermute(parts[d], axis, ring(4, -d)) for d in (1, 2, 3)]


def local(act, wq, wk, wv, dq, uq, dv, uv, grad_out, levels, order, slot):
    keep, send, rank = project(act, wq, wk, wv, dq, dv, uq, uv, grad_out)
    kv, qg = assemble(keep, swap(send))
    kvs = relay(kv, "x")
    qgs = relay(qg, "y")
    lists = visible_lists(slot, levels, order)
    stats = spread(row_stats(lists, qgs, kvs), "y")
    parts = attention_grads(lists, stats, qgs, kvs)
    act_t = columns(act, parts[0])
    a = collect(parts[:4], "y")
    b = collect(parts[4:], "x")
    o_keep, o_send, rg_keep, rg_send, up = finish(b, a, rank, swap(rank), uq, uv, act_t)
    o_other = swap(o_send)
    rg, low = add_cores(rg_keep, swap(rg_send))
    mine, theirs = down_terms(act_t, rg, spread(low, "z")[1:])
    terms = lax.all_to_all(pack(mine, swap(theirs), up), ("x", "y"), 0, 0, tiled=True)
    wide = lax.all_to_all(total_for_all(terms, o_other), ("z", "x", "y"), 0, 0, tiled=True)
    down_q, down_v, own_up = emit_own(wide)
    att, down_q, up_q, down_v, up_v = emit_other(swap(wide), own_up, o_keep, o_other, down_q, down_v)
    return att, down_q, up_q, down_v, up_v


def solution(mesh):
    torus = Mesh(mesh.devices.reshape(4, 4, 2, 4), ("x", "y", "c", "z"))
    tm = ("x", "y", "c")
    return jax.shard_map(
        local,
        mesh=torus,
        in_specs=(
            P(tm, None),
            P(None, "z"),
            P(None, "z"),
            P(None, "z"),
            P(),
            P(None, "z"),
            P(),
            P(None, "z"),
            P(tm, "z"),
            P(),
            P(),
            P(),
        ),
        out_specs=(P(tm, "z"), P(), P(None, "z"), P(), P(None, "z")),
        check_vma=False,
    )
```
